512 devices in a mesh: freq: 16 (over y_hi, x, core), rgrp: 32 (over z, y_lo).
Axes of the slice: x: 4, y: 4 (y_hi: 2, y_lo: 2; y = y_hi * 2 + y_lo), z: 16, core: 2. Of those that a mesh axis runs over, the one named last changes fastest.
Arguments:
- traces: bfloat16 [1024, 147456], P('rgrp', 'freq'), may hold values from -6 to 6
- segment_offsets: int32 [64], P('freq'), may hold values from 0 to 1024
- channel_order: int32 [32, 32], P('rgrp'), may hold values from 0 to 31, each once within a row
- pilot_channel: int32 [1], replicated, may hold values from 0 to 1023
Outputs:
- cross_spectra: bfloat16 [2, 1024, 32, 2048], P(None, 'rgrp', None, 'freq')
The draws below stay inside these ranges and needn't reach their ends.
All inputs are finite; a program needn't handle non-finite values.
Results may differ from the reference program's by a relative error of at most 0.0077.
Values may be sent and summed in bfloat16 or wider, within the bound.
No kernel may reach another device: no remote copies, remote signals or barrier semaphores. Data moves between devices by JAX's collectives and lax.ppermute only.
A program may use at most 64 MiB of HBM per device.

```python
import math
import jax
import jax.numpy as jnp
from jax import lax

L = 2048
K = 1024
CH_DEV = 32
SEG_DEV = 4
MARGIN = 1024
SPAN = 9216
SEGMENTS = 64
GROUPS = 32
CHANNELS = 1024
N_FREQ = 16


def draw_segment_offsets(key, part):
    values = jax.random.randint(key, (SEGMENTS,), 0, MARGIN + 1, dtype=jnp.int32)
    values = values.at[0].set(0)
    values = values.at[SEGMENTS - 1].set(MARGIN)
    return values


def levels(stream_key, extent, pieces, least, largest):
    factor_of = 1.0
    for position, blocks in pieces:
        draws = jax.random.uniform(jax.random.fold_in(jax.random.fold_in(stream_key, 6), position), (blocks,), jnp.float32, least / len(pieces), largest / len(pieces))
        factor_of = factor_of * jnp.repeat(jnp.exp(draws), extent[position] // blocks).reshape((-1,) + (1,) * (len(extent) - 1 - position))
    return factor_of


def bell_draw(key, extent, deviation, limit, pieces=(), kind=jnp.bfloat16):
    array = deviation * jax.random.normal(key, extent, jnp.float32)
    if pieces:
        array = array * levels(key, extent, pieces, -0.22, 0.18)
    return jnp.clip(array, -limit, limit).astype(kind)


def setup_inputs(seed: int = 0) -> dict:
    arg_keys = jax.random.split(jax.random.key(seed), 5)
    return {
        "traces": bell_draw(arg_keys[0], (CHANNELS, N_FREQ * SPAN), 1.0, 6.0, ((0, 32), (1, 16))),
        "segment_offsets": draw_segment_offsets(jax.random.fold_in(arg_keys[4], 71), 0),
        "channel_order": jax.vmap(lambda own: jax.random.permutation(own, CH_DEV))(jax.random.split(arg_keys[2], GROUPS)).reshape((GROUPS, CH_DEV)).astype(jnp.int32),
        "pilot_channel": jax.random.randint(arg_keys[3], (1,), 0, CHANNELS).astype(jnp.int32),
    }


def build_table(length, bin_count, blocks):
    sample = jnp.arange(length, dtype=jnp.int32)[:, None]
    which_bin = jnp.arange(bin_count, dtype=jnp.int32)[None, :] + 1
    residue = sample * which_bin % length
    phase_angle = residue.astype(jnp.float32) * (2.0 * math.pi / length)
    factor = 1.0 / math.sqrt(length)
    cosine = jnp.cos(phase_angle) * factor
    sine = -jnp.sin(phase_angle) * factor
    width_block = bin_count // blocks
    stacked = jnp.stack([cosine.reshape(length, blocks, width_block), sine.reshape(length, blocks, width_block)], axis=2)
    return stacked.reshape(length, 2 * bin_count).astype(jnp.bfloat16)

def whiten(spectra, pilot_spec, blocks):
    seg_count, chan_count, columns = spectra.shape
    width_block = columns // (2 * blocks)
    parts = spectra.reshape(seg_count, chan_count, blocks, 2, width_block)
    guide = pilot_spec.astype(jnp.float32).reshape(seg_count, 1, blocks, 2, width_block)
    real_x = parts[:, :, :, 0]
    imag_x = parts[:, :, :, 1]
    real_p = guide[:, :, :, 0]
    imag_p = guide[:, :, :, 1]
    real_z = real_x * real_p + imag_x * imag_p
    imag_z = imag_x * real_p - real_x * imag_p
    energy = real_z * real_z + imag_z * imag_z
    average = lax.optimization_barrier(jnp.mean(energy, axis=(2, 3), keepdims=True))
    factor = lax.rsqrt(energy + 0.1 * average + 1e-06)
    return jnp.stack([real_z * factor, imag_z * factor], axis=3).reshape(seg_count, chan_count, columns).astype(jnp.bfloat16)

def cross_stack(first_block, second_block, blocks):
    seg_count, chan_count, columns = first_block.shape
    width_block = columns // (2 * blocks)
    first = first_block.astype(jnp.float32).reshape(seg_count, chan_count, blocks, 2, width_block)
    second = second_block.astype(jnp.float32).reshape(seg_count, chan_count, blocks, 2, width_block)

    def product(left_part, right_part):
        return jnp.einsum('sibk,sjbk->ijbk', left_part, right_part, precision=lax.Precision.HIGHEST)
    real_c = product(first[:, :, :, 0], second[:, :, :, 0]) + product(first[:, :, :, 1], second[:, :, :, 1])
    imag_c = product(first[:, :, :, 1], second[:, :, :, 0]) - product(first[:, :, :, 0], second[:, :, :, 1])
    factor = 1.0 / math.sqrt(seg_count)
    return (jnp.stack([real_c, imag_c], axis=3) * factor).reshape(chan_count, chan_count, columns)

def reference(traces, segment_offsets, channel_order, pilot_channel):
    dft_table = build_table(L, K, N_FREQ).astype(jnp.float32)
    seg_index = jnp.arange(SEGMENTS, dtype=jnp.int32)
    window_starts = (seg_index // SEG_DEV * SPAN + seg_index % SEG_DEV * L + segment_offsets).astype(jnp.int32)

    def spectra_of(group_index):
        records = lax.dynamic_slice_in_dim(traces, (group_index * CH_DEV).astype(jnp.int32), CH_DEV, 0)
        order_row = lax.dynamic_index_in_dim(channel_order, group_index, 0, keepdims=False)
        picked = jnp.take(records, order_row, axis=0)
        windows = jax.vmap(lambda window_start: lax.dynamic_slice_in_dim(picked, window_start, L, 1))(window_starts)
        flat = jnp.dot(windows.astype(jnp.float32).reshape(-1, L), dft_table, precision=lax.Precision.HIGHEST)
        return flat.reshape(SEGMENTS, CH_DEV, 2 * K)
    owner_group = (pilot_channel[0] // CH_DEV).astype(jnp.int32)
    owner_spectra = spectra_of(owner_group)
    pilot_spec = lax.dynamic_index_in_dim(owner_spectra, (pilot_channel[0] % CH_DEV).astype(jnp.int32), 1, keepdims=False).astype(jnp.bfloat16)
    group_ids = jnp.arange(GROUPS, dtype=jnp.int32)
    whitened = lax.map(lambda group_index: whiten(spectra_of(group_index), pilot_spec, N_FREQ), group_ids)

    def pair_block(group_index):
        own_block = whitened[group_index]
        nearest = whitened[(group_index - 1) % GROUPS]
        farther = whitened[(group_index - 2) % GROUPS]
        return jnp.stack([cross_stack(own_block, nearest, N_FREQ), cross_stack(own_block, farther, N_FREQ)]).astype(jnp.bfloat16)
    stacked = lax.map(pair_block, group_ids)
    return stacked.transpose(1, 0, 2, 3, 4).reshape(2, CHANNELS, CH_DEV, 2 * K)
```

```python
import functools
import math

import jax
import jax.numpy as jnp
import ml_dtypes
import numpy as np
from jax import lax
from jax.experimental import pallas as pl
from jax.experimental.pallas import tpu as pltpu
from jax.sharding import PartitionSpec as P

L = 2048
HALF = 1024
BANDS = 16
SEG = 4
CH = 32
PAIRS = 32
SPAN = 9216
ROWS = SEG * PAIRS
LANES = 128
BANDS_STEP = 2
BF16 = jnp.bfloat16
F32 = jnp.float32


def half_table():
    band, parity, pair = np.ogrid[:BANDS, :2, :PAIRS]
    which_bin = 64 * band + 2 * pair + parity + 1
    sample = np.arange(HALF)
    residue = (which_bin[..., None] * sample) % L
    phase_angle = residue.astype(np.float32) * np.float32(2.0 * math.pi / L)
    factor = np.float32(1.0 / math.sqrt(L))
    cosine = np.cos(phase_angle) * factor
    sine = -np.sin(phase_angle) * factor
    return np.concatenate([cosine, sine], axis=2).astype(ml_dtypes.bfloat16)


def lane_index(rows):
    return lax.broadcasted_iota(jnp.int32, (rows, LANES), 1)


def cut_windows(offset_ref, order_ref, traces_ref, wave_ref):
    lane = lane_index(CH)
    row = lax.broadcasted_iota(jnp.int32, (CH, CH), 0)
    picked = jnp.zeros((CH, CH), jnp.int32)
    for channel in range(CH):
        picked = jnp.where(row == channel, order_ref[0, channel], picked)
    chosen = (lax.broadcasted_iota(jnp.int32, (CH, CH), 1) == picked).astype(F32).astype(BF16)
    tiles = L // LANES
    for seg in range(SEG):
        start = seg * L + offset_ref[seg]
        base = jnp.minimum((start // LANES) * LANES, SPAN - (L + LANES))
        base = pl.multiple_of(base, LANES)
        rest = start - base
        turn = lax.rem(LANES - rest, LANES)
        rolled = []
        for tile in range(tiles + 1):
            part = traces_ref[:, pl.ds(pl.multiple_of(base + tile * LANES, LANES), LANES)]
            rolled.append(pltpu.roll(part.astype(F32), turn, 1))
        window = [
            jnp.where(lane < LANES - rest, rolled[tile], rolled[tile + 1]) for tile in range(tiles)
        ]
        rows = pl.ds(seg * CH, CH)
        for parity in range(2):
            sign = -1.0 if parity == 0 else 1.0
            folded = jnp.concatenate(
                [window[t] + sign * window[t + tiles // 2] for t in range(tiles // 2)], axis=1
            ).astype(BF16)
            wave_ref[parity, rows, :] = jnp.dot(
                chosen, folded, preferred_element_type=F32
            ).astype(BF16)


def spectra_kernel(
    offset_ref, order_ref, pilot_ref, traces_ref, table_ref, block_ref, guide_ref, wave_ref, power_ref
):
    step = pl.program_id(0)

    @pl.when(step == 0)
    def _():
        power_ref[...] = jnp.zeros_like(power_ref)
        cut_windows(offset_ref, order_ref, traces_ref, wave_ref)

    lane = lane_index(PAIRS)
    channel = lax.rem(pilot_ref[0], CH)
    for local_band in range(BANDS_STEP):
        band = step * BANDS_STEP + local_band
        parts = {}
        for parity in range(2):
            product = lax.dot_general(
                table_ref[local_band, parity],
                wave_ref[parity],
                (((1,), (1,)), ((), ())),
                preferred_element_type=F32,
            )
            for side in range(2):
                parts[side, parity] = product[side * PAIRS : (side + 1) * PAIRS]
            real = parts[0, parity].astype(BF16).astype(F32)
            imag = parts[1, parity].astype(BF16).astype(F32)
            place = 2 * band + parity
            power = pltpu.roll(real * real + imag * imag, lax.rem(place - channel + LANES, LANES), 1)
            power_ref[...] = jnp.where(lane % 32 == place, power, power_ref[...])
        for seg in range(SEG):
            line = None
            for side in range(2):
                for parity in range(2):
                    group = side * 2 + parity
                    part = parts[side, parity]
                    if group != seg:
                        part = pltpu.roll(part, (group - seg) * 32 % LANES, 1)
                    line = part if line is None else jnp.where(lane // 32 == group, part, line)
            block_ref[local_band, seg * PAIRS : (seg + 1) * PAIRS, :] = line.astype(BF16)

    @pl.when(step == BANDS // BANDS_STEP - 1)
    def _():
        guide_ref[...] = jnp.sqrt(power_ref[...]).astype(BF16)


def spectra_of(offsets, order, pilot, traces, table):
    steps = BANDS // BANDS_STEP
    smem = pl.BlockSpec(memory_space=pltpu.SMEM)
    return pl.pallas_call(
        spectra_kernel,
        grid=(steps,),
        in_specs=[
            smem,
            smem,
            smem,
            pl.BlockSpec((CH, SPAN), lambda i: (0, 0)),
            pl.BlockSpec((BANDS_STEP, 2, 2 * PAIRS, HALF), lambda i: (i, 0, 0, 0)),
        ],
        out_specs=[
            pl.BlockSpec((BANDS_STEP, ROWS, LANES), lambda i: (i, 0, 0)),
            pl.BlockSpec((PAIRS, LANES), lambda i: (0, 0)),
        ],
        out_shape=[
            jax.ShapeDtypeStruct((BANDS, ROWS, LANES), BF16),
            jax.ShapeDtypeStruct((PAIRS, LANES), BF16),
        ],
        scratch_shapes=[
            pltpu.VMEM((2, SEG * CH, HALF), BF16),
            pltpu.VMEM((PAIRS, LANES), F32),
        ],
        compiler_params=pltpu.CompilerParams(vmem_limit_bytes=32 * 1024 * 1024),
        name="spectra",
    )(offsets, order, pilot, traces, table)


def level_kernel(pilot_ref, guides_ref, block_ref, note_ref, turned_ref):
    owner = pilot_ref[0] // (2 * CH)
    guide = guides_ref[owner].astype(F32)
    lane = lane_index(PAIRS)
    even = (lane // 32) % 2 == 0
    totals = [jnp.zeros((PAIRS, LANES), F32) for _ in range(SEG)]
    for band in range(BANDS):
        for seg in range(SEG):
            first = 32 * seg + 2 * band
            weight = jnp.where(even, guide[:, first : first + 1], guide[:, first + 1 : first + 2])
            part = block_ref[band, seg * PAIRS : (seg + 1) * PAIRS, :].astype(F32) * weight
            totals[seg] = totals[seg] + part * part
    levels = []
    for seg in range(SEG):
        total = jnp.sum(totals[seg], axis=0, keepdims=True)
        total = jnp.broadcast_to(total, (8, LANES))
        total = total + pltpu.roll(total, 64, 1)
        total = total + pltpu.roll(total, 32, 1)
        levels.append((total * (0.1 / (64.0 * BANDS)) + 1e-06)[:1])
    level = jnp.concatenate(levels + levels, axis=0)
    turned_ref[...] = jnp.transpose(
        jnp.concatenate([guide] * (LANES // PAIRS), axis=0)
    )
    for band in range(BANDS):
        even_rows = turned_ref[pl.ds(2 * band, SEG, stride=32), :]
        odd_rows = turned_ref[pl.ds(2 * band + 1, SEG, stride=32), :]
        note_ref[band] = jnp.concatenate([even_rows, odd_rows, level], axis=0).astype(BF16)


def notes_of(pilot, guides, blocks):
    vmem = pl.BlockSpec(memory_space=pltpu.VMEM)
    return pl.pallas_call(
        level_kernel,
        in_specs=[pl.BlockSpec(memory_space=pltpu.SMEM), vmem, vmem],
        out_specs=vmem,
        out_shape=jax.ShapeDtypeStruct((BANDS, 16, LANES), BF16),
        scratch_shapes=[pltpu.VMEM((LANES, LANES), F32)],
        compiler_params=pltpu.CompilerParams(vmem_limit_bytes=32 * 1024 * 1024),
        name="level",
    )(pilot, guides, blocks)


def cross_kernel(
    own_ref, near_ref, far_ref, own_note_ref, near_note_ref, far_note_ref, out_ref,
    own_white, near_white, far_white, stack_ref, guide_ref,
):
    lane = lane_index(PAIRS)
    even = (lane // 32) % 2 == 0
    rows = jnp.concatenate([own_note_ref[t, :8, :] for t in range(BANDS)], axis=0).astype(F32)
    guide_ref[...] = jnp.transpose(rows)[:PAIRS]
    for window in range(BANDS):
        for seg in range(SEG):
            first = 8 * window + seg
            guide = jnp.where(
                even, guide_ref[:, first : first + 1], guide_ref[:, first + 4 : first + 5]
            )
            for block_ref, note_ref, white_ref in (
                (own_ref, own_note_ref, own_white),
                (near_ref, near_note_ref, near_white),
                (far_ref, far_note_ref, far_white),
            ):
                value = block_ref[window, seg * PAIRS : (seg + 1) * PAIRS, :].astype(F32) * guide
                energy = value * value
                energy = energy + pltpu.roll(energy, 64, 1)
                level = note_ref[window, 8 + seg : 9 + seg, :].astype(F32)
                at = window * ROWS + seg * PAIRS
                white_ref[at : at + PAIRS, :] = value * lax.rsqrt(energy + level)

    wide = lane_index(BANDS * SEG)
    even_wide = (wide // 32) % 2 == 0
    sign = jnp.where(lane < 64, 1.0, -1.0)

    def bin_pair(pair, carry):
        at = pl.ds(pair, BANDS * SEG, stride=PAIRS)
        own = jnp.transpose(own_white[at, :]).astype(BF16)
        near = near_white[at, :]
        far = far_white[at, :]
        mixes = (
            jnp.where(even_wide, near, pltpu.roll(far, 32, 1)),
            jnp.where(even_wide, pltpu.roll(near, 96, 1), far),
        )
        for parity in range(2):
            left = jnp.concatenate(
                [own[parity * 32 : parity * 32 + 32], own[64 + parity * 32 : 96 + parity * 32]], axis=0
            )
            product = jnp.dot(left, mixes[parity].astype(BF16), preferred_element_type=F32)
            value = sign * product[:CH] + pltpu.roll(product[CH:], 64, 1)
            stack_ref[pl.ds(pl.multiple_of((2 * pair + parity) * CH, CH), CH), :] = value
        return carry

    lax.fori_loop(0, PAIRS, bin_pair, 0, unroll=4)

    full = lane_index(64)
    low = full < 64
    for half in range(CH // 2):
        first = stack_ref[pl.ds(2 * half, 64, stride=CH), :]
        second = stack_ref[pl.ds(2 * half + 1, 64, stride=CH), :]
        turned = jnp.transpose(jnp.concatenate([first, second], axis=0)) * 0.125
        real = turned[:64]
        imag = turned[64:]
        lines = (
            jnp.where(low, real, pltpu.roll(imag, 64, 1)),
            jnp.where(low, pltpu.roll(real, 64, 1), imag),
        )
        for k in range(2):
            for back in range(2):
                out_ref[back, 2 * half + k] = lines[k][back * 32 : back * 32 + 32].astype(BF16)


def cross_of(blocks, notes):
    vmem = pl.BlockSpec(memory_space=pltpu.VMEM)
    white = pltpu.VMEM((BANDS * ROWS, LANES), F32)
    return pl.pallas_call(
        cross_kernel,
        in_specs=[vmem] * 6,
        out_specs=vmem,
        out_shape=jax.ShapeDtypeStruct((2, CH, CH, LANES), BF16),
        scratch_shapes=[
            white,
            white,
            white,
            pltpu.VMEM((64 * CH, LANES), F32),
            pltpu.VMEM((PAIRS, LANES), F32),
        ],
        compiler_params=pltpu.CompilerParams(vmem_limit_bytes=48 * 1024 * 1024),
        name="cross",
    )(*blocks, *notes)


def shifted(value, steps):
    pairs = [(source, (source + steps) % 32) for source in range(32)]
    return lax.ppermute(value, "rgrp", pairs)


def local(table, traces, segment_offsets, channel_order, pilot_channel):
    blocks, guide = spectra_of(segment_offsets, channel_order, pilot_channel, traces, table)
    banded = lax.all_to_all(blocks, "freq", split_axis=0, concat_axis=0, tiled=True)

    group = lax.axis_index("rgrp")
    owner_side = (pilot_channel[0] // CH) % 2
    other = lax.ppermute(guide, "rgrp", [(g, g ^ 1) for g in range(32)])
    guide = jnp.where(group % 2 == owner_side, guide, other)
    lines = [[2 * z + side for z in range(16)] for side in range(2)]
    guides = lax.all_to_all(
        jnp.broadcast_to(guide, (16, PAIRS, LANES)),
        "rgrp",
        split_axis=0,
        concat_axis=0,
        tiled=True,
        axis_index_groups=lines,
    )
    notes = notes_of(pilot_channel, guides, blocks)
    own_note = lax.all_to_all(notes, "freq", split_axis=0, concat_axis=0, tiled=True)
    return cross_of(
        (banded, shifted(banded, 1), shifted(banded, 2)),
        (own_note, shifted(own_note, 1), shifted(own_note, 2)),
    )


def solution(mesh):
    table = half_table()
    specs = (P(), P("rgrp", "freq"), P("freq"), P("rgrp", None), P())
    inner = jax.shard_map(
        local, mesh=mesh, in_specs=specs, out_specs=P(None, "rgrp", None, "freq"), check_vma=False
    )

    def run(traces, segment_offsets, channel_order, pilot_channel):
        return inner(jnp.asarray(table), traces, segment_offsets, channel_order, pilot_channel)

    return run
```

```python
import functools
import math

import jax
import jax.numpy as jnp
import ml_dtypes
import numpy as np
from jax import lax
from jax.experimental import pallas as pl
from jax.experimental.pallas import tpu as pltpu
from jax.sharding import PartitionSpec as P

L = 2048
HALF = 1024
BANDS = 16
SEG = 4
CH = 32
PAIRS = 32
SPAN = 9216
ROWS = SEG * PAIRS
LANES = 128
BF16 = jnp.bfloat16
F32 = jnp.float32


def half_table():
    band, parity, pair = np.ogrid[:BANDS, :2, :PAIRS]
    which_bin = 64 * band + 2 * pair + parity + 1
    sample = np.arange(HALF)
    residue = (which_bin[..., None] * sample) % L
    phase_angle = residue.astype(np.float32) * np.float32(2.0 * math.pi / L)
    factor = np.float32(1.0 / math.sqrt(L))
    cosine = np.cos(phase_angle) * factor
    sine = -np.sin(phase_angle) * factor
    return np.concatenate([cosine, sine], axis=2).astype(ml_dtypes.bfloat16)


def lane_index(rows):
    return lax.broadcasted_iota(jnp.int32, (rows, LANES), 1)


def cut_windows(offset_ref, order_ref, traces_ref, wave_ref):
    lane = lane_index(CH)
    row = lax.broadcasted_iota(jnp.int32, (CH, CH), 0)
    picked = jnp.zeros((CH, CH), jnp.int32)
    for channel in range(CH):
        picked = jnp.where(row == channel, order_ref[0, channel], picked)
    chosen = (lax.broadcasted_iota(jnp.int32, (CH, CH), 1) == picked).astype(F32).astype(BF16)
    tiles = L // LANES
    for seg in range(SEG):
        start = seg * L + offset_ref[seg]
        base = jnp.minimum((start // LANES) * LANES, SPAN - (L + LANES))
        base = pl.multiple_of(base, LANES)
        rest = start - base
        turn = lax.rem(LANES - rest, LANES)
        rolled = []
        for tile in range(tiles + 1):
            part = traces_ref[:, pl.ds(pl.multiple_of(base + tile * LANES, LANES), LANES)]
            rolled.append(pltpu.roll(part.astype(F32), turn, 1))
        window = [
            jnp.where(lane < LANES - rest, rolled[tile], rolled[tile + 1]) for tile in range(tiles)
        ]
        rows = pl.ds(seg * CH, CH)
        for parity in range(2):
            sign = -1.0 if parity == 0 else 1.0
            folded = jnp.concatenate(
                [window[t] + sign * window[t + tiles // 2] for t in range(tiles // 2)], axis=1
            ).astype(BF16)
            wave_ref[parity, rows, :] = jnp.dot(
                chosen, folded, preferred_element_type=F32
            ).astype(BF16)


def spectra_kernel(
    offset_hbm, order_hbm, pilot_hbm, traces_hbm, table_hbm, block_ref, guide_ref,
    offset_ref, order_ref, pilot_ref, traces_ref, table_ref, wave_ref, power_ref, sems, table_sems,
):
    small = [
        pltpu.make_async_copy(source, target, sems.at[k])
        for k, (source, target) in enumerate(
            (
                (offset_hbm, offset_ref),
                (order_hbm, order_ref),
                (pilot_hbm, pilot_ref),
                (traces_hbm, traces_ref),
            )
        )
    ]
    for copy in small:
        copy.start()
    for part in range(4):
        pltpu.make_async_copy(
            table_hbm.at[pl.ds(4 * part, 4)], table_ref.at[pl.ds(4 * part, 4)], table_sems.at[part]
        ).start()
    power_ref[...] = jnp.zeros_like(power_ref)
    for copy in small:
        copy.wait()
    cut_windows(offset_ref, order_ref, traces_ref, wave_ref)

    lane = lane_index(PAIRS)
    channel = lax.rem(pilot_ref[0], CH)
    for quarter in range(4):
        pltpu.make_async_copy(
            table_hbm.at[pl.ds(4 * quarter, 4)],
            table_ref.at[pl.ds(4 * quarter, 4)],
            table_sems.at[quarter],
        ).wait()
        for local_band in range(4):
            band = quarter * 4 + local_band
            parts = {}
            for parity in range(2):
                product = lax.dot_general(
                    table_ref[band, parity],
                    wave_ref[parity],
                    (((1,), (1,)), ((), ())),
                    preferred_element_type=F32,
                )
                for side in range(2):
                    parts[side, parity] = product[side * PAIRS : (side + 1) * PAIRS]
                real = parts[0, parity].astype(BF16).astype(F32)
                imag = parts[1, parity].astype(BF16).astype(F32)
                place = 2 * band + parity
                power = pltpu.roll(
                    real * real + imag * imag, lax.rem(place - channel + LANES, LANES), 1
                )
                power_ref[...] = jnp.where(lane % 32 == place, power, power_ref[...])
            for seg in range(SEG):
                line = None
                for side in range(2):
                    for parity in range(2):
                        group = side * 2 + parity
                        part = parts[side, parity]
                        if group != seg:
                            part = pltpu.roll(part, (group - seg) * 32 % LANES, 1)
                        line = part if line is None else jnp.where(lane // 32 == group, part, line)
                block_ref[band, seg * PAIRS : (seg + 1) * PAIRS, :] = line
    mine = pilot_ref[0] // CH == lax.axis_index("rgrp")
    guide_ref[...] = jnp.where(mine, jnp.sqrt(power_ref[...]), 0.0).astype(BF16)


def spectra_of(offsets, order, pilot, traces, table):
    vmem = pl.BlockSpec(memory_space=pltpu.VMEM)
    return pl.pallas_call(
        spectra_kernel,
        in_specs=[pl.BlockSpec(memory_space=pl.ANY)] * 5,
        out_specs=[vmem, vmem],
        out_shape=[
            jax.ShapeDtypeStruct((BANDS, ROWS, LANES), F32),
            jax.ShapeDtypeStruct((PAIRS, LANES), BF16),
        ],
        scratch_shapes=[
            pltpu.SMEM((SEG,), jnp.int32),
            pltpu.SMEM((1, CH), jnp.int32),
            pltpu.SMEM((1,), jnp.int32),
            pltpu.VMEM((CH, SPAN), BF16),
            pltpu.VMEM((BANDS, 2, 2 * PAIRS, HALF), BF16),
            pltpu.VMEM((2, SEG * CH, HALF), BF16),
            pltpu.VMEM((PAIRS, LANES), F32),
            pltpu.SemaphoreType.DMA((4,)),
            pltpu.SemaphoreType.DMA((4,)),
        ],
        compiler_params=pltpu.CompilerParams(vmem_limit_bytes=56 * 1024 * 1024),
        name="spectra",
    )(offsets, order, pilot, traces, table)


def whiten_kernel(guides_ref, block_ref, white_ref, value_ref, guide_ref):
    guide = guides_ref[0].astype(F32)
    for line in range(1, 16):
        guide = guide + guides_ref[line].astype(F32)
    guide_ref[...] = guide
    lane = lane_index(PAIRS)
    even = (lane // 32) % 2 == 0
    totals = [jnp.zeros((PAIRS, LANES), F32) for _ in range(SEG)]
    for band in range(BANDS):
        for seg in range(SEG):
            first = 32 * seg + 2 * band
            rows = slice(seg * PAIRS, (seg + 1) * PAIRS)
            weight = jnp.where(
                even, guide_ref[:, first : first + 1], guide_ref[:, first + 1 : first + 2]
            )
            value = block_ref[band, rows, :] * weight
            value_ref[band, rows, :] = value
            totals[seg] = totals[seg] + value * value
    levels = []
    for seg in range(SEG):
        total = jnp.sum(totals[seg], axis=0, keepdims=True)
        total = jnp.broadcast_to(total, (8, LANES))
        total = total + pltpu.roll(total, 64, 1)
        total = total + pltpu.roll(total, 32, 1)
        levels.append((total * (0.1 / (64.0 * BANDS)) + 1e-06)[:1])
    for band in range(BANDS):
        for seg in range(SEG):
            rows = slice(seg * PAIRS, (seg + 1) * PAIRS)
            value = value_ref[band, rows, :]
            energy = value * value
            energy = energy + pltpu.roll(energy, 64, 1)
            white_ref[band, rows, :] = (value * lax.rsqrt(energy + levels[seg])).astype(BF16)


def whitened_of(guides, blocks):
    vmem = pl.BlockSpec(memory_space=pltpu.VMEM)
    return pl.pallas_call(
        whiten_kernel,
        in_specs=[vmem, vmem],
        out_specs=vmem,
        out_shape=jax.ShapeDtypeStruct((BANDS, ROWS, LANES), BF16),
        scratch_shapes=[pltpu.VMEM((BANDS, ROWS, LANES), F32), pltpu.VMEM((PAIRS, LANES), F32)],
        compiler_params=pltpu.CompilerParams(vmem_limit_bytes=32 * 1024 * 1024),
        name="whiten",
    )(guides, blocks)


def gather_kernel(band_ref, right_ref, wide_ref):
    for window in range(BANDS):
        wide_ref[window * ROWS : (window + 1) * ROWS, :] = band_ref[window].astype(F32)

    def bin_pair(pair, carry):
        right_ref[pair] = wide_ref[pl.ds(pair, BANDS * SEG, stride=PAIRS), :].astype(BF16)
        return carry

    lax.fori_loop(0, PAIRS, bin_pair, 0, unroll=4)


def gathered_of(banded):
    vmem = pl.BlockSpec(memory_space=pltpu.VMEM)
    return pl.pallas_call(
        gather_kernel,
        in_specs=[vmem],
        out_specs=vmem,
        out_shape=jax.ShapeDtypeStruct((PAIRS, BANDS * SEG, LANES), BF16),
        scratch_shapes=[pltpu.VMEM((BANDS * ROWS, LANES), F32)],
        compiler_params=pltpu.CompilerParams(vmem_limit_bytes=32 * 1024 * 1024),
        name="gather",
    )(banded)


def left_kernel(right_ref, left_ref):
    def bin_pair(pair, carry):
        turned = jnp.transpose(right_ref[pair].astype(F32))
        left_ref[pair] = jnp.concatenate([turned[:64], turned[64:]], axis=1).astype(BF16)
        return carry

    lax.fori_loop(0, PAIRS, bin_pair, 0, unroll=4)


def left_of(right):
    vmem = pl.BlockSpec(memory_space=pltpu.VMEM)
    return pl.pallas_call(
        left_kernel,
        in_specs=[vmem],
        out_specs=vmem,
        out_shape=jax.ShapeDtypeStruct((PAIRS, 2 * CH, LANES), BF16),
        compiler_params=pltpu.CompilerParams(vmem_limit_bytes=32 * 1024 * 1024),
        name="left",
    )(right)


def cross_one(left_ref, right_ref, stack_ref, store):
    side = jnp.where(lane_index(BANDS * SEG) < 64, 1.0, -1.0)

    def bin_pair(pair, carry):
        right = right_ref[pair].astype(F32)
        mix = jnp.concatenate([right * side, pltpu.roll(right, 64, 1)], axis=0).astype(BF16)
        product = jnp.dot(left_ref[pair], mix, preferred_element_type=F32)
        stack_ref[pl.ds(pl.multiple_of(pair * 2 * CH, 2 * CH), 2 * CH), :] = product
        return carry

    lax.fori_loop(0, PAIRS, bin_pair, 0, unroll=4)

    lane = lane_index(CH)
    low = lane < 64
    even = lane % 2 == 0
    for half in range(CH // 2):
        first = stack_ref[pl.ds(2 * half, 64, stride=CH), :]
        second = stack_ref[pl.ds(2 * half + 1, 64, stride=CH), :]
        turned = jnp.transpose(jnp.concatenate([first, second], axis=0)) * 0.125
        real = jnp.where(even, turned[:32], turned[32:64])
        imag = jnp.where(even, turned[64:96], turned[96:])
        store(2 * half, jnp.where(low, real, pltpu.roll(imag, 64, 1)).astype(BF16))
        store(2 * half + 1, jnp.where(low, pltpu.roll(real, 64, 1), imag).astype(BF16))


def near_kernel(left_ref, right_ref, out_ref, stack_ref):
    def store(channel, lines):
        out_ref[channel] = lines

    cross_one(left_ref, right_ref, stack_ref, store)


def far_kernel(left_ref, right_ref, near_ref, out_ref, stack_ref):
    def store(channel, lines):
        out_ref[1, channel] = lines

    out_ref[0] = near_ref[...]
    cross_one(left_ref, right_ref, stack_ref, store)


def cross_of(kernel, shape, *arrays):
    vmem = pl.BlockSpec(memory_space=pltpu.VMEM)
    return pl.pallas_call(
        kernel,
        in_specs=[vmem] * len(arrays),
        out_specs=vmem,
        out_shape=jax.ShapeDtypeStruct(shape, BF16),
        scratch_shapes=[pltpu.VMEM((64 * CH, LANES), F32)],
        compiler_params=pltpu.CompilerParams(vmem_limit_bytes=32 * 1024 * 1024),
        name=kernel.__name__,
    )(*arrays)


def shifted(value, steps):
    pairs = [(source, (source + steps) % 32) for source in range(32)]
    return lax.ppermute(value, "rgrp", pairs)


def local(table, traces, segment_offsets, channel_order, pilot_channel):
    blocks, guide = spectra_of(segment_offsets, channel_order, pilot_channel, traces, table)
    guide = guide + lax.ppermute(guide, "rgrp", [(g, g ^ 1) for g in range(32)])
    lines = [[2 * z + side for z in range(16)] for side in range(2)]
    guides = lax.all_to_all(
        jnp.broadcast_to(guide, (16, PAIRS, LANES)),
        "rgrp",
        split_axis=0,
        concat_axis=0,
        tiled=True,
        axis_index_groups=lines,
    )
    white = whitened_of(guides, blocks)
    banded = lax.all_to_all(white, "freq", split_axis=0, concat_axis=0, tiled=True)
    own = gathered_of(banded)
    near, far = shifted(own, 1), shifted(own, 2)
    left = left_of(own)
    first = cross_of(near_kernel, (CH, CH, LANES), left, near)
    return cross_of(far_kernel, (2, CH, CH, LANES), left, far, first)


def solution(mesh):
    table = half_table()
    specs = (P(), P("rgrp", "freq"), P("freq"), P("rgrp", None), P())
    inner = jax.shard_map(
        local, mesh=mesh, in_specs=specs, out_specs=P(None, "rgrp", None, "freq"), check_vma=False
    )

    def run(traces, segment_offsets, channel_order, pilot_channel):
        return inner(jnp.asarray(table), traces, segment_offsets, channel_order, pilot_channel)

    return run
```

```python
import functools
import math

import jax
import jax.numpy as jnp
import ml_dtypes
import numpy as np
from jax import lax
from jax.experimental import pallas as pl
from jax.experimental.pallas import tpu as pltpu
from jax.sharding import PartitionSpec as P

L = 2048
HALF = 1024
BANDS = 16
SEG = 4
CH = 32
PAIRS = 32
SPAN = 9216
ROWS = SEG * PAIRS
LANES = 128
CHIPS = 8
BF16 = jnp.bfloat16
F32 = jnp.float32


def half_table():
    band, parity, pair = np.ogrid[:BANDS, :2, :PAIRS]
    which_bin = 64 * band + 2 * pair + parity + 1
    sample = np.arange(HALF)
    residue = (which_bin[..., None] * sample) % L
    phase_angle = residue.astype(np.float32) * np.float32(2.0 * math.pi / L)
    factor = np.float32(1.0 / math.sqrt(L))
    cosine = np.cos(phase_angle) * factor
    sine = -np.sin(phase_angle) * factor
    return np.concatenate([cosine, sine], axis=2).astype(ml_dtypes.bfloat16)


def lane_index(rows):
    return lax.broadcasted_iota(jnp.int32, (rows, LANES), 1)


def relative(band):
    mine = lax.axis_index("freq")
    place = (band // 8 + mine // 8) % 2 * 4 + ((band // 2) % 4 - (mine // 2) % 4 + 4) % 4
    return (band + mine) % 2 == 0, place


def cut_windows(offset_ref, order_ref, traces_ref, wave_ref):
    lane = lane_index(CH)
    row = lax.broadcasted_iota(jnp.int32, (CH, CH), 0)
    picked = jnp.zeros((CH, CH), jnp.int32)
    for channel in range(CH):
        picked = jnp.where(row == channel, order_ref[0, channel], picked)
    chosen = (lax.broadcasted_iota(jnp.int32, (CH, CH), 1) == picked).astype(F32).astype(BF16)
    tiles = L // LANES
    for seg in range(SEG):
        start = seg * L + offset_ref[seg]
        base = jnp.minimum((start // LANES) * LANES, SPAN - (L + LANES))
        base = pl.multiple_of(base, LANES)
        rest = start - base
        turn = lax.rem(LANES - rest, LANES)
        rolled = []
        for tile in range(tiles + 1):
            part = traces_ref[:, pl.ds(pl.multiple_of(base + tile * LANES, LANES), LANES)]
            rolled.append(pltpu.roll(part.astype(F32), turn, 1))
        window = [
            jnp.where(lane < LANES - rest, rolled[tile], rolled[tile + 1]) for tile in range(tiles)
        ]
        rows = pl.ds(seg * CH, CH)
        for parity in range(2):
            sign = -1.0 if parity == 0 else 1.0
            folded = jnp.concatenate(
                [window[t] + sign * window[t + tiles // 2] for t in range(tiles // 2)], axis=1
            ).astype(BF16)
            wave_ref[parity, rows, :] = jnp.dot(
                chosen, folded, preferred_element_type=F32
            ).astype(BF16)


def spectra_kernel(
    offset_hbm, order_hbm, pilot_hbm, traces_hbm, table_hbm, same_ref, other_ref, guide_ref,
    offset_ref, order_ref, pilot_ref, traces_ref, table_ref, wave_ref, power_ref, sems, table_sems,
):
    small = [
        pltpu.make_async_copy(source, target, sems.at[k])
        for k, (source, target) in enumerate(
            (
                (offset_hbm, offset_ref),
                (order_hbm, order_ref),
                (pilot_hbm, pilot_ref),
                (traces_hbm, traces_ref),
            )
        )
    ]
    for copy in small:
        copy.start()
    for part in range(4):
        pltpu.make_async_copy(
            table_hbm.at[pl.ds(4 * part, 4)], table_ref.at[pl.ds(4 * part, 4)], table_sems.at[part]
        ).start()
    power_ref[...] = jnp.zeros_like(power_ref)
    for copy in small:
        copy.wait()
    cut_windows(offset_ref, order_ref, traces_ref, wave_ref)

    lane = lane_index(PAIRS)
    channel = lax.rem(pilot_ref[0], CH)
    for quarter in range(4):
        pltpu.make_async_copy(
            table_hbm.at[pl.ds(4 * quarter, 4)],
            table_ref.at[pl.ds(4 * quarter, 4)],
            table_sems.at[quarter],
        ).wait()
        for local_band in range(4):
            band = quarter * 4 + local_band
            parts = {}
            for parity in range(2):
                product = lax.dot_general(
                    table_ref[band, parity],
                    wave_ref[parity],
                    (((1,), (1,)), ((), ())),
                    preferred_element_type=F32,
                )
                for side in range(2):
                    parts[side, parity] = product[side * PAIRS : (side + 1) * PAIRS]
                real = parts[0, parity].astype(BF16).astype(F32)
                imag = parts[1, parity].astype(BF16).astype(F32)
                place = 2 * band + parity
                power = pltpu.roll(
                    real * real + imag * imag, lax.rem(place - channel + LANES, LANES), 1
                )
                power_ref[...] = jnp.where(lane % 32 == place, power, power_ref[...])
            lines = []
            for seg in range(SEG):
                line = None
                for side in range(2):
                    for parity in range(2):
                        group = side * 2 + parity
                        part = parts[side, parity]
                        if group != seg:
                            part = pltpu.roll(part, (group - seg) * 32 % LANES, 1)
                        line = part if line is None else jnp.where(lane // 32 == group, part, line)
                lines.append(line)
            value = jnp.concatenate(lines, axis=0).astype(BF16)
            same_core, place = relative(band)

            @pl.when(same_core)
            def _():
                same_ref[place] = value

            @pl.when(jnp.logical_not(same_core))
            def _():
                other_ref[place] = value

    mine = pilot_ref[0] // CH == lax.axis_index("rgrp")
    guide_ref[...] = jnp.where(mine, jnp.sqrt(power_ref[...]), 0.0).astype(BF16)


def spectra_of(offsets, order, pilot, traces, table):
    vmem = pl.BlockSpec(memory_space=pltpu.VMEM)
    offsets, order, traces, table = (
        pltpu.with_memory_space_constraint(value, pltpu.HBM)
        for value in (offsets, order, traces, table)
    )
    return pl.pallas_call(
        spectra_kernel,
        in_specs=[pl.BlockSpec(memory_space=pl.ANY)] * 5,
        out_specs=[vmem, vmem, vmem],
        out_shape=[
            jax.ShapeDtypeStruct((CHIPS, ROWS, LANES), BF16),
            jax.ShapeDtypeStruct((CHIPS, ROWS, LANES), BF16),
            jax.ShapeDtypeStruct((PAIRS, LANES), BF16),
        ],
        scratch_shapes=[
            pltpu.SMEM((SEG,), jnp.int32),
            pltpu.SMEM((1, CH), jnp.int32),
            pltpu.SMEM((1,), jnp.int32),
            pltpu.VMEM((CH, SPAN), BF16),
            pltpu.VMEM((BANDS, 2, 2 * PAIRS, HALF), BF16),
            pltpu.VMEM((2, SEG * CH, HALF), BF16),
            pltpu.VMEM((PAIRS, LANES), F32),
            pltpu.SemaphoreType.DMA((4,)),
            pltpu.SemaphoreType.DMA((4,)),
        ],
        compiler_params=pltpu.CompilerParams(vmem_limit_bytes=16 * 1024 * 1024),
        name="spectra",
    )(offsets, order, pilot, traces, table)


def level_kernel(guides_ref, same_ref, other_ref, note_ref, guide_ref, turned_ref):
    guide = guides_ref[0].astype(F32)
    for line in range(1, 16):
        guide = guide + guides_ref[line].astype(F32)
    guide_ref[...] = guide
    turned_ref[...] = jnp.transpose(jnp.concatenate([guide] * (LANES // PAIRS), axis=0))
    even = (lane_index(PAIRS) // 32) % 2 == 0
    totals = [jnp.zeros((PAIRS, LANES), F32) for _ in range(SEG)]
    for band in range(BANDS):
        same_core, place = relative(band)
        for seg in range(SEG):
            first = 32 * seg + 2 * band
            rows = slice(seg * PAIRS, (seg + 1) * PAIRS)
            weight = jnp.where(
                even, guide_ref[:, first : first + 1], guide_ref[:, first + 1 : first + 2]
            )
            block = jnp.where(same_core, same_ref[place, rows, :], other_ref[place, rows, :])
            value = block.astype(F32) * weight
            totals[seg] = totals[seg] + value * value
    levels = []
    for seg in range(SEG):
        total = jnp.sum(totals[seg], axis=0, keepdims=True)
        total = jnp.broadcast_to(total, (8, LANES))
        total = total + pltpu.roll(total, 64, 1)
        total = total + pltpu.roll(total, 32, 1)
        levels.append((total * (0.1 / (64.0 * BANDS)) + 1e-06)[:1])
    level = jnp.concatenate(levels, axis=0)
    low = lane_index(SEG) < PAIRS
    for band in range(BANDS):
        even_rows = turned_ref[pl.ds(2 * band, SEG, stride=32), :]
        odd_rows = turned_ref[pl.ds(2 * band + 1, SEG, stride=32), :]
        power = jnp.where(low, even_rows, odd_rows)
        note_ref[band] = jnp.concatenate([power, level, power, level], axis=0).astype(BF16)


def notes_of(guides, same, other):
    vmem = pl.BlockSpec(memory_space=pltpu.VMEM)
    return pl.pallas_call(
        level_kernel,
        in_specs=[vmem] * 3,
        out_specs=vmem,
        out_shape=jax.ShapeDtypeStruct((BANDS, 16, LANES), BF16),
        scratch_shapes=[pltpu.VMEM((PAIRS, LANES), F32), pltpu.VMEM((LANES, LANES), F32)],
        compiler_params=pltpu.CompilerParams(vmem_limit_bytes=32 * 1024 * 1024),
        name="level",
    )(guides, same, other)


def merge_kernel(same_ref, other_ref, *out_refs):
    for k, out_ref in enumerate(out_refs):
        out_ref[0] = same_ref[k + 1]
        out_ref[1] = other_ref[k + 1]


def merged_of(same, other):
    vmem = pl.BlockSpec(memory_space=pltpu.VMEM)
    return pl.pallas_call(
        merge_kernel,
        in_specs=[vmem] * 2,
        out_specs=[vmem] * (CHIPS - 1),
        out_shape=[jax.ShapeDtypeStruct((2, ROWS, LANES), BF16)] * (CHIPS - 1),
        compiler_params=pltpu.CompilerParams(vmem_limit_bytes=32 * 1024 * 1024),
        name="merge",
    )(same, other)


def gather_kernel(same_ref, other_ref, *refs):
    part_refs, right_ref, wide_ref = refs[:-2], refs[-2], refs[-1]
    for place in range(CHIPS):
        for core in range(2):
            if place == 0:
                part = (same_ref, other_ref)[core][0]
            else:
                part = part_refs[place - 1][core]
            window = 2 * place + core
            wide_ref[window * ROWS : (window + 1) * ROWS, :] = part.astype(F32)

    def bin_pair(pair, carry):
        right_ref[pair] = wide_ref[pl.ds(pair, BANDS * SEG, stride=PAIRS), :].astype(BF16)
        return carry

    lax.fori_loop(0, PAIRS, bin_pair, 0, unroll=4)


def gathered_of(same, other, parts):
    vmem = pl.BlockSpec(memory_space=pltpu.VMEM)
    return pl.pallas_call(
        gather_kernel,
        in_specs=[vmem] * (1 + CHIPS),
        out_specs=vmem,
        out_shape=jax.ShapeDtypeStruct((PAIRS, BANDS * SEG, LANES), BF16),
        scratch_shapes=[pltpu.VMEM((BANDS * ROWS, LANES), F32)],
        compiler_params=pltpu.CompilerParams(vmem_limit_bytes=32 * 1024 * 1024),
        name="gather",
    )(same, other, *parts)


def note_rows(note_ref, first, wide_ref):
    mine = lax.axis_index("freq")
    for place in range(CHIPS):
        for core in range(2):
            chip = (mine // 8 + place // 4) % 2 * 4 + ((mine // 2) % 4 - place % 4 + 4) % 4
            window = 2 * chip + (mine + core) % 2
            at = (2 * place + core) * SEG
            wide_ref[at : at + SEG, :] = note_ref[window].astype(F32)[first : first + SEG]


def whitened(value, level):
    energy = value * value
    energy = energy + pltpu.roll(energy, 64, 1)
    return value * lax.rsqrt(energy + level)


def left_kernel(right_ref, note_ref, left_ref, power_ref, level_ref, wide_ref):
    note_rows(note_ref, SEG, level_ref)
    note_rows(note_ref, 0, wide_ref)
    level = level_ref[...]
    even = (lane_index(BANDS * SEG) // 32) % 2 == 0
    for pair in range(PAIRS):
        power = jnp.where(
            even, wide_ref[:, pair : pair + 1], wide_ref[:, PAIRS + pair : PAIRS + pair + 1]
        )
        power_ref[pair] = power.astype(BF16)
        white = whitened(right_ref[pair].astype(F32) * power, level)
        turned = jnp.transpose(white)
        left_ref[pair] = jnp.concatenate([turned[:64], turned[64:]], axis=1).astype(BF16)


def left_of(right, note):
    vmem = pl.BlockSpec(memory_space=pltpu.VMEM)
    rows = pltpu.VMEM((BANDS * SEG, LANES), F32)
    return pl.pallas_call(
        left_kernel,
        in_specs=[vmem] * 2,
        out_specs=[vmem] * 2,
        out_shape=[
            jax.ShapeDtypeStruct((PAIRS, 2 * CH, LANES), BF16),
            jax.ShapeDtypeStruct((PAIRS, BANDS * SEG, LANES), BF16),
        ],
        scratch_shapes=[rows, rows],
        compiler_params=pltpu.CompilerParams(vmem_limit_bytes=32 * 1024 * 1024),
        name="left",
    )(right, note)


def cross_one(left_ref, power_ref, right_ref, note_ref, stack_ref, level_ref, store):
    side = jnp.where(lane_index(BANDS * SEG) < 64, 1.0, -1.0)
    note_rows(note_ref, SEG, level_ref)
    level = level_ref[...]

    def bin_pair(pair, carry):
        value = right_ref[pair].astype(F32) * power_ref[pair].astype(F32)
        right = whitened(value, level)
        mix = jnp.concatenate([right * side, pltpu.roll(right, 64, 1)], axis=0).astype(BF16)
        product = jnp.dot(left_ref[pair], mix, preferred_element_type=F32)
        stack_ref[pl.ds(pl.multiple_of(pair * 2 * CH, 2 * CH), 2 * CH), :] = product
        return carry

    lax.fori_loop(0, PAIRS, bin_pair, 0, unroll=4)

    lane = lane_index(CH)
    low = lane < 64
    even = lane % 2 == 0
    for half in range(CH // 2):
        first = stack_ref[pl.ds(2 * half, 64, stride=CH), :]
        second = stack_ref[pl.ds(2 * half + 1, 64, stride=CH), :]
        turned = jnp.transpose(jnp.concatenate([first, second], axis=0)) * 0.125
        real = jnp.where(even, turned[:32], turned[32:64])
        imag = jnp.where(even, turned[64:96], turned[96:])
        store(2 * half, jnp.where(low, real, pltpu.roll(imag, 64, 1)).astype(BF16))
        store(2 * half + 1, jnp.where(low, pltpu.roll(real, 64, 1), imag).astype(BF16))


def near_kernel(left_ref, power_ref, right_ref, note_ref, out_ref, stack_ref, level_ref):
    def store(channel, lines):
        out_ref[channel] = lines

    cross_one(left_ref, power_ref, right_ref, note_ref, stack_ref, level_ref, store)


def far_kernel(left_ref, power_ref, right_ref, note_ref, near_ref, out_ref, stack_ref, level_ref):
    def store(channel, lines):
        out_ref[1, channel] = lines

    out_ref[0] = near_ref[...]
    cross_one(left_ref, power_ref, right_ref, note_ref, stack_ref, level_ref, store)


def cross_of(kernel, shape, *arrays):
    vmem = pl.BlockSpec(memory_space=pltpu.VMEM)
    return pl.pallas_call(
        kernel,
        in_specs=[vmem] * len(arrays),
        out_specs=vmem,
        out_shape=jax.ShapeDtypeStruct(shape, BF16),
        scratch_shapes=[
            pltpu.VMEM((64 * CH, LANES), F32),
            pltpu.VMEM((BANDS * SEG, LANES), F32),
        ],
        compiler_params=pltpu.CompilerParams(vmem_limit_bytes=32 * 1024 * 1024),
        name=kernel.__name__,
    )(*arrays)


def shifted(value, steps):
    pairs = [(source, (source + steps) % 32) for source in range(32)]
    return lax.ppermute(value, "rgrp", pairs)


def to_chip(value, place):
    pairs = []
    for f in range(BANDS):
        chip = (f // 8 + place // 4) % 2 * 4 + (f // 2 + place) % 4
        pairs.append((f, 2 * chip + f % 2))
    return lax.ppermute(value, "freq", pairs)


def local(table, traces, segment_offsets, channel_order, pilot_channel):
    same, other, guide = spectra_of(segment_offsets, channel_order, pilot_channel, traces, table)
    swapped = lax.ppermute(other, "freq", [(f, f ^ 1) for f in range(BANDS)])
    merged = merged_of(same, swapped)
    parts = [to_chip(value, place + 1) for place, value in enumerate(merged)]
    own = gathered_of(same, swapped, parts)
    near, far = shifted(own, 1), shifted(own, 2)

    guide = guide + lax.ppermute(guide, "rgrp", [(g, g ^ 1) for g in range(32)])
    lines = [[2 * z + side for z in range(16)] for side in range(2)]
    guides = lax.all_to_all(
        jnp.broadcast_to(guide, (16, PAIRS, LANES)),
        "rgrp",
        split_axis=0,
        concat_axis=0,
        tiled=True,
        axis_index_groups=lines,
    )
    notes = notes_of(guides, same, other)
    note = lax.all_to_all(notes, "freq", split_axis=0, concat_axis=0, tiled=True)
    left, power = left_of(own, note)
    first = cross_of(near_kernel, (CH, CH, LANES), left, power, near, shifted(note, 1))
    return cross_of(
        far_kernel, (2, CH, CH, LANES), left, power, far, shifted(note, 2), first
    )


def solution(mesh):
    table = half_table()
    specs = (P(), P("rgrp", "freq"), P("freq"), P("rgrp", None), P())
    inner = jax.shard_map(
        local, mesh=mesh, in_specs=specs, out_specs=P(None, "rgrp", None, "freq"), check_vma=False
    )

    def run(traces, segment_offsets, channel_order, pilot_channel):
        return inner(jnp.asarray(table), traces, segment_offsets, channel_order, pilot_channel)

    return run
```

```python
import functools
import math

import jax
import jax.numpy as jnp
import ml_dtypes
import numpy as np
from jax import lax
from jax.experimental import pallas as pl
from jax.experimental.pallas import tpu as pltpu
from jax.sharding import PartitionSpec as P

L = 2048
HALF = 1024
BANDS = 16
SEG = 4
CH = 32
PAIRS = 32
SPAN = 9216
HALVES = 2
FEW = 16
ROWS = SEG * FEW
LANES = 128
BF16 = jnp.bfloat16
F32 = jnp.float32


def half_table():
    band, parity, pair = np.ogrid[:BANDS, :2, :PAIRS]
    which_bin = 64 * band + 2 * pair + parity + 1
    sample = np.arange(HALF)
    residue = (which_bin[..., None] * sample) % L
    phase_angle = residue.astype(np.float32) * np.float32(2.0 * math.pi / L)
    factor = np.float32(1.0 / math.sqrt(L))
    cosine = np.cos(phase_angle) * factor
    sine = -np.sin(phase_angle) * factor
    return np.concatenate([cosine, sine], axis=2).astype(ml_dtypes.bfloat16)


def lane_index(rows):
    return lax.broadcasted_iota(jnp.int32, (rows, LANES), 1)


def cut_windows(offset_ref, order_ref, traces_ref, wave_ref):
    lane = lane_index(CH)
    row = lax.broadcasted_iota(jnp.int32, (CH, CH), 0)
    picked = jnp.zeros((CH, CH), jnp.int32)
    for channel in range(CH):
        picked = jnp.where(row == channel, order_ref[0, channel], picked)
    chosen = (lax.broadcasted_iota(jnp.int32, (CH, CH), 1) == picked).astype(F32).astype(BF16)
    tiles = L // LANES
    for seg in range(SEG):
        start = seg * L + offset_ref[seg]
        base = jnp.minimum((start // LANES) * LANES, SPAN - (L + LANES))
        base = pl.multiple_of(base, LANES)
        rest = start - base
        turn = lax.rem(LANES - rest, LANES)
        rolled = []
        for tile in range(tiles + 1):
            part = traces_ref[:, pl.ds(pl.multiple_of(base + tile * LANES, LANES), LANES)]
            rolled.append(pltpu.roll(part.astype(F32), turn, 1))
        window = [
            jnp.where(lane < LANES - rest, rolled[tile], rolled[tile + 1]) for tile in range(tiles)
        ]
        rows = pl.ds(seg * CH, CH)
        for parity in range(2):
            sign = -1.0 if parity == 0 else 1.0
            folded = jnp.concatenate(
                [window[t] + sign * window[t + tiles // 2] for t in range(tiles // 2)], axis=1
            ).astype(BF16)
            wave_ref[parity, rows, :] = jnp.dot(
                chosen, folded, preferred_element_type=F32
            ).astype(BF16)


def spectra_kernel(
    offset_hbm, order_hbm, pilot_hbm, traces_hbm, table_hbm, block_ref, guide_ref,
    offset_ref, order_ref, pilot_ref, traces_ref, table_ref, wave_ref, power_ref, sems, table_sems,
):
    small = [
        pltpu.make_async_copy(source, target, sems.at[k])
        for k, (source, target) in enumerate(
            (
                (offset_hbm, offset_ref),
                (order_hbm, order_ref),
                (pilot_hbm, pilot_ref),
                (traces_hbm, traces_ref),
            )
        )
    ]
    for copy in small:
        copy.start()
    for part in range(4):
        pltpu.make_async_copy(
            table_hbm.at[pl.ds(4 * part, 4)], table_ref.at[pl.ds(4 * part, 4)], table_sems.at[part]
        ).start()
    power_ref[...] = jnp.zeros_like(power_ref)
    for copy in small:
        copy.wait()
    cut_windows(offset_ref, order_ref, traces_ref, wave_ref)

    lane = lane_index(PAIRS)
    channel = lax.rem(pilot_ref[0], CH)
    for quarter in range(4):
        pltpu.make_async_copy(
            table_hbm.at[pl.ds(4 * quarter, 4)],
            table_ref.at[pl.ds(4 * quarter, 4)],
            table_sems.at[quarter],
        ).wait()
        for local_band in range(4):
            band = quarter * 4 + local_band
            parts = {}
            for parity in range(2):
                product = lax.dot_general(
                    table_ref[band, parity],
                    wave_ref[parity],
                    (((1,), (1,)), ((), ())),
                    preferred_element_type=F32,
                )
                for side in range(2):
                    parts[side, parity] = product[side * PAIRS : (side + 1) * PAIRS]
                real = parts[0, parity].astype(BF16).astype(F32)
                imag = parts[1, parity].astype(BF16).astype(F32)
                place = 2 * band + parity
                power = pltpu.roll(
                    real * real + imag * imag, lax.rem(place - channel + LANES, LANES), 1
                )
                power_ref[...] = jnp.where(lane % 32 == place, power, power_ref[...])
            for seg in range(SEG):
                line = None
                for side in range(2):
                    for parity in range(2):
                        group = side * 2 + parity
                        part = parts[side, parity]
                        if group != seg:
                            part = pltpu.roll(part, (group - seg) * 32 % LANES, 1)
                        line = part if line is None else jnp.where(lane // 32 == group, part, line)
                line = line.astype(BF16)
                for half in range(HALVES):
                    block_ref[band, half, seg * FEW : (seg + 1) * FEW, :] = line[
                        half * FEW : (half + 1) * FEW
                    ]
    mine = pilot_ref[0] // CH == lax.axis_index("rgrp")
    guide_ref[...] = jnp.where(mine, jnp.sqrt(power_ref[...]), 0.0).astype(BF16)


def spectra_of(offsets, order, pilot, traces, table):
    vmem = pl.BlockSpec(memory_space=pltpu.VMEM)
    offsets, order, traces, table = (
        pltpu.with_memory_space_constraint(value, pltpu.HBM)
        for value in (offsets, order, traces, table)
    )
    return pl.pallas_call(
        spectra_kernel,
        in_specs=[pl.BlockSpec(memory_space=pl.ANY)] * 5,
        out_specs=[vmem, vmem],
        out_shape=[
            jax.ShapeDtypeStruct((BANDS, HALVES, SEG * FEW, LANES), BF16),
            jax.ShapeDtypeStruct((PAIRS, LANES), BF16),
        ],
        scratch_shapes=[
            pltpu.SMEM((SEG,), jnp.int32),
            pltpu.SMEM((1, CH), jnp.int32),
            pltpu.SMEM((1,), jnp.int32),
            pltpu.VMEM((CH, SPAN), BF16),
            pltpu.VMEM((BANDS, 2, 2 * PAIRS, HALF), BF16),
            pltpu.VMEM((2, SEG * CH, HALF), BF16),
            pltpu.VMEM((PAIRS, LANES), F32),
            pltpu.SemaphoreType.DMA((4,)),
            pltpu.SemaphoreType.DMA((4,)),
        ],
        compiler_params=pltpu.CompilerParams(vmem_limit_bytes=16 * 1024 * 1024),
        name="spectra",
    )(offsets, order, pilot, traces, table)


def whiten_kernel(guides_ref, own_ref, far_ref, white_ref, value_ref, guide_ref):
    guide = guides_ref[0].astype(F32)
    for line in range(1, 16):
        guide = guide + guides_ref[line].astype(F32)
    guide_ref[...] = guide
    even = (lane_index(PAIRS) // 32) % 2 == 0
    blocks = (own_ref, far_ref)
    totals = [[jnp.zeros((FEW, LANES), F32) for _ in range(SEG)] for _ in blocks]
    for band in range(BANDS):
        for seg in range(SEG):
            first = 32 * seg + 2 * band
            rows = slice(seg * FEW, (seg + 1) * FEW)
            weight = jnp.where(
                even, guide_ref[:, first : first + 1], guide_ref[:, first + 1 : first + 2]
            )
            for half in range(HALVES):
                part = weight[half * FEW : (half + 1) * FEW]
                for k, block_ref in enumerate(blocks):
                    value = block_ref[band, half, rows, :].astype(F32) * part
                    value_ref[band * HALVES + half, k, rows, :] = value
                    totals[k][seg] = totals[k][seg] + value * value
    for k in range(len(blocks)):
        for seg in range(SEG):
            total = jnp.sum(totals[k][seg], axis=0, keepdims=True)
            total = jnp.broadcast_to(total, (8, LANES))
            total = total + pltpu.roll(total, 64, 1)
            total = total + pltpu.roll(total, 32, 1)
            level = (total * (0.1 / (64.0 * BANDS)) + 1e-06)[:1]
            rows = slice(seg * FEW, (seg + 1) * FEW)
            for place in range(BANDS * HALVES):
                value = value_ref[place, k, rows, :]
                energy = value * value
                energy = energy + pltpu.roll(energy, 64, 1)
                white_ref[place, k, rows, :] = (value * lax.rsqrt(energy + level)).astype(BF16)


def whitened_of(guides, own, far):
    vmem = pl.BlockSpec(memory_space=pltpu.VMEM)
    shape = (BANDS * HALVES, 2, ROWS, LANES)
    return pl.pallas_call(
        whiten_kernel,
        in_specs=[vmem] * 3,
        out_specs=vmem,
        out_shape=jax.ShapeDtypeStruct(shape, BF16),
        scratch_shapes=[pltpu.VMEM(shape, F32), pltpu.VMEM((PAIRS, LANES), F32)],
        compiler_params=pltpu.CompilerParams(vmem_limit_bytes=32 * 1024 * 1024),
        name="whiten",
    )(guides, own, far)


def gather_kernel(parts_ref, block_ref, wide_ref):
    for place in range(BANDS * HALVES):
        for k in range(2):
            at = (place * 2 + k) * ROWS
            wide_ref[at : at + ROWS, :] = parts_ref[place, k].astype(F32)

    def bin_pair(pair, carry):
        for which in range(4):
            rows = [
                wide_ref[pl.ds(which * ROWS + seg * FEW + pair, BANDS, stride=4 * ROWS), :]
                for seg in range(SEG)
            ]
            block_ref[pair, which] = jnp.concatenate(rows, axis=0).astype(BF16)
        return carry

    lax.fori_loop(0, FEW, bin_pair, 0, unroll=2)


def gathered_of(parts):
    vmem = pl.BlockSpec(memory_space=pltpu.VMEM)
    return pl.pallas_call(
        gather_kernel,
        in_specs=[vmem],
        out_specs=vmem,
        out_shape=jax.ShapeDtypeStruct((FEW, 4, BANDS * SEG, LANES), BF16),
        scratch_shapes=[pltpu.VMEM((BANDS * HALVES * 2 * ROWS, LANES), F32)],
        compiler_params=pltpu.CompilerParams(vmem_limit_bytes=32 * 1024 * 1024),
        name="gather",
    )(parts)


def cross_kernel(mine, block_ref, out_ref, near_ref, far_ref):
    side = lax.axis_index("rgrp") % 2
    left_side = side if mine else 1 - side
    sign = jnp.where(lane_index(BANDS * SEG) < 64, 1.0, -1.0)

    def bin_pair(pair, carry):
        turned = jnp.transpose(block_ref[pair, 2 * left_side].astype(F32))
        left = jnp.concatenate([turned[:64], turned[64:]], axis=1).astype(BF16)
        for which, stack_ref in ((3 * (1 - left_side), near_ref), (2 * left_side + 1, far_ref)):
            right = block_ref[pair, which].astype(F32)
            mix = jnp.concatenate([right * sign, pltpu.roll(right, 64, 1)], axis=0).astype(BF16)
            product = jnp.dot(left, mix, preferred_element_type=F32)
            stack_ref[pl.ds(pl.multiple_of(pair * 2 * CH, 2 * CH), 2 * CH), :] = product
        return carry

    lax.fori_loop(0, FEW, bin_pair, 0, unroll=4)

    lane = lane_index(CH)
    even = lane % 2 == 0
    for first in range(0, CH, 4):
        pieces = {}
        for back, stack_ref in enumerate((near_ref, far_ref)):
            rows = [stack_ref[pl.ds(first + k, 2 * FEW, stride=CH), :] for k in range(4)]
            turned = jnp.transpose(jnp.concatenate(rows, axis=0)) * 0.125
            pieces[back] = jnp.where(even, turned[:32], turned[32:64])
            pieces[2 + back] = jnp.where(even, turned[64:96], turned[96:])
        for k in range(4):
            line = None
            for group in range(4):
                part = pieces[group]
                if group != k:
                    part = pltpu.roll(part, (group - k) * 32 % LANES, 1)
                line = part if line is None else jnp.where(lane // 32 == group, part, line)
            out_ref[first + k] = line.astype(BF16)


def cross_of(mine, blocks):
    vmem = pl.BlockSpec(memory_space=pltpu.VMEM)
    stack = pltpu.VMEM((2 * FEW * CH, LANES), F32)
    return pl.pallas_call(
        functools.partial(cross_kernel, mine),
        in_specs=[vmem],
        out_specs=vmem,
        out_shape=jax.ShapeDtypeStruct((CH, CH, LANES), BF16),
        scratch_shapes=[stack, stack],
        compiler_params=pltpu.CompilerParams(vmem_limit_bytes=32 * 1024 * 1024),
        cost_estimate=pl.CostEstimate(flops=2**28, bytes_accessed=2**23, transcendentals=0),
        name="cross_mine" if mine else "cross_other",
    )(blocks)


def merge_kernel(own_ref, other_ref, out_ref):
    first = lax.axis_index("rgrp") % 2 == 0
    even = (lane_index(CH) // 32) % 2 == 0

    def channel(i, carry):
        own = own_ref[i].astype(F32)
        other = other_ref[i].astype(F32)
        low = jnp.where(first, own, other)
        high = jnp.where(first, other, own)
        out_ref[0, i] = jnp.where(even, low, pltpu.roll(high, 32, 1)).astype(BF16)
        out_ref[1, i] = jnp.where(even, pltpu.roll(low, 96, 1), high).astype(BF16)
        return carry

    lax.fori_loop(0, CH, channel, 0, unroll=4)


def merged_of(own, other):
    vmem = pl.BlockSpec(memory_space=pltpu.VMEM)
    return pl.pallas_call(
        merge_kernel,
        in_specs=[vmem] * 2,
        out_specs=vmem,
        out_shape=jax.ShapeDtypeStruct((2, CH, CH, LANES), BF16),
        compiler_params=pltpu.CompilerParams(vmem_limit_bytes=32 * 1024 * 1024),
        name="merge",
    )(own, other)


def beside(value):
    return lax.ppermute(value, "rgrp", [(g, g ^ 1) for g in range(32)])


def local(table, traces, segment_offsets, channel_order, pilot_channel):
    own, guide = spectra_of(segment_offsets, channel_order, pilot_channel, traces, table)
    far = lax.ppermute(own, "rgrp", [(g, (g + 2) % 32) for g in range(32)])
    guide = guide + beside(guide)
    lines = [[2 * z + side for z in range(16)] for side in range(2)]
    guides = lax.all_to_all(
        jnp.broadcast_to(guide, (16, PAIRS, LANES)),
        "rgrp",
        split_axis=0,
        concat_axis=0,
        tiled=True,
        axis_index_groups=lines,
    )
    white = whitened_of(guides, own, far)
    planes = [[32 * f + 2 * z + side for f in range(BANDS) for side in range(2)] for z in range(16)]
    parts = lax.all_to_all(
        white, ("freq", "rgrp"), split_axis=0, concat_axis=0, tiled=True, axis_index_groups=planes
    )
    blocks = gathered_of(parts)
    other = beside(cross_of(False, blocks))
    return merged_of(cross_of(True, blocks), other)


def solution(mesh):
    table = half_table()
    specs = (P(), P("rgrp", "freq"), P("freq"), P("rgrp", None), P())
    inner = jax.shard_map(
        local, mesh=mesh, in_specs=specs, out_specs=P(None, "rgrp", None, "freq"), check_vma=False
    )

    def run(traces, segment_offsets, channel_order, pilot_channel):
        return inner(jnp.asarray(table), traces, segment_offsets, channel_order, pilot_channel)

    return run
```

```python
import functools
import math

import jax
import jax.numpy as jnp
import ml_dtypes
import numpy as np
from jax import lax
from jax.experimental import pallas as pl
from jax.experimental.pallas import tpu as pltpu
from jax.sharding import PartitionSpec as P

L = 2048
QUARTER = 512
PARTS = 1
BANDS = 16
SEG = 4
CH = 32
PAIRS = 32
SPAN = 9216
HALVES = 2
FEW = 16
ROWS = SEG * FEW
PITCH = 4 * ROWS + 8
LANES = 128
BF16 = jnp.bfloat16
F32 = jnp.float32


def quarter_table():
    part, parity, band, pair = np.ogrid[:PARTS, :2, : BANDS // PARTS, :PAIRS]
    which_bin = 64 * (part * (BANDS // PARTS) + band) + 2 * pair + parity + 1
    sample = np.arange(QUARTER)
    residue = (which_bin[..., None] * sample) % L
    phase_angle = residue.astype(np.float32) * np.float32(2.0 * math.pi / L)
    factor = np.float32(1.0 / math.sqrt(L))
    both = np.stack([np.cos(phase_angle) * factor, np.sin(phase_angle) * factor], axis=3)
    return both.reshape(PARTS, 2, -1, QUARTER).astype(ml_dtypes.bfloat16)


def lane_index(rows):
    return lax.broadcasted_iota(jnp.int32, (rows, LANES), 1)


def cut_windows(offset_ref, order_ref, traces_ref, wide_ref, wave_ref):
    lane = lane_index(CH)
    row = lax.broadcasted_iota(jnp.int32, (CH, CH), 0)
    picked = jnp.zeros((CH, CH), jnp.int32)
    for channel in range(CH):
        picked = jnp.where(row == channel, order_ref[0, channel], picked)
    chosen = (lax.broadcasted_iota(jnp.int32, (CH, CH), 1) == picked).astype(F32).astype(BF16)
    tiles = L // LANES
    for seg in range(SEG):
        start = seg * L + offset_ref[seg]
        base = jnp.minimum((start // LANES) * LANES, SPAN - (L + LANES))
        base = pl.multiple_of(base, LANES)
        rest = start - base
        turn = lax.rem(LANES - rest, LANES)
        rolled = []
        for tile in range(tiles + 1):
            part = traces_ref[:, pl.ds(pl.multiple_of(base + tile * LANES, LANES), LANES)]
            rolled.append(pltpu.roll(part.astype(F32), turn, 1))
        window = [
            jnp.where(lane < LANES - rest, rolled[tile], rolled[tile + 1]) for tile in range(tiles)
        ]
        quarter = tiles // 4
        first, second, third, fourth = (
            jnp.concatenate(window[k * quarter : (k + 1) * quarter], axis=1) for k in range(4)
        )
        even, odd = first + third, second + fourth
        mixes = (first - third, second - fourth, even - odd, even + odd)
        for k, mix in enumerate(mixes):
            mix = jnp.dot(chosen, mix.astype(BF16), preferred_element_type=F32)
            at = (k % 2) * LANES + seg * CH
            wide_ref[k // 2, at : at + CH, :] = mix
    for parity in range(2):
        wave_ref[parity] = jnp.transpose(wide_ref[parity]).astype(BF16)


def spectra_kernel(
    offset_hbm, order_hbm, pilot_hbm, traces_hbm, table_hbm, block_ref, guide_ref,
    offset_ref, order_ref, pilot_ref, traces_ref, table_ref, wide_ref, wave_ref,
    power_ref, sems, table_sems,
):
    small = [
        pltpu.make_async_copy(source, target, sems.at[k])
        for k, (source, target) in enumerate(
            (
                (traces_hbm, traces_ref),
                (offset_hbm, offset_ref),
                (order_hbm, order_ref),
                (pilot_hbm, pilot_ref),
            )
        )
    ]
    for copy in small:
        copy.start()
    table = [
        pltpu.make_async_copy(table_hbm.at[part], table_ref.at[part], table_sems.at[part])
        for part in range(PARTS)
    ]
    for copy in table:
        copy.start()
    power_ref[...] = jnp.zeros_like(power_ref)
    for copy in small:
        copy.wait()
    cut_windows(offset_ref, order_ref, traces_ref, wide_ref, wave_ref)

    lane = lane_index(PAIRS)
    channel = lax.rem(pilot_ref[0], CH)
    odd_pair = lax.broadcasted_iota(jnp.int32, (PAIRS, LANES), 0) % 2 == 1
    flip = jnp.where(odd_pair, -1.0, 1.0)
    for slab in range(PARTS):
        table[slab].wait()
        products = [
            jnp.dot(table_ref[slab, parity], wave_ref[parity], preferred_element_type=F32)
            for parity in range(2)
        ]
        for local_band in range(BANDS // PARTS):
            band = slab * (BANDS // PARTS) + local_band
            at = 2 * PAIRS * local_band
            parts = {}
            cosine = products[0][at : at + PAIRS]
            sine = products[0][at + PAIRS : at + 2 * PAIRS]
            parts[0, 0] = cosine[:, :LANES] - flip * sine[:, LANES:]
            parts[1, 0] = -sine[:, :LANES] - flip * cosine[:, LANES:]
            cosine = products[1][at : at + PAIRS]
            sine = products[1][at + PAIRS : at + 2 * PAIRS]
            parts[0, 1] = jnp.where(odd_pair, cosine[:, LANES:], cosine[:, :LANES])
            parts[1, 1] = -jnp.where(odd_pair, sine[:, LANES:], sine[:, :LANES])
            for parity in range(2):
                real = parts[0, parity].astype(BF16).astype(F32)
                imag = parts[1, parity].astype(BF16).astype(F32)
                place = 2 * band + parity
                power = pltpu.roll(
                    real * real + imag * imag, lax.rem(place - channel + LANES, LANES), 1
                )
                power_ref[...] = jnp.where(lane % 32 == place, power, power_ref[...])
            for seg in range(SEG):
                line = None
                for side in range(2):
                    for parity in range(2):
                        group = side * 2 + parity
                        part = parts[side, parity]
                        if group != seg:
                            part = pltpu.roll(part, (group - seg) * 32 % LANES, 1)
                        line = part if line is None else jnp.where(lane // 32 == group, part, line)
                line = line.astype(BF16)
                for half in range(HALVES):
                    block_ref[band, half, seg * FEW : (seg + 1) * FEW, :] = line[
                        half * FEW : (half + 1) * FEW
                    ]
    mine = pilot_ref[0] // CH == lax.axis_index("rgrp")
    guide_ref[...] = jnp.where(mine, jnp.sqrt(power_ref[...]), 0.0).astype(BF16)


def spectra_of(offsets, order, pilot, traces, table):
    vmem = pl.BlockSpec(memory_space=pltpu.VMEM)
    offsets, order, traces, table = (
        pltpu.with_memory_space_constraint(value, pltpu.HBM)
        for value in (offsets, order, traces, table)
    )
    return pl.pallas_call(
        spectra_kernel,
        in_specs=[pl.BlockSpec(memory_space=pl.ANY)] * 5,
        out_specs=[vmem, vmem],
        out_shape=[
            jax.ShapeDtypeStruct((BANDS, HALVES, SEG * FEW, LANES), BF16),
            jax.ShapeDtypeStruct((PAIRS, LANES), BF16),
        ],
        scratch_shapes=[
            pltpu.SMEM((SEG,), jnp.int32),
            pltpu.SMEM((1, CH), jnp.int32),
            pltpu.SMEM((1,), jnp.int32),
            pltpu.VMEM((CH, SPAN), BF16),
            pltpu.VMEM((PARTS, 2, 2 * PAIRS * BANDS // PARTS, QUARTER), BF16),
            pltpu.VMEM((2, 2 * LANES, QUARTER), F32),
            pltpu.VMEM((2, QUARTER, 2 * LANES), BF16),
            pltpu.VMEM((PAIRS, LANES), F32),
            pltpu.SemaphoreType.DMA((4,)),
            pltpu.SemaphoreType.DMA((PARTS,)),
        ],
        compiler_params=pltpu.CompilerParams(vmem_limit_bytes=16 * 1024 * 1024),
        name="spectra",
    )(offsets, order, pilot, traces, table)


def whiten_kernel(guides_ref, own_ref, far_ref, white_ref, value_ref, guide_ref):
    guide = guides_ref[0].astype(F32)
    for line in range(1, 16):
        guide = guide + guides_ref[line].astype(F32)
    guide_ref[...] = guide
    even = (lane_index(PAIRS) // 32) % 2 == 0
    blocks = (own_ref, far_ref)
    totals = [[jnp.zeros((FEW, LANES), F32) for _ in range(SEG)] for _ in blocks]
    for band in range(BANDS):
        for seg in range(SEG):
            first = 32 * seg + 2 * band
            rows = slice(seg * FEW, (seg + 1) * FEW)
            weight = jnp.where(
                even, guide_ref[:, first : first + 1], guide_ref[:, first + 1 : first + 2]
            )
            for half in range(HALVES):
                part = weight[half * FEW : (half + 1) * FEW]
                for k, block_ref in enumerate(blocks):
                    value = block_ref[band, half, rows, :].astype(F32) * part
                    value_ref[band * HALVES + half, k, rows, :] = value
                    totals[k][seg] = totals[k][seg] + value * value
    for k in range(len(blocks)):
        for seg in range(SEG):
            total = jnp.sum(totals[k][seg], axis=0, keepdims=True)
            total = jnp.broadcast_to(total, (8, LANES))
            total = total + pltpu.roll(total, 64, 1)
            total = total + pltpu.roll(total, 32, 1)
            level = (total * (0.1 / (64.0 * BANDS)) + 1e-06)[:1]
            rows = slice(seg * FEW, (seg + 1) * FEW)
            for place in range(BANDS * HALVES):
                value = value_ref[place, k, rows, :]
                energy = value * value
                energy = energy + pltpu.roll(energy, 64, 1)
                white_ref[place, k, rows, :] = (value * lax.rsqrt(energy + level)).astype(BF16)


def whitened_of(guides, own, far):
    vmem = pl.BlockSpec(memory_space=pltpu.VMEM)
    shape = (BANDS * HALVES, 2, ROWS, LANES)
    return pl.pallas_call(
        whiten_kernel,
        in_specs=[vmem] * 3,
        out_specs=vmem,
        out_shape=jax.ShapeDtypeStruct(shape, BF16),
        scratch_shapes=[pltpu.VMEM(shape, F32), pltpu.VMEM((PAIRS, LANES), F32)],
        compiler_params=pltpu.CompilerParams(vmem_limit_bytes=32 * 1024 * 1024),
        name="whiten",
    )(guides, own, far)


def gather_rows(parts_ref, block_ref, wide_ref):
    for window in range(BANDS):
        for which in range(4):
            at = window * PITCH + which * ROWS
            part = parts_ref[window * HALVES + which // 2, which % 2]
            wide_ref[at : at + ROWS, :] = part.astype(F32)
    for pair in range(FEW):
        for which in range(4):
            rows = [
                wide_ref[pl.ds(which * ROWS + seg * FEW + pair, BANDS, stride=PITCH), :]
                for seg in range(SEG)
            ]
            block_ref[pair, which] = jnp.concatenate(rows, axis=0).astype(BF16)


def cross_rows(left_side, block_ref, out_ref, near_ref, far_ref):
    sign = jnp.where(lane_index(BANDS * SEG) < 64, 1.0, -1.0)
    for pair in range(FEW):
        turned = jnp.transpose(block_ref[pair, 2 * left_side].astype(F32))
        left = jnp.concatenate([turned[:64], turned[64:]], axis=1).astype(BF16)
        for which, stack_ref in ((3 * (1 - left_side), near_ref), (2 * left_side + 1, far_ref)):
            right = block_ref[pair, which].astype(F32)
            mix = jnp.concatenate([right * sign, pltpu.roll(right, 64, 1)], axis=0).astype(BF16)
            product = jnp.dot(left, mix, preferred_element_type=F32)
            stack_ref[pair * 2 * CH : (pair + 1) * 2 * CH, :] = product

    lane = lane_index(CH)
    even = lane % 2 == 0
    for first in range(0, CH, 4):
        pieces = {}
        for back, stack_ref in enumerate((near_ref, far_ref)):
            rows = [stack_ref[pl.ds(first + k, 2 * FEW, stride=CH), :] for k in range(4)]
            turned = jnp.transpose(jnp.concatenate(rows, axis=0)) * 0.125
            pieces[back] = jnp.where(even, turned[:32], turned[32:64])
            pieces[2 + back] = jnp.where(even, turned[64:96], turned[96:])
        for k in range(4):
            line = None
            for group in range(4):
                part = pieces[group]
                if group != k:
                    part = pltpu.roll(part, (group - k) * 32 % LANES, 1)
                line = part if line is None else jnp.where(lane // 32 == group, part, line)
            out_ref[first + k] = line.astype(BF16)


def other_kernel(parts_ref, out_ref, block_ref, wide_ref, near_ref, far_ref):
    gather_rows(parts_ref, block_ref, wide_ref)
    cross_rows(1 - lax.axis_index("rgrp") % 2, block_ref, out_ref, near_ref, far_ref)


def mine_kernel(block_ref, out_ref, near_ref, far_ref):
    cross_rows(lax.axis_index("rgrp") % 2, block_ref, out_ref, near_ref, far_ref)


STACK = pltpu.VMEM((2 * FEW * CH, LANES), F32)
CROSS = jax.ShapeDtypeStruct((CH, CH, LANES), BF16)


def other_of(parts):
    vmem = pl.BlockSpec(memory_space=pltpu.VMEM)
    return pl.pallas_call(
        other_kernel,
        in_specs=[vmem],
        out_specs=[vmem, vmem],
        out_shape=[CROSS, jax.ShapeDtypeStruct((FEW, 4, BANDS * SEG, LANES), BF16)],
        scratch_shapes=[pltpu.VMEM((BANDS * PITCH, LANES), F32), STACK, STACK],
        compiler_params=pltpu.CompilerParams(vmem_limit_bytes=32 * 1024 * 1024),
        name="cross_other",
    )(parts)


def mine_of(blocks):
    vmem = pl.BlockSpec(memory_space=pltpu.VMEM)
    return pl.pallas_call(
        mine_kernel,
        in_specs=[vmem],
        out_specs=vmem,
        out_shape=CROSS,
        scratch_shapes=[STACK, STACK],
        compiler_params=pltpu.CompilerParams(vmem_limit_bytes=32 * 1024 * 1024),
        cost_estimate=pl.CostEstimate(flops=2**28, bytes_accessed=2**23, transcendentals=0),
        name="cross_mine",
    )(blocks)


def merge_kernel(own_ref, other_ref, out_ref):
    first = lax.axis_index("rgrp") % 2 == 0
    even = (lane_index(CH) // 32) % 2 == 0

    def channel(i, carry):
        own = own_ref[i].astype(F32)
        other = other_ref[i].astype(F32)
        low = jnp.where(first, own, other)
        high = jnp.where(first, other, own)
        out_ref[0, i] = jnp.where(even, low, pltpu.roll(high, 32, 1)).astype(BF16)
        out_ref[1, i] = jnp.where(even, pltpu.roll(low, 96, 1), high).astype(BF16)
        return carry

    lax.fori_loop(0, CH, channel, 0, unroll=CH)


def merged_of(own, other):
    vmem = pl.BlockSpec(memory_space=pltpu.VMEM)
    return pl.pallas_call(
        merge_kernel,
        in_specs=[vmem] * 2,
        out_specs=vmem,
        out_shape=jax.ShapeDtypeStruct((2, CH, CH, LANES), BF16),
        compiler_params=pltpu.CompilerParams(vmem_limit_bytes=32 * 1024 * 1024),
        name="merge",
    )(own, other)


def beside(value):
    return lax.ppermute(value, "rgrp", [(g, g ^ 1) for g in range(32)])


def local(table, traces, segment_offsets, channel_order, pilot_channel):
    own, guide = spectra_of(segment_offsets, channel_order, pilot_channel, traces, table)
    far = lax.ppermute(own, "rgrp", [(g, (g + 2) % 32) for g in range(32)])
    guide = guide + beside(guide)
    lines = [[2 * z + side for z in range(16)] for side in range(2)]
    guides = lax.all_to_all(
        jnp.broadcast_to(guide, (16, PAIRS, LANES)),
        "rgrp",
        split_axis=0,
        concat_axis=0,
        tiled=True,
        axis_index_groups=lines,
    )
    white = whitened_of(guides, own, far)
    planes = [[32 * f + 2 * z + side for f in range(BANDS) for side in range(2)] for z in range(16)]
    parts = lax.all_to_all(
        white, ("freq", "rgrp"), split_axis=0, concat_axis=0, tiled=True, axis_index_groups=planes
    )
    other, blocks = other_of(parts)
    other = beside(other)
    return merged_of(mine_of(blocks), other)


def solution(mesh):
    table = quarter_table()
    specs = (P(), P("rgrp", "freq"), P("freq"), P("rgrp", None), P())
    inner = jax.shard_map(
        local, mesh=mesh, in_specs=specs, out_specs=P(None, "rgrp", None, "freq"), check_vma=False
    )

    def run(traces, segment_offsets, channel_order, pilot_channel):
        return inner(jnp.asarray(table), traces, segment_offsets, channel_order, pilot_channel)

    return run
```

```python
import functools
import math

import jax
import jax.numpy as jnp
import ml_dtypes
import numpy as np
from jax import lax
from jax.experimental import pallas as pl
from jax.experimental.pallas import tpu as pltpu
from jax.sharding import PartitionSpec as P

L = 2048
QUARTER = 512
PARTS = 1
BANDS = 16
SEG = 4
CH = 32
PAIRS = 32
SPAN = 9216
HALVES = 2
FEW = 16
ROWS = SEG * FEW
PITCH = 4 * ROWS + 8
LANES = 128
BF16 = jnp.bfloat16
F32 = jnp.float32


def quarter_table():
    part, parity, band, pair = np.ogrid[:PARTS, :2, : BANDS // PARTS, :PAIRS]
    which_bin = 64 * (part * (BANDS // PARTS) + band) + 2 * pair + parity + 1
    sample = np.arange(QUARTER)
    residue = (which_bin[..., None] * sample) % L
    phase_angle = residue.astype(np.float32) * np.float32(2.0 * math.pi / L)
    factor = np.float32(1.0 / math.sqrt(L))
    both = np.stack([np.cos(phase_angle) * factor, np.sin(phase_angle) * factor], axis=3)
    return both.reshape(PARTS, 2, -1, QUARTER).astype(ml_dtypes.bfloat16)


def lane_index(rows):
    return lax.broadcasted_iota(jnp.int32, (rows, LANES), 1)


def cut_windows(offset_ref, order_ref, traces_ref, wide_ref, wave_ref):
    lane = lane_index(CH)
    row = lax.broadcasted_iota(jnp.int32, (CH, CH), 0)
    picked = jnp.zeros((CH, CH), jnp.int32)
    for channel in range(CH):
        picked = jnp.where(row == channel, order_ref[0, channel], picked)
    chosen = (lax.broadcasted_iota(jnp.int32, (CH, CH), 1) == picked).astype(F32).astype(BF16)
    tiles = L // LANES
    for seg in range(SEG):
        start = seg * L + offset_ref[seg]
        base = jnp.minimum((start // LANES) * LANES, SPAN - (L + LANES))
        base = pl.multiple_of(base, LANES)
        rest = start - base
        turn = lax.rem(LANES - rest, LANES)
        rolled = []
        for tile in range(tiles + 1):
            part = traces_ref[:, pl.ds(pl.multiple_of(base + tile * LANES, LANES), LANES)]
            rolled.append(pltpu.roll(part.astype(F32), turn, 1))
        window = [
            jnp.where(lane < LANES - rest, rolled[tile], rolled[tile + 1]) for tile in range(tiles)
        ]
        quarter = tiles // 4
        first, second, third, fourth = (
            jnp.concatenate(window[k * quarter : (k + 1) * quarter], axis=1) for k in range(4)
        )
        even, odd = first + third, second + fourth
        mixes = (first - third, second - fourth, even - odd, even + odd)
        for k, mix in enumerate(mixes):
            mix = jnp.dot(chosen, mix.astype(BF16), preferred_element_type=F32)
            at = (k % 2) * LANES + seg * CH
            wide_ref[k // 2, at : at + CH, :] = mix
    for parity in range(2):
        wave_ref[parity] = jnp.transpose(wide_ref[parity]).astype(BF16)


def spectra_kernel(
    offset_hbm, order_hbm, pilot_hbm, traces_hbm, table_hbm, block_ref, guide_ref,
    offset_ref, order_ref, pilot_ref, traces_ref, table_ref, wide_ref, wave_ref,
    power_ref, sems, table_sems,
):
    small = [
        pltpu.make_async_copy(source, target, sems.at[k])
        for k, (source, target) in enumerate(
            (
                (traces_hbm, traces_ref),
                (offset_hbm, offset_ref),
                (order_hbm, order_ref),
                (pilot_hbm, pilot_ref),
            )
        )
    ]
    for copy in small:
        copy.start()
    table = [
        pltpu.make_async_copy(table_hbm.at[part], table_ref.at[part], table_sems.at[part])
        for part in range(PARTS)
    ]
    for copy in table:
        copy.start()
    power_ref[...] = jnp.zeros_like(power_ref)
    for copy in small:
        copy.wait()
    cut_windows(offset_ref, order_ref, traces_ref, wide_ref, wave_ref)

    lane = lane_index(PAIRS)
    channel = lax.rem(pilot_ref[0], CH)
    odd_pair = lax.broadcasted_iota(jnp.int32, (PAIRS, LANES), 0) % 2 == 1
    flip = jnp.where(odd_pair, -1.0, 1.0)
    for slab in range(PARTS):
        table[slab].wait()
        products = [
            jnp.dot(table_ref[slab, parity], wave_ref[parity], preferred_element_type=F32)
            for parity in range(2)
        ]
        for local_band in range(BANDS // PARTS):
            band = slab * (BANDS // PARTS) + local_band
            at = 2 * PAIRS * local_band
            parts = {}
            cosine = products[0][at : at + PAIRS]
            sine = products[0][at + PAIRS : at + 2 * PAIRS]
            parts[0, 0] = cosine[:, :LANES] - flip * sine[:, LANES:]
            parts[1, 0] = -sine[:, :LANES] - flip * cosine[:, LANES:]
            cosine = products[1][at : at + PAIRS]
            sine = products[1][at + PAIRS : at + 2 * PAIRS]
            parts[0, 1] = jnp.where(odd_pair, cosine[:, LANES:], cosine[:, :LANES])
            parts[1, 1] = -jnp.where(odd_pair, sine[:, LANES:], sine[:, :LANES])
            for parity in range(2):
                real = parts[0, parity].astype(BF16).astype(F32)
                imag = parts[1, parity].astype(BF16).astype(F32)
                place = 2 * band + parity
                power = pltpu.roll(
                    real * real + imag * imag, lax.rem(place - channel + LANES, LANES), 1
                )
                power_ref[...] = jnp.where(lane % 32 == place, power, power_ref[...])
            for seg in range(SEG):
                line = None
                for side in range(2):
                    for parity in range(2):
                        group = side * 2 + parity
                        part = parts[side, parity]
                        if group != seg:
                            part = pltpu.roll(part, (group - seg) * 32 % LANES, 1)
                        line = part if line is None else jnp.where(lane // 32 == group, part, line)
                line = line.astype(BF16)
                for half in range(HALVES):
                    block_ref[band, half, seg * FEW : (seg + 1) * FEW, :] = line[
                        half * FEW : (half + 1) * FEW
                    ]
    mine = pilot_ref[0] // CH == lax.axis_index("rgrp")
    guide_ref[...] = jnp.where(mine, jnp.sqrt(power_ref[...]), 0.0).astype(BF16)


def spectra_of(offsets, order, pilot, traces, table):
    vmem = pl.BlockSpec(memory_space=pltpu.VMEM)
    offsets, order, traces, table = (
        pltpu.with_memory_space_constraint(value, pltpu.HBM)
        for value in (offsets, order, traces, table)
    )
    return pl.pallas_call(
        spectra_kernel,
        in_specs=[pl.BlockSpec(memory_space=pl.ANY)] * 5,
        out_specs=[vmem, vmem],
        out_shape=[
            jax.ShapeDtypeStruct((BANDS, HALVES, SEG * FEW, LANES), BF16),
            jax.ShapeDtypeStruct((PAIRS, LANES), BF16),
        ],
        scratch_shapes=[
            pltpu.SMEM((SEG,), jnp.int32),
            pltpu.SMEM((1, CH), jnp.int32),
            pltpu.SMEM((1,), jnp.int32),
            pltpu.VMEM((CH, SPAN), BF16),
            pltpu.VMEM((PARTS, 2, 2 * PAIRS * BANDS // PARTS, QUARTER), BF16),
            pltpu.VMEM((2, 2 * LANES, QUARTER), F32),
            pltpu.VMEM((2, QUARTER, 2 * LANES), BF16),
            pltpu.VMEM((PAIRS, LANES), F32),
            pltpu.SemaphoreType.DMA((4,)),
            pltpu.SemaphoreType.DMA((PARTS,)),
        ],
        compiler_params=pltpu.CompilerParams(vmem_limit_bytes=16 * 1024 * 1024),
        name="spectra",
    )(offsets, order, pilot, traces, table)


def total_kernel(guides_ref, guide_ref):
    guide = guides_ref[0].astype(F32)
    for line in range(1, 16):
        guide = guide + guides_ref[line].astype(F32)
    guide_ref[...] = guide


def total_of(guides):
    vmem = pl.BlockSpec(memory_space=pltpu.VMEM)
    return pl.pallas_call(
        total_kernel,
        in_specs=[vmem],
        out_specs=vmem,
        out_shape=jax.ShapeDtypeStruct((PAIRS, LANES), F32),
        cost_estimate=pl.CostEstimate(flops=2**28, bytes_accessed=2**17, transcendentals=0),
        name="total",
    )(guides)


def whiten_kernel(guide_ref, own_ref, far_ref, white_ref, value_ref):
    even = (lane_index(PAIRS) // 32) % 2 == 0
    blocks = (own_ref, far_ref)
    totals = [[jnp.zeros((FEW, LANES), F32) for _ in range(SEG)] for _ in blocks]
    for band in range(BANDS):
        for seg in range(SEG):
            first = 32 * seg + 2 * band
            rows = slice(seg * FEW, (seg + 1) * FEW)
            weight = jnp.where(
                even, guide_ref[:, first : first + 1], guide_ref[:, first + 1 : first + 2]
            )
            for half in range(HALVES):
                part = weight[half * FEW : (half + 1) * FEW]
                for k, block_ref in enumerate(blocks):
                    value = block_ref[band, half, rows, :].astype(F32) * part
                    value_ref[band * HALVES + half, k, rows, :] = value
                    totals[k][seg] = totals[k][seg] + value * value
    for k in range(len(blocks)):
        for seg in range(SEG):
            total = jnp.sum(totals[k][seg], axis=0, keepdims=True)
            total = jnp.broadcast_to(total, (8, LANES))
            total = total + pltpu.roll(total, 64, 1)
            total = total + pltpu.roll(total, 32, 1)
            level = (total * (0.1 / (64.0 * BANDS)) + 1e-06)[:1]
            rows = slice(seg * FEW, (seg + 1) * FEW)
            for place in range(BANDS * HALVES):
                value = value_ref[place, k, rows, :]
                energy = value * value
                energy = energy + pltpu.roll(energy, 64, 1)
                white_ref[place, k, rows, :] = (value * lax.rsqrt(energy + level)).astype(BF16)


def whitened_of(guides, own, far):
    vmem = pl.BlockSpec(memory_space=pltpu.VMEM)
    shape = (BANDS * HALVES, 2, ROWS, LANES)
    return pl.pallas_call(
        whiten_kernel,
        in_specs=[vmem] * 3,
        out_specs=vmem,
        out_shape=jax.ShapeDtypeStruct(shape, BF16),
        scratch_shapes=[pltpu.VMEM(shape, F32)],
        compiler_params=pltpu.CompilerParams(vmem_limit_bytes=32 * 1024 * 1024),
        name="whiten",
    )(guides, own, far)


def gather_rows(parts_ref, block_ref, wide_ref):
    for window in range(BANDS):
        for which in range(4):
            at = window * PITCH + which * ROWS
            part = parts_ref[window * HALVES + which // 2, which % 2]
            wide_ref[at : at + ROWS, :] = part.astype(F32)
    for pair in range(FEW):
        for which in range(4):
            rows = [
                wide_ref[pl.ds(which * ROWS + seg * FEW + pair, BANDS, stride=PITCH), :]
                for seg in range(SEG)
            ]
            block_ref[pair, which] = jnp.concatenate(rows, axis=0).astype(BF16)


def cross_rows(left_side, block_ref, out_ref, near_ref, far_ref):
    sign = jnp.where(lane_index(BANDS * SEG) < 64, 1.0, -1.0)
    for pair in range(FEW):
        turned = jnp.transpose(block_ref[pair, 2 * left_side].astype(F32))
        left = jnp.concatenate([turned[:64], turned[64:]], axis=1).astype(BF16)
        for which, stack_ref in ((3 * (1 - left_side), near_ref), (2 * left_side + 1, far_ref)):
            right = block_ref[pair, which].astype(F32)
            mix = jnp.concatenate([right * sign, pltpu.roll(right, 64, 1)], axis=0).astype(BF16)
            product = jnp.dot(left, mix, preferred_element_type=F32)
            stack_ref[pair * 2 * CH : (pair + 1) * 2 * CH, :] = product

    lane = lane_index(CH)
    even = lane % 2 == 0
    for first in range(0, CH, 4):
        pieces = {}
        for back, stack_ref in enumerate((near_ref, far_ref)):
            rows = [stack_ref[pl.ds(first + k, 2 * FEW, stride=CH), :] for k in range(4)]
            turned = jnp.transpose(jnp.concatenate(rows, axis=0)) * 0.125
            pieces[back] = jnp.where(even, turned[:32], turned[32:64])
            pieces[2 + back] = jnp.where(even, turned[64:96], turned[96:])
        for k in range(4):
            line = None
            for group in range(4):
                part = pieces[group]
                if group != k:
                    part = pltpu.roll(part, (group - k) * 32 % LANES, 1)
                line = part if line is None else jnp.where(lane // 32 == group, part, line)
            out_ref[first + k] = line.astype(BF16)


def other_kernel(parts_ref, out_ref, block_ref, wide_ref, near_ref, far_ref):
    gather_rows(parts_ref, block_ref, wide_ref)
    cross_rows(1 - lax.axis_index("rgrp") % 2, block_ref, out_ref, near_ref, far_ref)


def mine_kernel(block_ref, out_ref, near_ref, far_ref):
    cross_rows(lax.axis_index("rgrp") % 2, block_ref, out_ref, near_ref, far_ref)


STACK = pltpu.VMEM((2 * FEW * CH, LANES), F32)
CROSS = jax.ShapeDtypeStruct((CH, CH, LANES), BF16)


def other_of(parts):
    vmem = pl.BlockSpec(memory_space=pltpu.VMEM)
    return pl.pallas_call(
        other_kernel,
        in_specs=[vmem],
        out_specs=[vmem, vmem],
        out_shape=[CROSS, jax.ShapeDtypeStruct((FEW, 4, BANDS * SEG, LANES), BF16)],
        scratch_shapes=[pltpu.VMEM((BANDS * PITCH, LANES), F32), STACK, STACK],
        compiler_params=pltpu.CompilerParams(vmem_limit_bytes=32 * 1024 * 1024),
        name="cross_other",
    )(parts)


def mine_of(blocks):
    vmem = pl.BlockSpec(memory_space=pltpu.VMEM)
    return pl.pallas_call(
        mine_kernel,
        in_specs=[vmem],
        out_specs=vmem,
        out_shape=CROSS,
        scratch_shapes=[STACK, STACK],
        compiler_params=pltpu.CompilerParams(vmem_limit_bytes=32 * 1024 * 1024),
        cost_estimate=pl.CostEstimate(flops=2**28, bytes_accessed=2**23, transcendentals=0),
        name="cross_mine",
    )(blocks)


def merge_kernel(own_ref, other_ref, out_ref):
    first = lax.axis_index("rgrp") % 2 == 0
    even = (lane_index(CH) // 32) % 2 == 0

    def channel(i, carry):
        own = own_ref[i].astype(F32)
        other = other_ref[i].astype(F32)
        low = jnp.where(first, own, other)
        high = jnp.where(first, other, own)
        out_ref[0, i] = jnp.where(even, low, pltpu.roll(high, 32, 1)).astype(BF16)
        out_ref[1, i] = jnp.where(even, pltpu.roll(low, 96, 1), high).astype(BF16)
        return carry

    lax.fori_loop(0, CH, channel, 0, unroll=CH)


def merged_of(own, other):
    vmem = pl.BlockSpec(memory_space=pltpu.VMEM)
    return pl.pallas_call(
        merge_kernel,
        in_specs=[vmem] * 2,
        out_specs=vmem,
        out_shape=jax.ShapeDtypeStruct((2, CH, CH, LANES), BF16),
        compiler_params=pltpu.CompilerParams(vmem_limit_bytes=32 * 1024 * 1024),
        name="merge",
    )(own, other)


def beside(value):
    return lax.ppermute(value, "rgrp", [(g, g ^ 1) for g in range(32)])


def local(table, traces, segment_offsets, channel_order, pilot_channel):
    own, guide = spectra_of(segment_offsets, channel_order, pilot_channel, traces, table)
    far = lax.ppermute(own, "rgrp", [(g, (g + 2) % 32) for g in range(32)])
    guide = guide + beside(guide)
    lines = [[2 * z + side for z in range(16)] for side in range(2)]
    guides = lax.all_to_all(
        jnp.broadcast_to(guide, (16, PAIRS, LANES)),
        "rgrp",
        split_axis=0,
        concat_axis=0,
        tiled=True,
        axis_index_groups=lines,
    )
    white = whitened_of(total_of(guides), own, far)
    planes = [[32 * f + 2 * z + side for f in range(BANDS) for side in range(2)] for z in range(16)]
    parts = lax.all_to_all(
        white, ("freq", "rgrp"), split_axis=0, concat_axis=0, tiled=True, axis_index_groups=planes
    )
    other, blocks = other_of(parts)
    other = beside(other)
    return merged_of(mine_of(blocks), other)


def solution(mesh):
    table = quarter_table()
    specs = (P(), P("rgrp", "freq"), P("freq"), P("rgrp", None), P())
    inner = jax.shard_map(
        local, mesh=mesh, in_specs=specs, out_specs=P(None, "rgrp", None, "freq"), check_vma=False
    )

    def run(traces, segment_offsets, channel_order, pilot_channel):
        return inner(jnp.asarray(table), traces, segment_offsets, channel_order, pilot_channel)

    return run
```

```python
import functools
import math

import jax
import jax.numpy as jnp
import ml_dtypes
import numpy as np
from jax import lax
from jax.experimental import pallas as pl
from jax.experimental.pallas import tpu as pltpu
from jax.sharding import PartitionSpec as P

L = 2048
QUARTER = 512
PARTS = 1
BANDS = 16
SEG = 4
CH = 32
PAIRS = 32
SPAN = 9216
HALVES = 2
FEW = 16
ROWS = SEG * FEW
PITCH = 4 * ROWS + 8
LANES = 128
BF16 = jnp.bfloat16
F32 = jnp.float32


def quarter_table():
    part, parity, band, pair = np.ogrid[:PARTS, :2, : BANDS // PARTS, :PAIRS]
    which_bin = 64 * (part * (BANDS // PARTS) + band) + 2 * pair + parity + 1
    sample = np.arange(QUARTER)
    residue = (which_bin[..., None] * sample) % L
    phase_angle = residue.astype(np.float32) * np.float32(2.0 * math.pi / L)
    factor = np.float32(1.0 / math.sqrt(L))
    both = np.stack([np.cos(phase_angle) * factor, np.sin(phase_angle) * factor], axis=3)
    return both.reshape(PARTS, 2, -1, QUARTER).astype(ml_dtypes.bfloat16)


def lane_index(rows):
    return lax.broadcasted_iota(jnp.int32, (rows, LANES), 1)


def cut_windows(offset_ref, order_ref, traces_ref, wide_ref, wave_ref):
    lane = lane_index(CH)
    row = lax.broadcasted_iota(jnp.int32, (CH, CH), 0)
    picked = jnp.zeros((CH, CH), jnp.int32)
    for channel in range(CH):
        picked = jnp.where(row == channel, order_ref[0, channel], picked)
    chosen = (lax.broadcasted_iota(jnp.int32, (CH, CH), 1) == picked).astype(F32).astype(BF16)
    tiles = L // LANES
    for seg in range(SEG):
        start = seg * L + offset_ref[seg]
        base = jnp.minimum((start // LANES) * LANES, SPAN - (L + LANES))
        base = pl.multiple_of(base, LANES)
        rest = start - base
        turn = lax.rem(LANES - rest, LANES)
        rolled = []
        for tile in range(tiles + 1):
            part = traces_ref[:, pl.ds(pl.multiple_of(base + tile * LANES, LANES), LANES)]
            rolled.append(pltpu.roll(part.astype(F32), turn, 1))
        window = [
            jnp.where(lane < LANES - rest, rolled[tile], rolled[tile + 1]) for tile in range(tiles)
        ]
        quarter = tiles // 4
        first, second, third, fourth = (
            jnp.concatenate(window[k * quarter : (k + 1) * quarter], axis=1) for k in range(4)
        )
        even, odd = first + third, second + fourth
        mixes = (first - third, second - fourth, even - odd, even + odd)
        for k, mix in enumerate(mixes):
            mix = jnp.dot(chosen, mix.astype(BF16), preferred_element_type=F32)
            at = (k % 2) * LANES + seg * CH
            wide_ref[k // 2, at : at + CH, :] = mix
    for parity in range(2):
        wave_ref[parity] = jnp.transpose(wide_ref[parity]).astype(BF16)


def spectra_kernel(
    offset_hbm, order_hbm, pilot_hbm, traces_hbm, table_hbm, block_ref, guide_ref,
    offset_ref, order_ref, pilot_ref, traces_ref, table_ref, wide_ref, wave_ref,
    power_ref, sems, table_sems,
):
    small = [
        pltpu.make_async_copy(source, target, sems.at[k])
        for k, (source, target) in enumerate(
            (
                (traces_hbm, traces_ref),
                (offset_hbm, offset_ref),
                (order_hbm, order_ref),
                (pilot_hbm, pilot_ref),
            )
        )
    ]
    for copy in small:
        copy.start()
    table = [
        pltpu.make_async_copy(table_hbm.at[part], table_ref.at[part], table_sems.at[part])
        for part in range(PARTS)
    ]
    for copy in table:
        copy.start()
    power_ref[...] = jnp.zeros_like(power_ref)
    for copy in small:
        copy.wait()
    cut_windows(offset_ref, order_ref, traces_ref, wide_ref, wave_ref)

    lane = lane_index(PAIRS)
    channel = lax.rem(pilot_ref[0], CH)
    odd_pair = lax.broadcasted_iota(jnp.int32, (PAIRS, LANES), 0) % 2 == 1
    flip = jnp.where(odd_pair, -1.0, 1.0)
    for slab in range(PARTS):
        table[slab].wait()
        products = [
            jnp.dot(table_ref[slab, parity], wave_ref[parity], preferred_element_type=F32)
            for parity in range(2)
        ]
        for local_band in range(BANDS // PARTS):
            band = slab * (BANDS // PARTS) + local_band
            at = 2 * PAIRS * local_band
            parts = {}
            cosine = products[0][at : at + PAIRS]
            sine = products[0][at + PAIRS : at + 2 * PAIRS]
            parts[0, 0] = cosine[:, :LANES] - flip * sine[:, LANES:]
            parts[1, 0] = -sine[:, :LANES] - flip * cosine[:, LANES:]
            cosine = products[1][at : at + PAIRS]
            sine = products[1][at + PAIRS : at + 2 * PAIRS]
            parts[0, 1] = jnp.where(odd_pair, cosine[:, LANES:], cosine[:, :LANES])
            parts[1, 1] = -jnp.where(odd_pair, sine[:, LANES:], sine[:, :LANES])
            for parity in range(2):
                real = parts[0, parity].astype(BF16).astype(F32)
                imag = parts[1, parity].astype(BF16).astype(F32)
                place = 2 * band + parity
                power = pltpu.roll(
                    real * real + imag * imag, lax.rem(place - channel + LANES, LANES), 1
                )
                power_ref[...] = jnp.where(lane % 32 == place, power, power_ref[...])
            for seg in range(SEG):
                line = None
                for side in range(2):
                    for parity in range(2):
                        group = side * 2 + parity
                        part = parts[side, parity]
                        if group != seg:
                            part = pltpu.roll(part, (group - seg) * 32 % LANES, 1)
                        line = part if line is None else jnp.where(lane // 32 == group, part, line)
                line = line.astype(BF16)
                for half in range(HALVES):
                    block_ref[band, half, seg * FEW : (seg + 1) * FEW, :] = line[
                        half * FEW : (half + 1) * FEW
                    ]
    mine = pilot_ref[0] // CH == lax.axis_index("rgrp")
    guide_ref[...] = jnp.where(mine, jnp.sqrt(power_ref[...]), 0.0).astype(BF16)


def spectra_of(offsets, order, pilot, traces, table):
    vmem = pl.BlockSpec(memory_space=pltpu.VMEM)
    offsets, order, traces, table = (
        pltpu.with_memory_space_constraint(value, pltpu.HBM)
        for value in (offsets, order, traces, table)
    )
    return pl.pallas_call(
        spectra_kernel,
        in_specs=[pl.BlockSpec(memory_space=pl.ANY)] * 5,
        out_specs=[vmem, vmem],
        out_shape=[
            jax.ShapeDtypeStruct((BANDS, HALVES, SEG * FEW, LANES), BF16),
            jax.ShapeDtypeStruct((PAIRS, LANES), BF16),
        ],
        scratch_shapes=[
            pltpu.SMEM((SEG,), jnp.int32),
            pltpu.SMEM((1, CH), jnp.int32),
            pltpu.SMEM((1,), jnp.int32),
            pltpu.VMEM((CH, SPAN), BF16),
            pltpu.VMEM((PARTS, 2, 2 * PAIRS * BANDS // PARTS, QUARTER), BF16),
            pltpu.VMEM((2, 2 * LANES, QUARTER), F32),
            pltpu.VMEM((2, QUARTER, 2 * LANES), BF16),
            pltpu.VMEM((PAIRS, LANES), F32),
            pltpu.SemaphoreType.DMA((4,)),
            pltpu.SemaphoreType.DMA((PARTS,)),
        ],
        compiler_params=pltpu.CompilerParams(vmem_limit_bytes=16 * 1024 * 1024),
        name="spectra",
    )(offsets, order, pilot, traces, table)


def total_kernel(guides_ref, guide_ref):
    guide = guides_ref[0].astype(F32)
    for line in range(1, 16):
        guide = guide + guides_ref[line].astype(F32)
    guide_ref[...] = guide


def total_of(guides):
    vmem = pl.BlockSpec(memory_space=pltpu.VMEM)
    return pl.pallas_call(
        total_kernel,
        in_specs=[vmem],
        out_specs=vmem,
        out_shape=jax.ShapeDtypeStruct((PAIRS, LANES), F32),
        compiler_params=pltpu.CompilerParams(vmem_limit_bytes=32 * 1024 * 1024),
        cost_estimate=pl.CostEstimate(flops=2**28, bytes_accessed=2**17, transcendentals=0),
        name="total",
    )(guides)


def whiten_kernel(guide_ref, own_ref, far_ref, white_ref, value_ref):
    even = (lane_index(PAIRS) // 32) % 2 == 0
    blocks = (own_ref, far_ref)
    totals = [[jnp.zeros((FEW, LANES), F32) for _ in range(SEG)] for _ in blocks]
    for band in range(BANDS):
        for seg in range(SEG):
            first = 32 * seg + 2 * band
            rows = slice(seg * FEW, (seg + 1) * FEW)
            weight = jnp.where(
                even, guide_ref[:, first : first + 1], guide_ref[:, first + 1 : first + 2]
            )
            for half in range(HALVES):
                part = weight[half * FEW : (half + 1) * FEW]
                for k, block_ref in enumerate(blocks):
                    value = block_ref[band, half, rows, :].astype(F32) * part
                    value_ref[band * HALVES + half, k, rows, :] = value
                    totals[k][seg] = totals[k][seg] + value * value
    for k in range(len(blocks)):
        for seg in range(SEG):
            total = jnp.sum(totals[k][seg], axis=0, keepdims=True)
            total = jnp.broadcast_to(total, (8, LANES))
            total = total + pltpu.roll(total, 64, 1)
            total = total + pltpu.roll(total, 32, 1)
            level = (total * (0.1 / (64.0 * BANDS)) + 1e-06)[:1]
            rows = slice(seg * FEW, (seg + 1) * FEW)
            for place in range(BANDS * HALVES):
                value = value_ref[place, k, rows, :]
                energy = value * value
                energy = energy + pltpu.roll(energy, 64, 1)
                white_ref[place, k, rows, :] = (value * lax.rsqrt(energy + level)).astype(BF16)


def whitened_of(guides, own, far):
    vmem = pl.BlockSpec(memory_space=pltpu.VMEM)
    shape = (BANDS * HALVES, 2, ROWS, LANES)
    return pl.pallas_call(
        whiten_kernel,
        in_specs=[vmem] * 3,
        out_specs=vmem,
        out_shape=jax.ShapeDtypeStruct(shape, BF16),
        scratch_shapes=[pltpu.VMEM(shape, F32)],
        compiler_params=pltpu.CompilerParams(vmem_limit_bytes=32 * 1024 * 1024),
        name="whiten",
    )(guides, own, far)


def gather_rows(parts_ref, block_ref, wide_ref):
    for window in range(BANDS):
        for which in range(4):
            at = window * PITCH + which * ROWS
            part = parts_ref[window * HALVES + which // 2, which % 2]
            wide_ref[at : at + ROWS, :] = part.astype(F32)
    for pair in range(FEW):
        for which in range(4):
            rows = [
                wide_ref[pl.ds(which * ROWS + seg * FEW + pair, BANDS, stride=PITCH), :]
                for seg in range(SEG)
            ]
            block_ref[pair, which] = jnp.concatenate(rows, axis=0).astype(BF16)


def cross_rows(left_side, block_ref, out_ref, near_ref, far_ref):
    sign = jnp.where(lane_index(BANDS * SEG) < 64, 1.0, -1.0)
    for pair in range(FEW):
        turned = jnp.transpose(block_ref[pair, 2 * left_side].astype(F32))
        left = jnp.concatenate([turned[:64], turned[64:]], axis=1).astype(BF16)
        for which, stack_ref in ((3 * (1 - left_side), near_ref), (2 * left_side + 1, far_ref)):
            right = block_ref[pair, which].astype(F32)
            mix = jnp.concatenate([right * sign, pltpu.roll(right, 64, 1)], axis=0).astype(BF16)
            product = jnp.dot(left, mix, preferred_element_type=F32)
            stack_ref[pair * 2 * CH : (pair + 1) * 2 * CH, :] = product

    lane = lane_index(CH)
    even = lane % 2 == 0
    for first in range(0, CH, 4):
        pieces = {}
        for back, stack_ref in enumerate((near_ref, far_ref)):
            rows = [stack_ref[pl.ds(first + k, 2 * FEW, stride=CH), :] for k in range(4)]
            turned = jnp.transpose(jnp.concatenate(rows, axis=0)) * 0.125
            pieces[back] = jnp.where(even, turned[:32], turned[32:64])
            pieces[2 + back] = jnp.where(even, turned[64:96], turned[96:])
        for k in range(4):
            line = None
            for group in range(4):
                part = pieces[group]
                if group != k:
                    part = pltpu.roll(part, (group - k) * 32 % LANES, 1)
                line = part if line is None else jnp.where(lane // 32 == group, part, line)
            out_ref[first + k] = line.astype(BF16)


def other_kernel(parts_ref, out_ref, block_ref, wide_ref, near_ref, far_ref):
    gather_rows(parts_ref, block_ref, wide_ref)
    cross_rows(1 - lax.axis_index("rgrp") % 2, block_ref, out_ref, near_ref, far_ref)


def mine_kernel(block_ref, out_ref, near_ref, far_ref):
    cross_rows(lax.axis_index("rgrp") % 2, block_ref, out_ref, near_ref, far_ref)


STACK = pltpu.VMEM((2 * FEW * CH, LANES), F32)
CROSS = jax.ShapeDtypeStruct((CH, CH, LANES), BF16)


def other_of(parts):
    vmem = pl.BlockSpec(memory_space=pltpu.VMEM)
    return pl.pallas_call(
        other_kernel,
        in_specs=[vmem],
        out_specs=[vmem, vmem],
        out_shape=[CROSS, jax.ShapeDtypeStruct((FEW, 4, BANDS * SEG, LANES), BF16)],
        scratch_shapes=[pltpu.VMEM((BANDS * PITCH, LANES), F32), STACK, STACK],
        compiler_params=pltpu.CompilerParams(vmem_limit_bytes=32 * 1024 * 1024),
        name="cross_other",
    )(parts)


def mine_of(blocks):
    vmem = pl.BlockSpec(memory_space=pltpu.VMEM)
    return pl.pallas_call(
        mine_kernel,
        in_specs=[vmem],
        out_specs=vmem,
        out_shape=CROSS,
        scratch_shapes=[STACK, STACK],
        compiler_params=pltpu.CompilerParams(vmem_limit_bytes=32 * 1024 * 1024),
        cost_estimate=pl.CostEstimate(flops=2**28, bytes_accessed=2**23, transcendentals=0),
        name="cross_mine",
    )(blocks)


def merge_kernel(own_ref, other_ref, out_ref):
    first = lax.axis_index("rgrp") % 2 == 0
    even = (lane_index(CH) // 32) % 2 == 0

    def channel(i, carry):
        own = own_ref[i].astype(F32)
        other = other_ref[i].astype(F32)
        low = jnp.where(first, own, other)
        high = jnp.where(first, other, own)
        out_ref[0, i] = jnp.where(even, low, pltpu.roll(high, 32, 1)).astype(BF16)
        out_ref[1, i] = jnp.where(even, pltpu.roll(low, 96, 1), high).astype(BF16)
        return carry

    lax.fori_loop(0, CH, channel, 0, unroll=CH)


def merged_of(own, other):
    vmem = pl.BlockSpec(memory_space=pltpu.VMEM)
    return pl.pallas_call(
        merge_kernel,
        in_specs=[vmem] * 2,
        out_specs=vmem,
        out_shape=jax.ShapeDtypeStruct((2, CH, CH, LANES), BF16),
        compiler_params=pltpu.CompilerParams(vmem_limit_bytes=32 * 1024 * 1024),
        name="merge",
    )(own, other)


def beside(value):
    return lax.ppermute(value, "rgrp", [(g, g ^ 1) for g in range(32)])


def local(table, traces, segment_offsets, channel_order, pilot_channel):
    own, guide = spectra_of(segment_offsets, channel_order, pilot_channel, traces, table)
    far = lax.ppermute(own, "rgrp", [(g, (g + 2) % 32) for g in range(32)])
    guide = guide + beside(guide)
    lines = [[2 * z + side for z in range(16)] for side in range(2)]
    guides = lax.all_to_all(
        jnp.broadcast_to(guide, (16, PAIRS, LANES)),
        "rgrp",
        split_axis=0,
        concat_axis=0,
        tiled=True,
        axis_index_groups=lines,
    )
    white = whitened_of(total_of(guides), own, far)
    planes = [[32 * f + 2 * z + side for f in range(BANDS) for side in range(2)] for z in range(16)]
    parts = lax.all_to_all(
        white, ("freq", "rgrp"), split_axis=0, concat_axis=0, tiled=True, axis_index_groups=planes
    )
    other, blocks = other_of(parts)
    other = beside(other)
    return merged_of(mine_of(blocks), other)


def solution(mesh):
    table = quarter_table()
    specs = (P(), P("rgrp", "freq"), P("freq"), P("rgrp", None), P())
    inner = jax.shard_map(
        local, mesh=mesh, in_specs=specs, out_specs=P(None, "rgrp", None, "freq"), check_vma=False
    )

    def run(traces, segment_offsets, channel_order, pilot_channel):
        return inner(jnp.asarray(table), traces, segment_offsets, channel_order, pilot_channel)

    return run
```

```python
import functools
import math

import jax
import jax.numpy as jnp
import ml_dtypes
import numpy as np
from jax import lax
from jax.experimental import pallas as pl
from jax.experimental.pallas import tpu as pltpu
from jax.sharding import PartitionSpec as P

L = 2048
QUARTER = 512
PARTS = 1
BANDS = 16
SEG = 4
CH = 32
PAIRS = 32
SPAN = 9216
HALVES = 2
FEW = 16
ROWS = SEG * FEW
PITCH = 4 * ROWS + 8
LANES = 128
BF16 = jnp.bfloat16
F32 = jnp.float32


def quarter_table():
    part, parity, band, pair = np.ogrid[:PARTS, :2, : BANDS // PARTS, :PAIRS]
    which_bin = 64 * (part * (BANDS // PARTS) + band) + 2 * pair + parity + 1
    sample = np.arange(QUARTER)
    residue = (which_bin[..., None] * sample) % L
    phase_angle = residue.astype(np.float32) * np.float32(2.0 * math.pi / L)
    factor = np.float32(1.0 / math.sqrt(L))
    both = np.stack([np.cos(phase_angle) * factor, np.sin(phase_angle) * factor], axis=3)
    return both.reshape(PARTS, 2, -1, QUARTER).astype(ml_dtypes.bfloat16)


def lane_index(rows):
    return lax.broadcasted_iota(jnp.int32, (rows, LANES), 1)


def cut_windows(offset_ref, order_ref, traces_ref, wide_ref, wave_ref):
    lane = lane_index(CH)
    row = lax.broadcasted_iota(jnp.int32, (CH, CH), 0)
    picked = jnp.zeros((CH, CH), jnp.int32)
    for channel in range(CH):
        picked = jnp.where(row == channel, order_ref[0, channel], picked)
    chosen = (lax.broadcasted_iota(jnp.int32, (CH, CH), 1) == picked).astype(F32).astype(BF16)
    tiles = L // LANES
    for seg in range(SEG):
        start = seg * L + offset_ref[seg]
        base = jnp.minimum((start // LANES) * LANES, SPAN - (L + LANES))
        base = pl.multiple_of(base, LANES)
        rest = start - base
        turn = lax.rem(LANES - rest, LANES)
        rolled = []
        for tile in range(tiles + 1):
            part = traces_ref[:, pl.ds(pl.multiple_of(base + tile * LANES, LANES), LANES)]
            rolled.append(pltpu.roll(part.astype(F32), turn, 1))
        window = [
            jnp.where(lane < LANES - rest, rolled[tile], rolled[tile + 1]) for tile in range(tiles)
        ]
        quarter = tiles // 4
        first, second, third, fourth = (
            jnp.concatenate(window[k * quarter : (k + 1) * quarter], axis=1) for k in range(4)
        )
        even, odd = first + third, second + fourth
        mixes = (first - third, second - fourth, even - odd, even + odd)
        for k, mix in enumerate(mixes):
            mix = jnp.dot(chosen, mix.astype(BF16), preferred_element_type=F32)
            at = (k % 2) * LANES + seg * CH
            wide_ref[k // 2, at : at + CH, :] = mix
    for parity in range(2):
        wave_ref[parity] = jnp.transpose(wide_ref[parity]).astype(BF16)


def spectra_kernel(
    offset_hbm, order_hbm, pilot_hbm, traces_hbm, table_hbm, block_ref, guide_ref,
    offset_ref, order_ref, pilot_ref, traces_ref, table_ref, wide_ref, wave_ref,
    power_ref, sems, table_sems,
):
    small = [
        pltpu.make_async_copy(source, target, sems.at[k])
        for k, (source, target) in enumerate(
            (
                (traces_hbm, traces_ref),
                (offset_hbm, offset_ref),
                (order_hbm, order_ref),
                (pilot_hbm, pilot_ref),
            )
        )
    ]
    for copy in small:
        copy.start()
    table = [
        pltpu.make_async_copy(table_hbm.at[part], table_ref.at[part], table_sems.at[part])
        for part in range(PARTS)
    ]
    for copy in table:
        copy.start()
    power_ref[...] = jnp.zeros_like(power_ref)
    for copy in small:
        copy.wait()
    cut_windows(offset_ref, order_ref, traces_ref, wide_ref, wave_ref)

    lane = lane_index(PAIRS)
    channel = lax.rem(pilot_ref[0], CH)
    odd_pair = lax.broadcasted_iota(jnp.int32, (PAIRS, LANES), 0) % 2 == 1
    flip = jnp.where(odd_pair, -1.0, 1.0)
    for slab in range(PARTS):
        table[slab].wait()
        products = [
            jnp.dot(table_ref[slab, parity], wave_ref[parity], preferred_element_type=F32)
            for parity in range(2)
        ]
        for local_band in range(BANDS // PARTS):
            band = slab * (BANDS // PARTS) + local_band
            at = 2 * PAIRS * local_band
            parts = {}
            cosine = products[0][at : at + PAIRS]
            sine = products[0][at + PAIRS : at + 2 * PAIRS]
            parts[0, 0] = cosine[:, :LANES] - flip * sine[:, LANES:]
            parts[1, 0] = -sine[:, :LANES] - flip * cosine[:, LANES:]
            cosine = products[1][at : at + PAIRS]
            sine = products[1][at + PAIRS : at + 2 * PAIRS]
            parts[0, 1] = jnp.where(odd_pair, cosine[:, LANES:], cosine[:, :LANES])
            parts[1, 1] = -jnp.where(odd_pair, sine[:, LANES:], sine[:, :LANES])
            for parity in range(2):
                real = parts[0, parity].astype(BF16).astype(F32)
                imag = parts[1, parity].astype(BF16).astype(F32)
                place = 2 * band + parity
                power = pltpu.roll(
                    real * real + imag * imag, lax.rem(place - channel + LANES, LANES), 1
                )
                power_ref[...] = jnp.where(lane % 32 == place, power, power_ref[...])
            for seg in range(SEG):
                line = None
                for side in range(2):
                    for parity in range(2):
                        group = side * 2 + parity
                        part = parts[side, parity]
                        if group != seg:
                            part = pltpu.roll(part, (group - seg) * 32 % LANES, 1)
                        line = part if line is None else jnp.where(lane // 32 == group, part, line)
                line = line.astype(BF16)
                for half in range(HALVES):
                    block_ref[band, half, seg * FEW : (seg + 1) * FEW, :] = line[
                        half * FEW : (half + 1) * FEW
                    ]
    mine = pilot_ref[0] // CH == lax.axis_index("rgrp")
    guide_ref[...] = jnp.where(mine, jnp.sqrt(power_ref[...]), 0.0).astype(BF16)


def spectra_of(offsets, order, pilot, traces, table):
    vmem = pl.BlockSpec(memory_space=pltpu.VMEM)
    offsets, order, traces, table = (
        pltpu.with_memory_space_constraint(value, pltpu.HBM)
        for value in (offsets, order, traces, table)
    )
    return pl.pallas_call(
        spectra_kernel,
        in_specs=[pl.BlockSpec(memory_space=pl.ANY)] * 5,
        out_specs=[vmem, vmem],
        out_shape=[
            jax.ShapeDtypeStruct((BANDS, HALVES, SEG * FEW, LANES), BF16),
            jax.ShapeDtypeStruct((PAIRS, LANES), BF16),
        ],
        scratch_shapes=[
            pltpu.SMEM((SEG,), jnp.int32),
            pltpu.SMEM((1, CH), jnp.int32),
            pltpu.SMEM((1,), jnp.int32),
            pltpu.VMEM((CH, SPAN), BF16),
            pltpu.VMEM((PARTS, 2, 2 * PAIRS * BANDS // PARTS, QUARTER), BF16),
            pltpu.VMEM((2, 2 * LANES, QUARTER), F32),
            pltpu.VMEM((2, QUARTER, 2 * LANES), BF16),
            pltpu.VMEM((PAIRS, LANES), F32),
            pltpu.SemaphoreType.DMA((4,)),
            pltpu.SemaphoreType.DMA((PARTS,)),
        ],
        compiler_params=pltpu.CompilerParams(vmem_limit_bytes=16 * 1024 * 1024),
        name="spectra",
    )(offsets, order, pilot, traces, table)


def total_kernel(guides_ref, guide_ref):
    guide = guides_ref[0].astype(F32)
    for line in range(1, 16):
        guide = guide + guides_ref[line].astype(F32)
    guide_ref[...] = guide


def total_of(guides):
    vmem = pl.BlockSpec(memory_space=pltpu.VMEM)
    return pl.pallas_call(
        total_kernel,
        in_specs=[vmem],
        out_specs=vmem,
        out_shape=jax.ShapeDtypeStruct((PAIRS, LANES), F32),
        compiler_params=pltpu.CompilerParams(vmem_limit_bytes=32 * 1024 * 1024),
        cost_estimate=pl.CostEstimate(flops=2**28, bytes_accessed=2**17, transcendentals=0),
        name="total",
    )(guides)


def whiten_kernel(guide_ref, own_ref, far_ref, white_ref, value_ref):
    guide = guide_ref[...]
    place = lane_index(PAIRS) // 2
    parity = lax.broadcasted_iota(jnp.int32, (LANES, LANES), 0) % 2
    spread = (parity == (lane_index(LANES) // 32) % 2).astype(F32).astype(BF16)
    blocks = (own_ref, far_ref)
    totals = [[jnp.zeros((FEW, LANES), F32) for _ in range(SEG)] for _ in blocks]
    for band in range(BANDS):
        picked = [jnp.where(place == seg * BANDS + band, guide, 0.0) for seg in range(SEG)]
        weight = jnp.dot(
            jnp.concatenate(picked, axis=0).astype(BF16), spread, preferred_element_type=F32
        )
        for seg in range(SEG):
            rows = slice(seg * FEW, (seg + 1) * FEW)
            for half in range(HALVES):
                at = seg * PAIRS + half * FEW
                part = weight[at : at + FEW]
                for k, block_ref in enumerate(blocks):
                    value = block_ref[band, half, rows, :].astype(F32) * part
                    value_ref[band * HALVES + half, k, rows, :] = value
                    totals[k][seg] = totals[k][seg] + value * value
    for k in range(len(blocks)):
        for seg in range(SEG):
            total = jnp.sum(totals[k][seg], axis=0, keepdims=True)
            total = jnp.broadcast_to(total, (8, LANES))
            total = total + pltpu.roll(total, 64, 1)
            total = total + pltpu.roll(total, 32, 1)
            level = (total * (0.1 / (64.0 * BANDS)) + 1e-06)[:1]
            rows = slice(seg * FEW, (seg + 1) * FEW)
            for place in range(BANDS * HALVES):
                value = value_ref[place, k, rows, :]
                energy = value * value
                energy = energy + pltpu.roll(energy, 64, 1)
                white_ref[place, k, rows, :] = (value * lax.rsqrt(energy + level)).astype(BF16)


def whitened_of(guides, own, far):
    vmem = pl.BlockSpec(memory_space=pltpu.VMEM)
    shape = (BANDS * HALVES, 2, ROWS, LANES)
    return pl.pallas_call(
        whiten_kernel,
        in_specs=[vmem] * 3,
        out_specs=vmem,
        out_shape=jax.ShapeDtypeStruct(shape, BF16),
        scratch_shapes=[pltpu.VMEM(shape, F32)],
        compiler_params=pltpu.CompilerParams(vmem_limit_bytes=32 * 1024 * 1024),
        name="whiten",
    )(guides, own, far)


def gather_rows(parts_ref, block_ref, wide_ref):
    for window in range(BANDS):
        for which in range(4):
            at = window * PITCH + which * ROWS
            part = parts_ref[window * HALVES + which // 2, which % 2]
            wide_ref[at : at + ROWS, :] = part.astype(F32)
    for pair in range(FEW):
        for which in range(4):
            rows = [
                wide_ref[pl.ds(which * ROWS + seg * FEW + pair, BANDS, stride=PITCH), :]
                for seg in range(SEG)
            ]
            block_ref[pair, which] = jnp.concatenate(rows, axis=0).astype(BF16)


def cross_rows(left_side, block_ref, out_ref, near_ref, far_ref):
    sign = jnp.where(lane_index(BANDS * SEG) < 64, 1.0, -1.0)
    for pair in range(FEW):
        turned = jnp.transpose(block_ref[pair, 2 * left_side].astype(F32))
        left = jnp.concatenate([turned[:64], turned[64:]], axis=1).astype(BF16)
        for which, stack_ref in ((3 * (1 - left_side), near_ref), (2 * left_side + 1, far_ref)):
            right = block_ref[pair, which].astype(F32)
            mix = jnp.concatenate([right * sign, pltpu.roll(right, 64, 1)], axis=0).astype(BF16)
            product = jnp.dot(left, mix, preferred_element_type=F32)
            stack_ref[pair * 2 * CH : (pair + 1) * 2 * CH, :] = product

    lane = lane_index(CH)
    even = lane % 2 == 0
    for first in range(0, CH, 4):
        pieces = {}
        for back, stack_ref in enumerate((near_ref, far_ref)):
            rows = [stack_ref[pl.ds(first + k, 2 * FEW, stride=CH), :] for k in range(4)]
            turned = jnp.transpose(jnp.concatenate(rows, axis=0)) * 0.125
            pieces[back] = jnp.where(even, turned[:32], turned[32:64])
            pieces[2 + back] = jnp.where(even, turned[64:96], turned[96:])
        for k in range(4):
            line = None
            for group in range(4):
                part = pieces[group]
                if group != k:
                    part = pltpu.roll(part, (group - k) * 32 % LANES, 1)
                line = part if line is None else jnp.where(lane // 32 == group, part, line)
            out_ref[first + k] = line.astype(BF16)


def other_kernel(parts_ref, out_ref, block_ref, wide_ref, near_ref, far_ref):
    gather_rows(parts_ref, block_ref, wide_ref)
    cross_rows(1 - lax.axis_index("rgrp") % 2, block_ref, out_ref, near_ref, far_ref)


def mine_kernel(block_ref, out_ref, near_ref, far_ref):
    cross_rows(lax.axis_index("rgrp") % 2, block_ref, out_ref, near_ref, far_ref)


STACK = pltpu.VMEM((2 * FEW * CH, LANES), F32)
CROSS = jax.ShapeDtypeStruct((CH, CH, LANES), BF16)


def other_of(parts):
    vmem = pl.BlockSpec(memory_space=pltpu.VMEM)
    return pl.pallas_call(
        other_kernel,
        in_specs=[vmem],
        out_specs=[vmem, vmem],
        out_shape=[CROSS, jax.ShapeDtypeStruct((FEW, 4, BANDS * SEG, LANES), BF16)],
        scratch_shapes=[pltpu.VMEM((BANDS * PITCH, LANES), F32), STACK, STACK],
        compiler_params=pltpu.CompilerParams(vmem_limit_bytes=32 * 1024 * 1024),
        name="cross_other",
    )(parts)


def mine_of(blocks):
    vmem = pl.BlockSpec(memory_space=pltpu.VMEM)
    return pl.pallas_call(
        mine_kernel,
        in_specs=[vmem],
        out_specs=vmem,
        out_shape=CROSS,
        scratch_shapes=[STACK, STACK],
        compiler_params=pltpu.CompilerParams(vmem_limit_bytes=32 * 1024 * 1024),
        cost_estimate=pl.CostEstimate(flops=2**28, bytes_accessed=2**23, transcendentals=0),
        name="cross_mine",
    )(blocks)


def merge_kernel(own_ref, other_ref, out_ref):
    first = lax.axis_index("rgrp") % 2 == 0
    even = (lane_index(CH) // 32) % 2 == 0

    def channel(i, carry):
        own = own_ref[i].astype(F32)
        other = other_ref[i].astype(F32)
        low = jnp.where(first, own, other)
        high = jnp.where(first, other, own)
        out_ref[0, i] = jnp.where(even, low, pltpu.roll(high, 32, 1)).astype(BF16)
        out_ref[1, i] = jnp.where(even, pltpu.roll(low, 96, 1), high).astype(BF16)
        return carry

    lax.fori_loop(0, CH, channel, 0, unroll=CH)


def merged_of(own, other):
    vmem = pl.BlockSpec(memory_space=pltpu.VMEM)
    return pl.pallas_call(
        merge_kernel,
        in_specs=[vmem] * 2,
        out_specs=vmem,
        out_shape=jax.ShapeDtypeStruct((2, CH, CH, LANES), BF16),
        compiler_params=pltpu.CompilerParams(vmem_limit_bytes=32 * 1024 * 1024),
        name="merge",
    )(own, other)


def beside(value):
    return lax.ppermute(value, "rgrp", [(g, g ^ 1) for g in range(32)])


def local(table, traces, segment_offsets, channel_order, pilot_channel):
    own, guide = spectra_of(segment_offsets, channel_order, pilot_channel, traces, table)
    far = lax.ppermute(own, "rgrp", [(g, (g + 2) % 32) for g in range(32)])
    guide = guide + beside(guide)
    lines = [[2 * z + side for z in range(16)] for side in range(2)]
    guides = lax.all_to_all(
        jnp.broadcast_to(guide, (16, PAIRS, LANES)),
        "rgrp",
        split_axis=0,
        concat_axis=0,
        tiled=True,
        axis_index_groups=lines,
    )
    white = whitened_of(total_of(guides), own, far)
    planes = [[32 * f + 2 * z + side for f in range(BANDS) for side in range(2)] for z in range(16)]
    parts = lax.all_to_all(
        white, ("freq", "rgrp"), split_axis=0, concat_axis=0, tiled=True, axis_index_groups=planes
    )
    other, blocks = other_of(parts)
    other = beside(other)
    return merged_of(mine_of(blocks), other)


def solution(mesh):
    table = quarter_table()
    specs = (P(), P("rgrp", "freq"), P("freq"), P("rgrp", None), P())
    inner = jax.shard_map(
        local, mesh=mesh, in_specs=specs, out_specs=P(None, "rgrp", None, "freq"), check_vma=False
    )

    def run(traces, segment_offsets, channel_order, pilot_channel):
        return inner(jnp.asarray(table), traces, segment_offsets, channel_order, pilot_channel)

    return run
```

```python
import functools
import math

import jax
import jax.numpy as jnp
import ml_dtypes
import numpy as np
from jax import lax
from jax.experimental import pallas as pl
from jax.experimental.pallas import tpu as pltpu
from jax.sharding import PartitionSpec as P

L = 2048
QUARTER = 512
PARTS = 1
BANDS = 16
SEG = 4
CH = 32
PAIRS = 32
SPAN = 9216
HALVES = 2
FEW = 16
ROWS = SEG * FEW
PITCH = 4 * ROWS + 8
LANES = 128
BF16 = jnp.bfloat16
F32 = jnp.float32


def quarter_table():
    part, parity, band, pair = np.ogrid[:PARTS, :2, : BANDS // PARTS, :PAIRS]
    which_bin = 64 * (part * (BANDS // PARTS) + band) + 2 * pair + parity + 1
    sample = np.arange(QUARTER)
    residue = (which_bin[..., None] * sample) % L
    phase_angle = residue.astype(np.float32) * np.float32(2.0 * math.pi / L)
    factor = np.float32(1.0 / math.sqrt(L))
    both = np.stack([np.cos(phase_angle) * factor, np.sin(phase_angle) * factor], axis=3)
    return both.reshape(PARTS, 2, -1, QUARTER).astype(ml_dtypes.bfloat16)


def lane_index(rows):
    return lax.broadcasted_iota(jnp.int32, (rows, LANES), 1)


def cut_windows(offset_ref, order_ref, traces_ref, wide_ref, wave_ref):
    lane = lane_index(CH)
    row = lax.broadcasted_iota(jnp.int32, (CH, CH), 0)
    picked = jnp.zeros((CH, CH), jnp.int32)
    for channel in range(CH):
        picked = jnp.where(row == channel, order_ref[0, channel], picked)
    chosen = (lax.broadcasted_iota(jnp.int32, (CH, CH), 1) == picked).astype(F32).astype(BF16)
    tiles = L // LANES
    for seg in range(SEG):
        start = seg * L + offset_ref[seg]
        base = jnp.minimum((start // LANES) * LANES, SPAN - (L + LANES))
        base = pl.multiple_of(base, LANES)
        rest = start - base
        turn = lax.rem(LANES - rest, LANES)
        rolled = []
        for tile in range(tiles + 1):
            part = traces_ref[:, pl.ds(pl.multiple_of(base + tile * LANES, LANES), LANES)]
            rolled.append(pltpu.roll(part.astype(F32), turn, 1))
        window = [
            jnp.where(lane < LANES - rest, rolled[tile], rolled[tile + 1]) for tile in range(tiles)
        ]
        ordered = jnp.dot(
            chosen, jnp.concatenate(window, axis=1).astype(BF16), preferred_element_type=F32
        )
        first, second, third, fourth = (
            ordered[:, k * QUARTER : (k + 1) * QUARTER] for k in range(4)
        )
        even, odd = first + third, second + fourth
        for k, mix in enumerate((first - third, second - fourth, even - odd, even + odd)):
            at = (k % 2) * LANES + seg * CH
            wide_ref[k // 2, at : at + CH, :] = mix
    for parity in range(2):
        mix = jnp.transpose(wide_ref[parity])
        high = mix.astype(BF16)
        wave_ref[parity, 0] = high
        wave_ref[parity, 1] = (mix - high.astype(F32)).astype(BF16)


def spectra_kernel(
    offset_hbm, order_hbm, pilot_hbm, traces_hbm, table_hbm, block_ref, guide_ref,
    offset_ref, order_ref, pilot_ref, traces_ref, table_ref, wide_ref, wave_ref,
    power_ref, sems, table_sems,
):
    small = [
        pltpu.make_async_copy(source, target, sems.at[k])
        for k, (source, target) in enumerate(
            (
                (traces_hbm, traces_ref),
                (offset_hbm, offset_ref),
                (order_hbm, order_ref),
                (pilot_hbm, pilot_ref),
            )
        )
    ]
    for copy in small:
        copy.start()
    table = [
        pltpu.make_async_copy(table_hbm.at[part], table_ref.at[part], table_sems.at[part])
        for part in range(PARTS)
    ]
    for copy in table:
        copy.start()
    power_ref[...] = jnp.zeros_like(power_ref)
    for copy in small:
        copy.wait()
    cut_windows(offset_ref, order_ref, traces_ref, wide_ref, wave_ref)

    lane = lane_index(PAIRS)
    channel = lax.rem(pilot_ref[0], CH)
    odd_pair = lax.broadcasted_iota(jnp.int32, (PAIRS, LANES), 0) % 2 == 1
    flip = jnp.where(odd_pair, -1.0, 1.0)
    for slab in range(PARTS):
        table[slab].wait()
        products = [
            jnp.dot(table_ref[slab, parity], wave_ref[parity, 0], preferred_element_type=F32)
            + jnp.dot(table_ref[slab, parity], wave_ref[parity, 1], preferred_element_type=F32)
            for parity in range(2)
        ]
        for local_band in range(BANDS // PARTS):
            band = slab * (BANDS // PARTS) + local_band
            at = 2 * PAIRS * local_band
            parts = {}
            cosine = products[0][at : at + PAIRS]
            sine = products[0][at + PAIRS : at + 2 * PAIRS]
            parts[0, 0] = cosine[:, :LANES] - flip * sine[:, LANES:]
            parts[1, 0] = -sine[:, :LANES] - flip * cosine[:, LANES:]
            cosine = products[1][at : at + PAIRS]
            sine = products[1][at + PAIRS : at + 2 * PAIRS]
            parts[0, 1] = jnp.where(odd_pair, cosine[:, LANES:], cosine[:, :LANES])
            parts[1, 1] = -jnp.where(odd_pair, sine[:, LANES:], sine[:, :LANES])
            for parity in range(2):
                real = parts[0, parity].astype(BF16).astype(F32)
                imag = parts[1, parity].astype(BF16).astype(F32)
                place = 2 * band + parity
                power = pltpu.roll(
                    real * real + imag * imag, lax.rem(place - channel + LANES, LANES), 1
                )
                power_ref[...] = jnp.where(lane % 32 == place, power, power_ref[...])
            for seg in range(SEG):
                line = None
                for side in range(2):
                    for parity in range(2):
                        group = side * 2 + parity
                        part = parts[side, parity]
                        if group != seg:
                            part = pltpu.roll(part, (group - seg) * 32 % LANES, 1)
                        line = part if line is None else jnp.where(lane // 32 == group, part, line)
                line = line.astype(BF16)
                for half in range(HALVES):
                    block_ref[band, half, seg * FEW : (seg + 1) * FEW, :] = line[
                        half * FEW : (half + 1) * FEW
                    ]
    mine = pilot_ref[0] // CH == lax.axis_index("rgrp")
    guide_ref[...] = jnp.where(mine, jnp.sqrt(power_ref[...]), 0.0).astype(BF16)


def spectra_of(offsets, order, pilot, traces, table):
    vmem = pl.BlockSpec(memory_space=pltpu.VMEM)
    offsets, order, traces, table = (
        pltpu.with_memory_space_constraint(value, pltpu.HBM)
        for value in (offsets, order, traces, table)
    )
    return pl.pallas_call(
        spectra_kernel,
        in_specs=[pl.BlockSpec(memory_space=pl.ANY)] * 5,
        out_specs=[vmem, vmem],
        out_shape=[
            jax.ShapeDtypeStruct((BANDS, HALVES, SEG * FEW, LANES), BF16),
            jax.ShapeDtypeStruct((PAIRS, LANES), BF16),
        ],
        scratch_shapes=[
            pltpu.SMEM((SEG,), jnp.int32),
            pltpu.SMEM((1, CH), jnp.int32),
            pltpu.SMEM((1,), jnp.int32),
            pltpu.VMEM((CH, SPAN), BF16),
            pltpu.VMEM((PARTS, 2, 2 * PAIRS * BANDS // PARTS, QUARTER), BF16),
            pltpu.VMEM((2, 2 * LANES, QUARTER), F32),
            pltpu.VMEM((2, 2, QUARTER, 2 * LANES), BF16),
            pltpu.VMEM((PAIRS, LANES), F32),
            pltpu.SemaphoreType.DMA((4,)),
            pltpu.SemaphoreType.DMA((PARTS,)),
        ],
        compiler_params=pltpu.CompilerParams(vmem_limit_bytes=16 * 1024 * 1024),
        name="spectra",
    )(offsets, order, pilot, traces, table)


def total_kernel(guides_ref, guide_ref):
    guide = guides_ref[0].astype(F32)
    for line in range(1, 16):
        guide = guide + guides_ref[line].astype(F32)
    guide_ref[...] = guide


def total_of(guides):
    vmem = pl.BlockSpec(memory_space=pltpu.VMEM)
    return pl.pallas_call(
        total_kernel,
        in_specs=[vmem],
        out_specs=vmem,
        out_shape=jax.ShapeDtypeStruct((PAIRS, LANES), F32),
        compiler_params=pltpu.CompilerParams(vmem_limit_bytes=32 * 1024 * 1024),
        cost_estimate=pl.CostEstimate(flops=2**28, bytes_accessed=2**17, transcendentals=0),
        name="total",
    )(guides)


def whiten_kernel(guide_ref, own_ref, far_ref, white_ref, value_ref):
    guide = guide_ref[...]
    place = lane_index(PAIRS) // 2
    parity = lax.broadcasted_iota(jnp.int32, (LANES, LANES), 0) % 2
    spread = (parity == (lane_index(LANES) // 32) % 2).astype(F32).astype(BF16)
    blocks = (own_ref, far_ref)
    totals = [[jnp.zeros((FEW, LANES), F32) for _ in range(SEG)] for _ in blocks]
    for band in range(BANDS):
        picked = [jnp.where(place == seg * BANDS + band, guide, 0.0) for seg in range(SEG)]
        weight = jnp.dot(
            jnp.concatenate(picked, axis=0).astype(BF16), spread, preferred_element_type=F32
        )
        for seg in range(SEG):
            rows = slice(seg * FEW, (seg + 1) * FEW)
            for half in range(HALVES):
                at = seg * PAIRS + half * FEW
                part = weight[at : at + FEW]
                for k, block_ref in enumerate(blocks):
                    value = block_ref[band, half, rows, :].astype(F32) * part
                    value_ref[band * HALVES + half, k, rows, :] = value
                    totals[k][seg] = totals[k][seg] + value * value
    for k in range(len(blocks)):
        for seg in range(SEG):
            total = jnp.sum(totals[k][seg], axis=0, keepdims=True)
            total = jnp.broadcast_to(total, (8, LANES))
            total = total + pltpu.roll(total, 64, 1)
            total = total + pltpu.roll(total, 32, 1)
            level = (total * (0.1 / (64.0 * BANDS)) + 1e-06)[:1]
            rows = slice(seg * FEW, (seg + 1) * FEW)
            for place in range(BANDS * HALVES):
                value = value_ref[place, k, rows, :]
                energy = value * value
                energy = energy + pltpu.roll(energy, 64, 1)
                white_ref[place, k, rows, :] = (value * lax.rsqrt(energy + level)).astype(BF16)


def whitened_of(guides, own, far):
    vmem = pl.BlockSpec(memory_space=pltpu.VMEM)
    shape = (BANDS * HALVES, 2, ROWS, LANES)
    return pl.pallas_call(
        whiten_kernel,
        in_specs=[vmem] * 3,
        out_specs=vmem,
        out_shape=jax.ShapeDtypeStruct(shape, BF16),
        scratch_shapes=[pltpu.VMEM(shape, F32)],
        compiler_params=pltpu.CompilerParams(vmem_limit_bytes=32 * 1024 * 1024),
        name="whiten",
    )(guides, own, far)


def gather_rows(parts_ref, block_ref, wide_ref):
    for window in range(BANDS):
        for which in range(4):
            at = window * PITCH + which * ROWS
            part = parts_ref[window * HALVES + which // 2, which % 2]
            wide_ref[at : at + ROWS, :] = part.astype(F32)
    for pair in range(FEW):
        for which in range(4):
            rows = [
                wide_ref[pl.ds(which * ROWS + seg * FEW + pair, BANDS, stride=PITCH), :]
                for seg in range(SEG)
            ]
            block_ref[pair, which] = jnp.concatenate(rows, axis=0).astype(BF16)


def cross_rows(left_side, block_ref, out_ref, near_ref, far_ref):
    sign = jnp.where(lane_index(BANDS * SEG) < 64, 1.0, -1.0)
    for pair in range(FEW):
        turned = jnp.transpose(block_ref[pair, 2 * left_side].astype(F32))
        left = jnp.concatenate([turned[:64], turned[64:]], axis=1).astype(BF16)
        for which, stack_ref in ((3 * (1 - left_side), near_ref), (2 * left_side + 1, far_ref)):
            right = block_ref[pair, which].astype(F32)
            mix = jnp.concatenate([right * sign, pltpu.roll(right, 64, 1)], axis=0).astype(BF16)
            product = jnp.dot(left, mix, preferred_element_type=F32)
            stack_ref[pair * 2 * CH : (pair + 1) * 2 * CH, :] = product

    lane = lane_index(CH)
    even = lane % 2 == 0
    for first in range(0, CH, 4):
        pieces = {}
        for back, stack_ref in enumerate((near_ref, far_ref)):
            rows = [stack_ref[pl.ds(first + k, 2 * FEW, stride=CH), :] for k in range(4)]
            turned = jnp.transpose(jnp.concatenate(rows, axis=0)) * 0.125
            pieces[back] = jnp.where(even, turned[:32], turned[32:64])
            pieces[2 + back] = jnp.where(even, turned[64:96], turned[96:])
        for k in range(4):
            line = None
            for group in range(4):
                part = pieces[group]
                if group != k:
                    part = pltpu.roll(part, (group - k) * 32 % LANES, 1)
                line = part if line is None else jnp.where(lane // 32 == group, part, line)
            out_ref[first + k] = line.astype(BF16)


def other_kernel(parts_ref, out_ref, block_ref, wide_ref, near_ref, far_ref):
    gather_rows(parts_ref, block_ref, wide_ref)
    cross_rows(1 - lax.axis_index("rgrp") % 2, block_ref, out_ref, near_ref, far_ref)


def mine_kernel(block_ref, out_ref, near_ref, far_ref):
    cross_rows(lax.axis_index("rgrp") % 2, block_ref, out_ref, near_ref, far_ref)


STACK = pltpu.VMEM((2 * FEW * CH, LANES), F32)
CROSS = jax.ShapeDtypeStruct((CH, CH, LANES), BF16)


def other_of(parts):
    vmem = pl.BlockSpec(memory_space=pltpu.VMEM)
    return pl.pallas_call(
        other_kernel,
        in_specs=[vmem],
        out_specs=[vmem, vmem],
        out_shape=[CROSS, jax.ShapeDtypeStruct((FEW, 4, BANDS * SEG, LANES), BF16)],
        scratch_shapes=[pltpu.VMEM((BANDS * PITCH, LANES), F32), STACK, STACK],
        compiler_params=pltpu.CompilerParams(vmem_limit_bytes=32 * 1024 * 1024),
        name="cross_other",
    )(parts)


def mine_of(blocks):
    vmem = pl.BlockSpec(memory_space=pltpu.VMEM)
    return pl.pallas_call(
        mine_kernel,
        in_specs=[vmem],
        out_specs=vmem,
        out_shape=CROSS,
        scratch_shapes=[STACK, STACK],
        compiler_params=pltpu.CompilerParams(vmem_limit_bytes=32 * 1024 * 1024),
        cost_estimate=pl.CostEstimate(flops=2**28, bytes_accessed=2**23, transcendentals=0),
        name="cross_mine",
    )(blocks)


def merge_kernel(own_ref, other_ref, out_ref):
    first = lax.axis_index("rgrp") % 2 == 0
    even = (lane_index(CH) // 32) % 2 == 0

    def channel(i, carry):
        own = own_ref[i].astype(F32)
        other = other_ref[i].astype(F32)
        low = jnp.where(first, own, other)
        high = jnp.where(first, other, own)
        out_ref[0, i] = jnp.where(even, low, pltpu.roll(high, 32, 1)).astype(BF16)
        out_ref[1, i] = jnp.where(even, pltpu.roll(low, 96, 1), high).astype(BF16)
        return carry

    lax.fori_loop(0, CH, channel, 0, unroll=CH)


def merged_of(own, other):
    vmem = pl.BlockSpec(memory_space=pltpu.VMEM)
    return pl.pallas_call(
        merge_kernel,
        in_specs=[vmem] * 2,
        out_specs=vmem,
        out_shape=jax.ShapeDtypeStruct((2, CH, CH, LANES), BF16),
        compiler_params=pltpu.CompilerParams(vmem_limit_bytes=32 * 1024 * 1024),
        name="merge",
    )(own, other)


def beside(value):
    return lax.ppermute(value, "rgrp", [(g, g ^ 1) for g in range(32)])


def local(table, traces, segment_offsets, channel_order, pilot_channel):
    own, guide = spectra_of(segment_offsets, channel_order, pilot_channel, traces, table)
    far = lax.ppermute(own, "rgrp", [(g, (g + 2) % 32) for g in range(32)])
    guide = guide + beside(guide)
    lines = [[2 * z + side for z in range(16)] for side in range(2)]
    guides = lax.all_to_all(
        jnp.broadcast_to(guide, (16, PAIRS, LANES)),
        "rgrp",
        split_axis=0,
        concat_axis=0,
        tiled=True,
        axis_index_groups=lines,
    )
    white = whitened_of(total_of(guides), own, far)
    planes = [[32 * f + 2 * z + side for f in range(BANDS) for side in range(2)] for z in range(16)]
    parts = lax.all_to_all(
        white, ("freq", "rgrp"), split_axis=0, concat_axis=0, tiled=True, axis_index_groups=planes
    )
    other, blocks = other_of(parts)
    other = beside(other)
    return merged_of(mine_of(blocks), other)


def solution(mesh):
    table = quarter_table()
    specs = (P(), P("rgrp", "freq"), P("freq"), P("rgrp", None), P())
    inner = jax.shard_map(
        local, mesh=mesh, in_specs=specs, out_specs=P(None, "rgrp", None, "freq"), check_vma=False
    )

    def run(traces, segment_offsets, channel_order, pilot_channel):
        return inner(jnp.asarray(table), traces, segment_offsets, channel_order, pilot_channel)

    return run
```

```python
import functools
import math

import jax
import jax.numpy as jnp
import ml_dtypes
import numpy as np
from jax import lax
from jax.experimental import pallas as pl
from jax.experimental.pallas import tpu as pltpu
from jax.sharding import PartitionSpec as P

L = 2048
QUARTER = 512
PARTS = 1
BANDS = 16
SEG = 4
CH = 32
PAIRS = 32
SPAN = 9216
HALVES = 2
FEW = 16
ROWS = SEG * FEW
PITCH = 4 * ROWS + 8
LANES = 128
BF16 = jnp.bfloat16
F32 = jnp.float32


def quarter_table():
    part, parity, band, pair = np.ogrid[:PARTS, :2, : BANDS // PARTS, :PAIRS]
    which_bin = 64 * (part * (BANDS // PARTS) + band) + 2 * pair + parity + 1
    sample = np.arange(QUARTER)
    residue = (which_bin[..., None] * sample) % L
    phase_angle = residue.astype(np.float32) * np.float32(2.0 * math.pi / L)
    factor = np.float32(1.0 / math.sqrt(L))
    both = np.stack([np.cos(phase_angle) * factor, np.sin(phase_angle) * factor], axis=3)
    return both.reshape(PARTS, 2, -1, QUARTER).astype(ml_dtypes.bfloat16)


def lane_index(rows):
    return lax.broadcasted_iota(jnp.int32, (rows, LANES), 1)


def cut_windows(offset_ref, order_ref, traces_ref, wide_ref, wave_ref):
    lane = lane_index(CH)
    row = lax.broadcasted_iota(jnp.int32, (CH, CH), 0)
    picked = jnp.zeros((CH, CH), jnp.int32)
    for channel in range(CH):
        picked = jnp.where(row == channel, order_ref[0, channel], picked)
    chosen = (lax.broadcasted_iota(jnp.int32, (CH, CH), 1) == picked).astype(F32).astype(BF16)
    tiles = L // LANES
    for seg in range(SEG):
        start = seg * L + offset_ref[seg]
        base = jnp.minimum((start // LANES) * LANES, SPAN - (L + LANES))
        base = pl.multiple_of(base, LANES)
        rest = start - base
        turn = lax.rem(LANES - rest, LANES)
        rolled = []
        for tile in range(tiles + 1):
            part = traces_ref[:, pl.ds(pl.multiple_of(base + tile * LANES, LANES), LANES)]
            rolled.append(pltpu.roll(part.astype(F32), turn, 1))
        window = [
            jnp.where(lane < LANES - rest, rolled[tile], rolled[tile + 1]) for tile in range(tiles)
        ]
        ordered = jnp.dot(
            chosen, jnp.concatenate(window, axis=1).astype(BF16), preferred_element_type=F32
        )
        first, second, third, fourth = (
            ordered[:, k * QUARTER : (k + 1) * QUARTER] for k in range(4)
        )
        even, odd = first + third, second + fourth
        for k, mix in enumerate((first - third, second - fourth, even - odd, even + odd)):
            at = (k % 2) * LANES + seg * CH
            wide_ref[k // 2, at : at + CH, :] = mix
    for parity in range(2):
        mix = jnp.transpose(wide_ref[parity])
        high = mix.astype(BF16)
        wave_ref[parity, 0] = high
        wave_ref[parity, 1] = (mix - high.astype(F32)).astype(BF16)


def spectra_kernel(
    offset_hbm, order_hbm, pilot_hbm, traces_hbm, table_hbm, block_ref, guide_ref,
    offset_ref, order_ref, pilot_ref, traces_ref, table_ref, wide_ref, wave_ref,
    power_ref, sems, table_sems,
):
    small = [
        pltpu.make_async_copy(source, target, sems.at[k])
        for k, (source, target) in enumerate(
            (
                (traces_hbm, traces_ref),
                (offset_hbm, offset_ref),
                (order_hbm, order_ref),
                (pilot_hbm, pilot_ref),
            )
        )
    ]
    for copy in small:
        copy.start()
    table = [
        pltpu.make_async_copy(table_hbm.at[part], table_ref.at[part], table_sems.at[part])
        for part in range(PARTS)
    ]
    for copy in table:
        copy.start()
    power_ref[...] = jnp.zeros_like(power_ref)
    for copy in small:
        copy.wait()
    cut_windows(offset_ref, order_ref, traces_ref, wide_ref, wave_ref)

    lane = lane_index(PAIRS)
    channel = lax.rem(pilot_ref[0], CH)
    odd_pair = lax.broadcasted_iota(jnp.int32, (PAIRS, LANES), 0) % 2 == 1
    flip = jnp.where(odd_pair, -1.0, 1.0)
    for slab in range(PARTS):
        table[slab].wait()
        products = [
            jnp.dot(table_ref[slab, parity], wave_ref[parity, 0], preferred_element_type=F32)
            + jnp.dot(table_ref[slab, parity], wave_ref[parity, 1], preferred_element_type=F32)
            for parity in range(2)
        ]
        for local_band in range(BANDS // PARTS):
            band = slab * (BANDS // PARTS) + local_band
            at = 2 * PAIRS * local_band
            parts = {}
            cosine = products[0][at : at + PAIRS]
            sine = products[0][at + PAIRS : at + 2 * PAIRS]
            parts[0, 0] = cosine[:, :LANES] - flip * sine[:, LANES:]
            parts[1, 0] = -sine[:, :LANES] - flip * cosine[:, LANES:]
            cosine = products[1][at : at + PAIRS]
            sine = products[1][at + PAIRS : at + 2 * PAIRS]
            parts[0, 1] = jnp.where(odd_pair, cosine[:, LANES:], cosine[:, :LANES])
            parts[1, 1] = -jnp.where(odd_pair, sine[:, LANES:], sine[:, :LANES])
            for parity in range(2):
                real = parts[0, parity].astype(BF16).astype(F32)
                imag = parts[1, parity].astype(BF16).astype(F32)
                place = 2 * band + parity
                power = pltpu.roll(
                    real * real + imag * imag, lax.rem(place - channel + LANES, LANES), 1
                )
                power_ref[...] = jnp.where(lane % 32 == place, power, power_ref[...])
            for seg in range(SEG):
                line = None
                for side in range(2):
                    for parity in range(2):
                        group = side * 2 + parity
                        part = parts[side, parity]
                        if group != seg:
                            part = pltpu.roll(part, (group - seg) * 32 % LANES, 1)
                        line = part if line is None else jnp.where(lane // 32 == group, part, line)
                line = line.astype(BF16)
                for half in range(HALVES):
                    block_ref[band, half, seg * FEW : (seg + 1) * FEW, :] = line[
                        half * FEW : (half + 1) * FEW
                    ]
    mine = pilot_ref[0] // CH == lax.axis_index("rgrp")
    guide_ref[...] = jnp.where(mine, jnp.sqrt(power_ref[...]), 0.0).astype(BF16)


def spectra_of(offsets, order, pilot, traces, table):
    vmem = pl.BlockSpec(memory_space=pltpu.VMEM)
    offsets, order, traces, table = (
        pltpu.with_memory_space_constraint(value, pltpu.HBM)
        for value in (offsets, order, traces, table)
    )
    return pl.pallas_call(
        spectra_kernel,
        in_specs=[pl.BlockSpec(memory_space=pl.ANY)] * 5,
        out_specs=[vmem, vmem],
        out_shape=[
            jax.ShapeDtypeStruct((BANDS, HALVES, SEG * FEW, LANES), BF16),
            jax.ShapeDtypeStruct((PAIRS, LANES), BF16),
        ],
        scratch_shapes=[
            pltpu.SMEM((SEG,), jnp.int32),
            pltpu.SMEM((1, CH), jnp.int32),
            pltpu.SMEM((1,), jnp.int32),
            pltpu.VMEM((CH, SPAN), BF16),
            pltpu.VMEM((PARTS, 2, 2 * PAIRS * BANDS // PARTS, QUARTER), BF16),
            pltpu.VMEM((2, 2 * LANES, QUARTER), F32),
            pltpu.VMEM((2, 2, QUARTER, 2 * LANES), BF16),
            pltpu.VMEM((PAIRS, LANES), F32),
            pltpu.SemaphoreType.DMA((4,)),
            pltpu.SemaphoreType.DMA((PARTS,)),
        ],
        compiler_params=pltpu.CompilerParams(vmem_limit_bytes=16 * 1024 * 1024),
        name="spectra",
    )(offsets, order, pilot, traces, table)


def total_kernel(guides_ref, guide_ref):
    guide = guides_ref[0].astype(F32)
    for line in range(1, 16):
        guide = guide + guides_ref[line].astype(F32)
    guide_ref[...] = guide


def total_of(guides):
    vmem = pl.BlockSpec(memory_space=pltpu.VMEM)
    return pl.pallas_call(
        total_kernel,
        in_specs=[vmem],
        out_specs=vmem,
        out_shape=jax.ShapeDtypeStruct((PAIRS, LANES), F32),
        compiler_params=pltpu.CompilerParams(vmem_limit_bytes=32 * 1024 * 1024),
        cost_estimate=pl.CostEstimate(flops=2**28, bytes_accessed=2**17, transcendentals=0),
        name="total",
    )(guides)


def whiten_kernel(guide_ref, own_ref, far_ref, white_ref, value_ref):
    guide = guide_ref[...]
    place = lane_index(PAIRS) // 2
    parity = lax.broadcasted_iota(jnp.int32, (LANES, LANES), 0) % 2
    spread = (parity == (lane_index(LANES) // 32) % 2).astype(F32).astype(BF16)
    blocks = (own_ref, far_ref)
    totals = [[jnp.zeros((FEW, LANES), F32) for _ in range(SEG)] for _ in blocks]
    for band in range(BANDS):
        picked = [jnp.where(place == seg * BANDS + band, guide, 0.0) for seg in range(SEG)]
        weight = jnp.dot(
            jnp.concatenate(picked, axis=0).astype(BF16), spread, preferred_element_type=F32
        )
        for seg in range(SEG):
            rows = slice(seg * FEW, (seg + 1) * FEW)
            for half in range(HALVES):
                at = seg * PAIRS + half * FEW
                part = weight[at : at + FEW]
                for k, block_ref in enumerate(blocks):
                    value = block_ref[band, half, rows, :].astype(F32) * part
                    value_ref[band * HALVES + half, k, rows, :] = value
                    totals[k][seg] = totals[k][seg] + value * value
    for k in range(len(blocks)):
        for seg in range(SEG):
            total = jnp.sum(totals[k][seg], axis=0, keepdims=True)
            total = jnp.broadcast_to(total, (8, LANES))
            total = total + pltpu.roll(total, 64, 1)
            total = total + pltpu.roll(total, 32, 1)
            level = (total * (0.1 / (64.0 * BANDS)) + 1e-06)[:1]
            rows = slice(seg * FEW, (seg + 1) * FEW)
            for place in range(BANDS * HALVES):
                value = value_ref[place, k, rows, :]
                energy = value * value
                energy = energy + pltpu.roll(energy, 64, 1)
                white_ref[place, k, rows, :] = (value * lax.rsqrt(energy + level)).astype(BF16)


def whitened_of(guides, own, far):
    vmem = pl.BlockSpec(memory_space=pltpu.VMEM)
    shape = (BANDS * HALVES, 2, ROWS, LANES)
    return pl.pallas_call(
        whiten_kernel,
        in_specs=[vmem] * 3,
        out_specs=vmem,
        out_shape=jax.ShapeDtypeStruct(shape, BF16),
        scratch_shapes=[pltpu.VMEM(shape, F32)],
        compiler_params=pltpu.CompilerParams(vmem_limit_bytes=32 * 1024 * 1024),
        name="whiten",
    )(guides, own, far)


def spread_rows(parts_ref, wide_ref):
    for window in range(BANDS):
        for which in range(4):
            at = window * PITCH + which * ROWS
            part = parts_ref[window * HALVES + which // 2, which % 2]
            wide_ref[at : at + ROWS, :] = part.astype(F32)


def gathered_row(pair, which, wide_ref):
    rows = [
        wide_ref[pl.ds(which * ROWS + seg * FEW + pair, BANDS, stride=PITCH), :]
        for seg in range(SEG)
    ]
    return jnp.concatenate(rows, axis=0)


def stack_pair(pair, left, rights, stack_refs):
    sign = jnp.where(lane_index(BANDS * SEG) < 64, 1.0, -1.0)
    turned = jnp.transpose(left)
    left = jnp.concatenate([turned[:64], turned[64:]], axis=1).astype(BF16)
    for right, stack_ref in zip(rights, stack_refs):
        mix = jnp.concatenate([right * sign, pltpu.roll(right, 64, 1)], axis=0).astype(BF16)
        product = jnp.dot(left, mix, preferred_element_type=F32)
        stack_ref[pair * 2 * CH : (pair + 1) * 2 * CH, :] = product


def unstack(out_ref, stack_refs):
    lane = lane_index(CH)
    even = lane % 2 == 0
    for first in range(0, CH, 4):
        pieces = {}
        for back, stack_ref in enumerate(stack_refs):
            rows = [stack_ref[pl.ds(first + k, 2 * FEW, stride=CH), :] for k in range(4)]
            turned = jnp.transpose(jnp.concatenate(rows, axis=0)) * 0.125
            pieces[back] = jnp.where(even, turned[:32], turned[32:64])
            pieces[2 + back] = jnp.where(even, turned[64:96], turned[96:])
        for k in range(4):
            line = None
            for group in range(4):
                part = pieces[group]
                if group != k:
                    part = pltpu.roll(part, (group - k) * 32 % LANES, 1)
                line = part if line is None else jnp.where(lane // 32 == group, part, line)
            out_ref[first + k] = line.astype(BF16)


def other_kernel(parts_ref, out_ref, block_ref, wide_ref, near_ref, far_ref):
    spread_rows(parts_ref, wide_ref)
    first = lax.axis_index("rgrp") % 2 == 0
    for pair in range(FEW):
        a, a_far, b, b_far = (gathered_row(pair, which, wide_ref) for which in range(4))
        left, near, far = (
            jnp.where(first, b, a), jnp.where(first, a, b_far), jnp.where(first, b_far, a_far)
        )
        stack_pair(pair, left, (near, far), (near_ref, far_ref))
        block_ref[pair, 0] = jnp.where(first, a, b).astype(BF16)
        block_ref[pair, 1] = jnp.where(first, b_far, a).astype(BF16)
        block_ref[pair, 2] = jnp.where(first, a_far, b_far).astype(BF16)
    unstack(out_ref, (near_ref, far_ref))


def mine_kernel(block_ref, out_ref, near_ref, far_ref):
    for pair in range(FEW):
        left, near, far = (block_ref[pair, k].astype(F32) for k in range(3))
        stack_pair(pair, left, (near, far), (near_ref, far_ref))
    unstack(out_ref, (near_ref, far_ref))


STACK = pltpu.VMEM((2 * FEW * CH, LANES), F32)
CROSS = jax.ShapeDtypeStruct((CH, CH, LANES), BF16)


def other_of(parts):
    vmem = pl.BlockSpec(memory_space=pltpu.VMEM)
    return pl.pallas_call(
        other_kernel,
        in_specs=[vmem],
        out_specs=[vmem, vmem],
        out_shape=[CROSS, jax.ShapeDtypeStruct((FEW, 3, BANDS * SEG, LANES), BF16)],
        scratch_shapes=[pltpu.VMEM((BANDS * PITCH, LANES), F32), STACK, STACK],
        compiler_params=pltpu.CompilerParams(vmem_limit_bytes=32 * 1024 * 1024),
        name="cross_other",
    )(parts)


def mine_of(blocks):
    vmem = pl.BlockSpec(memory_space=pltpu.VMEM)
    return pl.pallas_call(
        mine_kernel,
        in_specs=[vmem],
        out_specs=vmem,
        out_shape=CROSS,
        scratch_shapes=[STACK, STACK],
        compiler_params=pltpu.CompilerParams(vmem_limit_bytes=32 * 1024 * 1024),
        cost_estimate=pl.CostEstimate(flops=2**28, bytes_accessed=2**23, transcendentals=0),
        name="cross_mine",
    )(blocks)


def merge_kernel(own_ref, other_ref, out_ref):
    first = lax.axis_index("rgrp") % 2 == 0
    even = (lane_index(CH) // 32) % 2 == 0

    def channel(i, carry):
        own = own_ref[i].astype(F32)
        other = other_ref[i].astype(F32)
        low = jnp.where(first, own, other)
        high = jnp.where(first, other, own)
        out_ref[0, i] = jnp.where(even, low, pltpu.roll(high, 32, 1)).astype(BF16)
        out_ref[1, i] = jnp.where(even, pltpu.roll(low, 96, 1), high).astype(BF16)
        return carry

    lax.fori_loop(0, CH, channel, 0, unroll=CH)


def merged_of(own, other):
    vmem = pl.BlockSpec(memory_space=pltpu.VMEM)
    return pl.pallas_call(
        merge_kernel,
        in_specs=[vmem] * 2,
        out_specs=vmem,
        out_shape=jax.ShapeDtypeStruct((2, CH, CH, LANES), BF16),
        compiler_params=pltpu.CompilerParams(vmem_limit_bytes=32 * 1024 * 1024),
        name="merge",
    )(own, other)


def beside(value):
    return lax.ppermute(value, "rgrp", [(g, g ^ 1) for g in range(32)])


def local(table, traces, segment_offsets, channel_order, pilot_channel):
    own, guide = spectra_of(segment_offsets, channel_order, pilot_channel, traces, table)
    far = lax.ppermute(own, "rgrp", [(g, (g + 2) % 32) for g in range(32)])
    guide = guide + beside(guide)
    lines = [[2 * z + side for z in range(16)] for side in range(2)]
    guides = lax.all_to_all(
        jnp.broadcast_to(guide, (16, PAIRS, LANES)),
        "rgrp",
        split_axis=0,
        concat_axis=0,
        tiled=True,
        axis_index_groups=lines,
    )
    white = whitened_of(total_of(guides), own, far)
    planes = [[32 * f + 2 * z + side for f in range(BANDS) for side in range(2)] for z in range(16)]
    parts = lax.all_to_all(
        white, ("freq", "rgrp"), split_axis=0, concat_axis=0, tiled=True, axis_index_groups=planes
    )
    other, blocks = other_of(parts)
    other = beside(other)
    return merged_of(mine_of(blocks), other)


def solution(mesh):
    table = quarter_table()
    specs = (P(), P("rgrp", "freq"), P("freq"), P("rgrp", None), P())
    inner = jax.shard_map(
        local, mesh=mesh, in_specs=specs, out_specs=P(None, "rgrp", None, "freq"), check_vma=False
    )

    def run(traces, segment_offsets, channel_order, pilot_channel):
        return inner(jnp.asarray(table), traces, segment_offsets, channel_order, pilot_channel)

    return run
```

```python
import functools
import math

import jax
import jax.numpy as jnp
import ml_dtypes
import numpy as np
from jax import lax
from jax.experimental import pallas as pl
from jax.experimental.pallas import tpu as pltpu
from jax.sharding import PartitionSpec as P

L = 2048
QUARTER = 512
BANDS = 16
SEG = 4
CH = 32
PAIRS = 32
SPAN = 9216
HALVES = 2
FEW = 16
ROWS = SEG * FEW
PITCH = 4 * ROWS + 8
LANES = 128
BF16 = jnp.bfloat16
F32 = jnp.float32


def quarter_table():
    place = np.arange(PAIRS)
    pair = 16 * (place // 16) + 2 * (place % 8) + place // 8 % 2
    band = 64 * np.arange(BANDS)[:, None]
    bins = np.stack([band + 2 * pair + 1, band + 2 * pair + 2])
    residue = (bins[..., None] * np.arange(QUARTER)) % L
    phase_angle = residue.astype(np.float32) * np.float32(2.0 * math.pi / L)
    factor = np.float32(1.0 / math.sqrt(L))
    odd, even = np.stack([np.cos(phase_angle) * factor, np.sin(phase_angle) * factor], axis=2)
    even = even.reshape(BANDS, 2, 2, 2, 8, QUARTER).transpose(3, 0, 1, 2, 4, 5)
    rows = [part.reshape(-1, QUARTER) for part in (odd, even)]
    return np.stack(rows).astype(ml_dtypes.bfloat16)


def lane_index(rows):
    return lax.broadcasted_iota(jnp.int32, (rows, LANES), 1)


def cut_windows(offset_ref, order_ref, traces_ref, wide_ref, wave_ref):
    lane = lane_index(CH)
    row = lax.broadcasted_iota(jnp.int32, (CH, CH), 0)
    picked = jnp.zeros((CH, CH), jnp.int32)
    for channel in range(CH):
        picked = jnp.where(row == channel, order_ref[0, channel], picked)
    chosen = (lax.broadcasted_iota(jnp.int32, (CH, CH), 1) == picked).astype(F32).astype(BF16)
    tiles = L // LANES
    for seg in range(SEG):
        start = seg * L + offset_ref[seg]
        base = jnp.minimum((start // LANES) * LANES, SPAN - (L + LANES))
        base = pl.multiple_of(base, LANES)
        rest = start - base
        turn = lax.rem(LANES - rest, LANES)
        rolled = []
        for tile in range(tiles + 1):
            part = traces_ref[:, pl.ds(pl.multiple_of(base + tile * LANES, LANES), LANES)]
            rolled.append(pltpu.roll(part.astype(F32), turn, 1))
        window = [
            jnp.where(lane < LANES - rest, rolled[tile], rolled[tile + 1]) for tile in range(tiles)
        ]
        ordered = jnp.dot(
            chosen, jnp.concatenate(window, axis=1).astype(BF16), preferred_element_type=F32
        )
        first, second, third, fourth = (
            ordered[:, k * QUARTER : (k + 1) * QUARTER] for k in range(4)
        )
        even, odd = first + third, second + fourth
        for k, mix in enumerate((first - third, second - fourth, even - odd, even + odd)):
            at = (k % 2) * LANES + seg * CH
            wide_ref[k // 2, at : at + CH, :] = mix
    for parity in range(2):
        mix = jnp.transpose(wide_ref[parity])
        high = mix.astype(BF16)
        low = (mix - high.astype(F32)).astype(BF16)
        if parity == 0:
            wave_ref[0, 0] = high
            wave_ref[0, 1] = low
        else:
            for k in range(2):
                lanes = slice(k * LANES, (k + 1) * LANES)
                wave_ref[1, k] = jnp.concatenate([high[:, lanes], low[:, lanes]], axis=1)


def spectra_kernel(
    offset_hbm, order_hbm, pilot_hbm, traces_hbm, table_hbm, block_ref, guide_ref,
    offset_ref, order_ref, pilot_ref, traces_ref, table_ref, wide_ref, wave_ref,
    power_ref, sems,
):
    small = [
        pltpu.make_async_copy(source, target, sems.at[k])
        for k, (source, target) in enumerate(
            (
                (traces_hbm, traces_ref),
                (offset_hbm, offset_ref),
                (order_hbm, order_ref),
                (pilot_hbm, pilot_ref),
            )
        )
    ]
    for copy in small:
        copy.start()
    table = pltpu.make_async_copy(table_hbm, table_ref, sems.at[len(small)])
    table.start()
    power_ref[...] = jnp.zeros_like(power_ref)
    for copy in small:
        copy.wait()
    cut_windows(offset_ref, order_ref, traces_ref, wide_ref, wave_ref)

    lane = lane_index(PAIRS)
    channel = lax.rem(pilot_ref[0], CH)
    odd_pair = lax.broadcasted_iota(jnp.int32, (PAIRS, LANES), 0) // 8 % 2 == 1
    flip = jnp.where(odd_pair, -1.0, 1.0)
    table.wait()
    odd = jnp.dot(table_ref[0], wave_ref[0, 0], preferred_element_type=F32)
    odd = odd + jnp.dot(table_ref[0], wave_ref[0, 1], preferred_element_type=F32)
    even = []
    for k in range(2):
        rows = pl.ds(k * BANDS * PAIRS, BANDS * PAIRS)
        product = jnp.dot(table_ref[1, rows], wave_ref[1, k], preferred_element_type=F32)
        even.append(product[:, :LANES] + product[:, LANES:])
    for band in range(BANDS):
        at = 2 * PAIRS * band
        cosine, sine = odd[at : at + PAIRS], odd[at + PAIRS : at + 2 * PAIRS]
        parts = {
            (0, 0): cosine[:, :LANES] - flip * sine[:, LANES:],
            (1, 0): -sine[:, :LANES] - flip * cosine[:, LANES:],
        }
        for side in range(2):
            at = PAIRS * band + FEW * side
            rows = [even[k][at + 8 * half : at + 8 * half + 8] for half in range(2) for k in range(2)]
            parts[side, 1] = jnp.concatenate(rows, axis=0) * (1.0, -1.0)[side]
        for parity in range(2):
            real = parts[0, parity].astype(BF16).astype(F32)
            imag = parts[1, parity].astype(BF16).astype(F32)
            place = 2 * band + parity
            power = pltpu.roll(
                real * real + imag * imag, lax.rem(place - channel + LANES, LANES), 1
            )
            power_ref[...] = jnp.where(lane % 32 == place, power, power_ref[...])
        for seg in range(SEG):
            line = None
            for side in range(2):
                for parity in range(2):
                    group = side * 2 + parity
                    part = parts[side, parity]
                    if group != seg:
                        part = pltpu.roll(part, (group - seg) * 32 % LANES, 1)
                    line = part if line is None else jnp.where(lane // 32 == group, part, line)
            line = line.astype(BF16)
            for half in range(HALVES):
                block_ref[band, half, seg * FEW : (seg + 1) * FEW, :] = line[
                    half * FEW : (half + 1) * FEW
                ]
    mine = pilot_ref[0] // CH == lax.axis_index("rgrp")
    guide_ref[...] = jnp.where(mine, jnp.sqrt(power_ref[...]), 0.0).astype(BF16)


def spectra_of(offsets, order, pilot, traces, table):
    vmem = pl.BlockSpec(memory_space=pltpu.VMEM)
    offsets, order, traces, table = (
        pltpu.with_memory_space_constraint(value, pltpu.HBM)
        for value in (offsets, order, traces, table)
    )
    return pl.pallas_call(
        spectra_kernel,
        in_specs=[pl.BlockSpec(memory_space=pl.ANY)] * 5,
        out_specs=[vmem, vmem],
        out_shape=[
            jax.ShapeDtypeStruct((BANDS, HALVES, SEG * FEW, LANES), BF16),
            jax.ShapeDtypeStruct((PAIRS, LANES), BF16),
        ],
        scratch_shapes=[
            pltpu.SMEM((SEG,), jnp.int32),
            pltpu.SMEM((1, CH), jnp.int32),
            pltpu.SMEM((1,), jnp.int32),
            pltpu.VMEM((CH, SPAN), BF16),
            pltpu.VMEM((2, 2 * PAIRS * BANDS, QUARTER), BF16),
            pltpu.VMEM((2, 2 * LANES, QUARTER), F32),
            pltpu.VMEM((2, 2, QUARTER, 2 * LANES), BF16),
            pltpu.VMEM((PAIRS, LANES), F32),
            pltpu.SemaphoreType.DMA((5,)),
        ],
        compiler_params=pltpu.CompilerParams(vmem_limit_bytes=16 * 1024 * 1024),
        name="spectra",
    )(offsets, order, pilot, traces, table)


def total_kernel(guides_ref, guide_ref):
    guide = guides_ref[0].astype(F32)
    for line in range(1, 16):
        guide = guide + guides_ref[line].astype(F32)
    guide_ref[...] = guide


def total_of(guides):
    vmem = pl.BlockSpec(memory_space=pltpu.VMEM)
    return pl.pallas_call(
        total_kernel,
        in_specs=[vmem],
        out_specs=vmem,
        out_shape=jax.ShapeDtypeStruct((PAIRS, LANES), F32),
        compiler_params=pltpu.CompilerParams(vmem_limit_bytes=32 * 1024 * 1024),
        cost_estimate=pl.CostEstimate(flops=2**28, bytes_accessed=2**17, transcendentals=0),
        name="total",
    )(guides)


def whiten_kernel(guide_ref, own_ref, far_ref, white_ref, value_ref):
    guide = guide_ref[...]
    place = lane_index(PAIRS) // 2
    parity = lax.broadcasted_iota(jnp.int32, (LANES, LANES), 0) % 2
    spread = (parity == (lane_index(LANES) // 32) % 2).astype(F32).astype(BF16)
    blocks = (own_ref, far_ref)
    totals = [[jnp.zeros((FEW, LANES), F32) for _ in range(SEG)] for _ in blocks]
    for band in range(BANDS):
        picked = [jnp.where(place == seg * BANDS + band, guide, 0.0) for seg in range(SEG)]
        weight = jnp.dot(
            jnp.concatenate(picked, axis=0).astype(BF16), spread, preferred_element_type=F32
        )
        for seg in range(SEG):
            rows = slice(seg * FEW, (seg + 1) * FEW)
            for half in range(HALVES):
                at = seg * PAIRS + half * FEW
                part = weight[at : at + FEW]
                for k, block_ref in enumerate(blocks):
                    value = block_ref[band, half, rows, :].astype(F32) * part
                    value_ref[band * HALVES + half, k, rows, :] = value
                    totals[k][seg] = totals[k][seg] + value * value
    for k in range(len(blocks)):
        for seg in range(SEG):
            total = jnp.sum(totals[k][seg], axis=0, keepdims=True)
            total = jnp.broadcast_to(total, (8, LANES))
            total = total + pltpu.roll(total, 64, 1)
            total = total + pltpu.roll(total, 32, 1)
            level = (total * (0.1 / (64.0 * BANDS)) + 1e-06)[:1]
            rows = slice(seg * FEW, (seg + 1) * FEW)
            for place in range(BANDS * HALVES):
                value = value_ref[place, k, rows, :]
                energy = value * value
                energy = energy + pltpu.roll(energy, 64, 1)
                white_ref[place, k, rows, :] = (value * lax.rsqrt(energy + level)).astype(BF16)


def whitened_of(guides, own, far):
    vmem = pl.BlockSpec(memory_space=pltpu.VMEM)
    shape = (BANDS * HALVES, 2, ROWS, LANES)
    return pl.pallas_call(
        whiten_kernel,
        in_specs=[vmem] * 3,
        out_specs=vmem,
        out_shape=jax.ShapeDtypeStruct(shape, BF16),
        scratch_shapes=[pltpu.VMEM(shape, F32)],
        compiler_params=pltpu.CompilerParams(vmem_limit_bytes=32 * 1024 * 1024),
        name="whiten",
    )(guides, own, far)


def spread_rows(parts_ref, wide_ref):
    for window in range(BANDS):
        for which in range(4):
            at = window * PITCH + which * ROWS
            part = parts_ref[window * HALVES + which // 2, which % 2]
            wide_ref[at : at + ROWS, :] = part.astype(F32)


def gathered_row(pair, which, wide_ref):
    rows = [
        wide_ref[pl.ds(which * ROWS + seg * FEW + pair, BANDS, stride=PITCH), :]
        for seg in range(SEG)
    ]
    return jnp.concatenate(rows, axis=0)


def stack_pair(pair, left, rights, stack_refs):
    pair = 2 * (pair % 8) + pair // 8
    sign = jnp.where(lane_index(BANDS * SEG) < 64, 1.0, -1.0)
    turned = jnp.transpose(left)
    left = jnp.concatenate([turned[:64], turned[64:]], axis=1).astype(BF16)
    for right, stack_ref in zip(rights, stack_refs):
        mix = jnp.concatenate([right * sign, pltpu.roll(right, 64, 1)], axis=0).astype(BF16)
        product = jnp.dot(left, mix, preferred_element_type=F32)
        stack_ref[pair * 2 * CH : (pair + 1) * 2 * CH, :] = product


def unstack(out_ref, stack_refs):
    lane = lane_index(CH)
    even = lane % 2 == 0
    for first in range(0, CH, 4):
        pieces = {}
        for back, stack_ref in enumerate(stack_refs):
            rows = [stack_ref[pl.ds(first + k, 2 * FEW, stride=CH), :] for k in range(4)]
            turned = jnp.transpose(jnp.concatenate(rows, axis=0)) * 0.125
            pieces[back] = jnp.where(even, turned[:32], turned[32:64])
            pieces[2 + back] = jnp.where(even, turned[64:96], turned[96:])
        for k in range(4):
            line = None
            for group in range(4):
                part = pieces[group]
                if group != k:
                    part = pltpu.roll(part, (group - k) * 32 % LANES, 1)
                line = part if line is None else jnp.where(lane // 32 == group, part, line)
            out_ref[first + k] = line.astype(BF16)


def other_kernel(parts_ref, out_ref, block_ref, wide_ref, near_ref, far_ref):
    spread_rows(parts_ref, wide_ref)
    first = lax.axis_index("rgrp") % 2 == 0
    for pair in range(FEW):
        a, a_far, b, b_far = (gathered_row(pair, which, wide_ref) for which in range(4))
        left, near, far = (
            jnp.where(first, b, a), jnp.where(first, a, b_far), jnp.where(first, b_far, a_far)
        )
        stack_pair(pair, left, (near, far), (near_ref, far_ref))
        block_ref[pair, 0] = jnp.where(first, a, b).astype(BF16)
        block_ref[pair, 1] = jnp.where(first, b_far, a).astype(BF16)
        block_ref[pair, 2] = jnp.where(first, a_far, b_far).astype(BF16)
    unstack(out_ref, (near_ref, far_ref))


def mine_kernel(block_ref, out_ref, near_ref, far_ref):
    for pair in range(FEW):
        left, near, far = (block_ref[pair, k].astype(F32) for k in range(3))
        stack_pair(pair, left, (near, far), (near_ref, far_ref))
    unstack(out_ref, (near_ref, far_ref))


STACK = pltpu.VMEM((2 * FEW * CH, LANES), F32)
CROSS = jax.ShapeDtypeStruct((CH, CH, LANES), BF16)


def other_of(parts):
    vmem = pl.BlockSpec(memory_space=pltpu.VMEM)
    return pl.pallas_call(
        other_kernel,
        in_specs=[vmem],
        out_specs=[vmem, vmem],
        out_shape=[CROSS, jax.ShapeDtypeStruct((FEW, 3, BANDS * SEG, LANES), BF16)],
        scratch_shapes=[pltpu.VMEM((BANDS * PITCH, LANES), F32), STACK, STACK],
        compiler_params=pltpu.CompilerParams(vmem_limit_bytes=32 * 1024 * 1024),
        name="cross_other",
    )(parts)


def mine_of(blocks):
    vmem = pl.BlockSpec(memory_space=pltpu.VMEM)
    return pl.pallas_call(
        mine_kernel,
        in_specs=[vmem],
        out_specs=vmem,
        out_shape=CROSS,
        scratch_shapes=[STACK, STACK],
        compiler_params=pltpu.CompilerParams(vmem_limit_bytes=32 * 1024 * 1024),
        cost_estimate=pl.CostEstimate(flops=2**28, bytes_accessed=2**23, transcendentals=0),
        name="cross_mine",
    )(blocks)


def merge_kernel(own_ref, other_ref, out_ref):
    first = lax.axis_index("rgrp") % 2 == 0
    even = (lane_index(CH) // 32) % 2 == 0

    def channel(i, carry):
        own = own_ref[i].astype(F32)
        other = other_ref[i].astype(F32)
        low = jnp.where(first, own, other)
        high = jnp.where(first, other, own)
        out_ref[0, i] = jnp.where(even, low, pltpu.roll(high, 32, 1)).astype(BF16)
        out_ref[1, i] = jnp.where(even, pltpu.roll(low, 96, 1), high).astype(BF16)
        return carry

    lax.fori_loop(0, CH, channel, 0, unroll=CH)


def merged_of(own, other):
    vmem = pl.BlockSpec(memory_space=pltpu.VMEM)
    return pl.pallas_call(
        merge_kernel,
        in_specs=[vmem] * 2,
        out_specs=vmem,
        out_shape=jax.ShapeDtypeStruct((2, CH, CH, LANES), BF16),
        compiler_params=pltpu.CompilerParams(vmem_limit_bytes=32 * 1024 * 1024),
        name="merge",
    )(own, other)


def beside(value):
    return lax.ppermute(value, "rgrp", [(g, g ^ 1) for g in range(32)])


def local(table, traces, segment_offsets, channel_order, pilot_channel):
    own, guide = spectra_of(segment_offsets, channel_order, pilot_channel, traces, table)
    far = lax.ppermute(own, "rgrp", [(g, (g + 2) % 32) for g in range(32)])
    guide = guide + beside(guide)
    lines = [[2 * z + side for z in range(16)] for side in range(2)]
    guides = lax.all_to_all(
        jnp.broadcast_to(guide, (16, PAIRS, LANES)),
        "rgrp",
        split_axis=0,
        concat_axis=0,
        tiled=True,
        axis_index_groups=lines,
    )
    white = whitened_of(total_of(guides), own, far)
    planes = [[32 * f + 2 * z + side for f in range(BANDS) for side in range(2)] for z in range(16)]
    parts = lax.all_to_all(
        white, ("freq", "rgrp"), split_axis=0, concat_axis=0, tiled=True, axis_index_groups=planes
    )
    other, blocks = other_of(parts)
    other = beside(other)
    return merged_of(mine_of(blocks), other)


def solution(mesh):
    table = quarter_table()
    specs = (P(), P("rgrp", "freq"), P("freq"), P("rgrp", None), P())
    inner = jax.shard_map(
        local, mesh=mesh, in_specs=specs, out_specs=P(None, "rgrp", None, "freq"), check_vma=False
    )

    def run(traces, segment_offsets, channel_order, pilot_channel):
        return inner(jnp.asarray(table), traces, segment_offsets, channel_order, pilot_channel)

    return run
```

```python
import functools
import math

import jax
import jax.numpy as jnp
import ml_dtypes
import numpy as np
from jax import lax
from jax.experimental import pallas as pl
from jax.experimental.pallas import tpu as pltpu
from jax.sharding import PartitionSpec as P

L = 2048
QUARTER = 512
BANDS = 16
SEG = 4
CH = 32
PAIRS = 32
SPAN = 9216
HALVES = 2
FEW = 16
ROWS = SEG * FEW
PITCH = 4 * ROWS + 8
LANES = 128
BF16 = jnp.bfloat16
F32 = jnp.float32


def quarter_table():
    place = np.arange(PAIRS)
    pair = 16 * (place // 16) + 2 * (place % 8) + place // 8 % 2
    band = 64 * np.arange(BANDS)[:, None]
    bins = np.stack([band + 2 * pair + 1, band + 2 * pair + 2])
    residue = (bins[..., None] * np.arange(QUARTER)) % L
    phase_angle = residue.astype(np.float32) * np.float32(2.0 * math.pi / L)
    factor = np.float32(1.0 / math.sqrt(L))
    odd, even = np.stack([np.cos(phase_angle) * factor, np.sin(phase_angle) * factor], axis=2)
    even = even.reshape(BANDS, 2, 2, 2, 8, QUARTER).transpose(3, 0, 1, 2, 4, 5)
    rows = [part.reshape(-1, QUARTER) for part in (odd, even)]
    return np.stack(rows).astype(ml_dtypes.bfloat16)


def lane_index(rows):
    return lax.broadcasted_iota(jnp.int32, (rows, LANES), 1)


def cut_windows(offset_ref, order_ref, traces_ref, wide_ref, wave_ref):
    lane = lane_index(CH)
    row = lax.broadcasted_iota(jnp.int32, (CH, CH), 0)
    picked = jnp.zeros((CH, CH), jnp.int32)
    for channel in range(CH):
        picked = jnp.where(row == channel, order_ref[0, channel], picked)
    chosen = (lax.broadcasted_iota(jnp.int32, (CH, CH), 1) == picked).astype(F32).astype(BF16)
    tiles = L // LANES
    for seg in range(SEG):
        start = seg * L + offset_ref[seg]
        base = jnp.minimum((start // LANES) * LANES, SPAN - (L + LANES))
        base = pl.multiple_of(base, LANES)
        rest = start - base
        turn = lax.rem(LANES - rest, LANES)
        rolled = []
        for tile in range(tiles + 1):
            part = traces_ref[:, pl.ds(pl.multiple_of(base + tile * LANES, LANES), LANES)]
            rolled.append(pltpu.roll(part.astype(F32), turn, 1))
        window = [
            jnp.where(lane < LANES - rest, rolled[tile], rolled[tile + 1]) for tile in range(tiles)
        ]
        ordered = jnp.dot(
            chosen, jnp.concatenate(window, axis=1).astype(BF16), preferred_element_type=F32
        )
        first, second, third, fourth = (
            ordered[:, k * QUARTER : (k + 1) * QUARTER] for k in range(4)
        )
        even, odd = first + third, second + fourth
        for k, mix in enumerate((first - third, second - fourth, even - odd, even + odd)):
            at = (k % 2) * LANES + seg * CH
            wide_ref[k // 2, at : at + CH, :] = mix
    for parity in range(2):
        mix = jnp.transpose(wide_ref[parity])
        high = mix.astype(BF16)
        low = (mix - high.astype(F32)).astype(BF16)
        if parity == 0:
            wave_ref[0, 0] = high
            wave_ref[0, 1] = low
        else:
            for k in range(2):
                lanes = slice(k * LANES, (k + 1) * LANES)
                wave_ref[1, k] = jnp.concatenate([high[:, lanes], low[:, lanes]], axis=1)


def spectra_kernel(
    offset_hbm, order_hbm, pilot_hbm, traces_hbm, table_hbm, block_ref, guide_ref,
    offset_ref, order_ref, pilot_ref, traces_ref, table_ref, wide_ref, wave_ref,
    power_ref, sems,
):
    small = [
        pltpu.make_async_copy(source, target, sems.at[k])
        for k, (source, target) in enumerate(
            (
                (traces_hbm, traces_ref),
                (offset_hbm, offset_ref),
                (order_hbm, order_ref),
                (pilot_hbm, pilot_ref),
            )
        )
    ]
    for copy in small:
        copy.start()
    table = pltpu.make_async_copy(table_hbm, table_ref, sems.at[len(small)])
    table.start()
    power_ref[...] = jnp.zeros_like(power_ref)
    for copy in small:
        copy.wait()
    cut_windows(offset_ref, order_ref, traces_ref, wide_ref, wave_ref)

    lane = lane_index(PAIRS)
    channel = lax.rem(pilot_ref[0], CH)
    odd_pair = lax.broadcasted_iota(jnp.int32, (PAIRS, LANES), 0) // 8 % 2 == 1
    flip = jnp.where(odd_pair, -1.0, 1.0)
    table.wait()
    odd = jnp.dot(table_ref[0], wave_ref[0, 0], preferred_element_type=F32)
    odd = odd + jnp.dot(table_ref[0], wave_ref[0, 1], preferred_element_type=F32)
    even = []
    for k in range(2):
        rows = pl.ds(k * BANDS * PAIRS, BANDS * PAIRS)
        product = jnp.dot(table_ref[1, rows], wave_ref[1, k], preferred_element_type=F32)
        even.append(product[:, :LANES] + product[:, LANES:])
    for band in range(BANDS):
        at = 2 * PAIRS * band
        cosine, sine = odd[at : at + PAIRS], odd[at + PAIRS : at + 2 * PAIRS]
        parts = {
            (0, 0): cosine[:, :LANES] - flip * sine[:, LANES:],
            (1, 0): -sine[:, :LANES] - flip * cosine[:, LANES:],
        }
        for side in range(2):
            at = PAIRS * band + FEW * side
            rows = [even[k][at + 8 * half : at + 8 * half + 8] for half in range(2) for k in range(2)]
            parts[side, 1] = jnp.concatenate(rows, axis=0) * (1.0, -1.0)[side]
        for parity in range(2):
            real = parts[0, parity].astype(BF16).astype(F32)
            imag = parts[1, parity].astype(BF16).astype(F32)
            place = 2 * band + parity
            power = pltpu.roll(
                real * real + imag * imag, lax.rem(place - channel + LANES, LANES), 1
            )
            power_ref[...] = jnp.where(lane % 32 == place, power, power_ref[...])
        for seg in range(SEG):
            line = None
            for side in range(2):
                for parity in range(2):
                    group = side * 2 + parity
                    part = parts[side, parity]
                    if group != seg:
                        part = pltpu.roll(part, (group - seg) * 32 % LANES, 1)
                    line = part if line is None else jnp.where(lane // 32 == group, part, line)
            line = line.astype(BF16)
            for half in range(HALVES):
                block_ref[band, half, seg * FEW : (seg + 1) * FEW, :] = line[
                    half * FEW : (half + 1) * FEW
                ]
    mine = pilot_ref[0] // CH == lax.axis_index("rgrp")
    guide_ref[...] = jnp.where(mine, jnp.sqrt(power_ref[...]), 0.0).astype(BF16)


def spectra_of(offsets, order, pilot, traces, table):
    vmem = pl.BlockSpec(memory_space=pltpu.VMEM)
    offsets, order, traces, table = (
        pltpu.with_memory_space_constraint(value, pltpu.HBM)
        for value in (offsets, order, traces, table)
    )
    return pl.pallas_call(
        spectra_kernel,
        in_specs=[pl.BlockSpec(memory_space=pl.ANY)] * 5,
        out_specs=[vmem, vmem],
        out_shape=[
            jax.ShapeDtypeStruct((BANDS, HALVES, SEG * FEW, LANES), BF16),
            jax.ShapeDtypeStruct((PAIRS, LANES), BF16),
        ],
        scratch_shapes=[
            pltpu.SMEM((SEG,), jnp.int32),
            pltpu.SMEM((1, CH), jnp.int32),
            pltpu.SMEM((1,), jnp.int32),
            pltpu.VMEM((CH, SPAN), BF16),
            pltpu.VMEM((2, 2 * PAIRS * BANDS, QUARTER), BF16),
            pltpu.VMEM((2, 2 * LANES, QUARTER), F32),
            pltpu.VMEM((2, 2, QUARTER, 2 * LANES), BF16),
            pltpu.VMEM((PAIRS, LANES), F32),
            pltpu.SemaphoreType.DMA((5,)),
        ],
        compiler_params=pltpu.CompilerParams(vmem_limit_bytes=16 * 1024 * 1024),
        name="spectra",
    )(offsets, order, pilot, traces, table)


def total_kernel(guides_ref, guide_ref):
    guide = guides_ref[0].astype(F32)
    for line in range(1, 16):
        guide = guide + guides_ref[line].astype(F32)
    guide_ref[...] = guide


def total_of(guides):
    vmem = pl.BlockSpec(memory_space=pltpu.VMEM)
    return pl.pallas_call(
        total_kernel,
        in_specs=[vmem],
        out_specs=vmem,
        out_shape=jax.ShapeDtypeStruct((PAIRS, LANES), F32),
        compiler_params=pltpu.CompilerParams(vmem_limit_bytes=32 * 1024 * 1024),
        cost_estimate=pl.CostEstimate(flops=2**28, bytes_accessed=2**17, transcendentals=0),
        name="total",
    )(guides)


def whiten_kernel(guide_ref, own_ref, far_ref, white_ref, value_ref):
    guide = guide_ref[...]
    place = lane_index(PAIRS) // 2
    parity = lax.broadcasted_iota(jnp.int32, (LANES, LANES), 0) % 2
    spread = (parity == (lane_index(LANES) // 32) % 2).astype(F32).astype(BF16)
    blocks = (own_ref, far_ref)
    totals = [[jnp.zeros((FEW, LANES), F32) for _ in range(SEG)] for _ in blocks]
    for band in range(BANDS):
        picked = [jnp.where(place == seg * BANDS + band, guide, 0.0) for seg in range(SEG)]
        weight = jnp.dot(
            jnp.concatenate(picked, axis=0).astype(BF16), spread, preferred_element_type=F32
        )
        for seg in range(SEG):
            rows = slice(seg * FEW, (seg + 1) * FEW)
            for half in range(HALVES):
                at = seg * PAIRS + half * FEW
                part = weight[at : at + FEW]
                for k, block_ref in enumerate(blocks):
                    value = block_ref[band, half, rows, :].astype(F32) * part
                    value_ref[band * HALVES + half, k, rows, :] = value
                    totals[k][seg] = totals[k][seg] + value * value
    for k in range(len(blocks)):
        for seg in range(SEG):
            total = jnp.sum(totals[k][seg], axis=0, keepdims=True)
            total = jnp.broadcast_to(total, (8, LANES))
            total = total + pltpu.roll(total, 64, 1)
            total = total + pltpu.roll(total, 32, 1)
            level = (total * (0.1 / (64.0 * BANDS)) + 1e-06)[:1]
            rows = slice(seg * FEW, (seg + 1) * FEW)
            for place in range(BANDS * HALVES):
                value = value_ref[place, k, rows, :]
                energy = value * value
                energy = energy + pltpu.roll(energy, 64, 1)
                white_ref[place, k, rows, :] = (value * lax.rsqrt(energy + level)).astype(BF16)


def whitened_of(guides, own, far):
    vmem = pl.BlockSpec(memory_space=pltpu.VMEM)
    shape = (BANDS * HALVES, 2, ROWS, LANES)
    return pl.pallas_call(
        whiten_kernel,
        in_specs=[vmem] * 3,
        out_specs=vmem,
        out_shape=jax.ShapeDtypeStruct(shape, BF16),
        scratch_shapes=[pltpu.VMEM(shape, F32)],
        compiler_params=pltpu.CompilerParams(vmem_limit_bytes=32 * 1024 * 1024),
        name="whiten",
    )(guides, own, far)


def spread_rows(parts_ref, wide_ref):
    for window in range(BANDS):
        for which in range(4):
            at = window * PITCH + which * ROWS
            part = parts_ref[window * HALVES + which // 2, which % 2]
            wide_ref[at : at + ROWS, :] = part.astype(F32)


def gathered_row(pair, which, wide_ref):
    rows = [
        wide_ref[pl.ds(which * ROWS + seg * FEW + pair, BANDS, stride=PITCH), :]
        for seg in range(SEG)
    ]
    return jnp.concatenate(rows, axis=0)


def stack_pair(pair, left, rights, stack_refs):
    pair = 2 * (pair % 8) + pair // 8
    sign = jnp.where(lane_index(BANDS * SEG) < 64, 1.0, -1.0)
    turned = jnp.transpose(left)
    left = jnp.concatenate([turned[:64], turned[64:]], axis=1).astype(BF16)
    for right, stack_ref in zip(rights, stack_refs):
        mix = jnp.concatenate([right * sign, pltpu.roll(right, 64, 1)], axis=0).astype(BF16)
        product = jnp.dot(left, mix, preferred_element_type=F32)
        stack_ref[pair * 2 * CH : (pair + 1) * 2 * CH, :] = product


def unstack(out_ref, stack_refs):
    lane = lane_index(CH)
    even = lane % 2 == 0
    for first in range(0, CH, 4):
        pieces = {}
        for back, stack_ref in enumerate(stack_refs):
            rows = [stack_ref[pl.ds(first + k, 2 * FEW, stride=CH), :] for k in range(4)]
            turned = jnp.transpose((jnp.concatenate(rows, axis=0) * 0.125).astype(BF16))
            pieces[back] = jnp.where(even, turned[:32], turned[32:64])
            pieces[2 + back] = jnp.where(even, turned[64:96], turned[96:])
        for k in range(4):
            line = None
            for group in range(4):
                part = pieces[group]
                if group != k:
                    part = pltpu.roll(part, (group - k) * 32 % LANES, 1)
                line = part if line is None else jnp.where(lane // 32 == group, part, line)
            out_ref[first + k] = line


def other_kernel(parts_ref, out_ref, block_ref, wide_ref, near_ref, far_ref):
    spread_rows(parts_ref, wide_ref)
    first = lax.axis_index("rgrp") % 2 == 0
    for pair in range(FEW):
        a, a_far, b, b_far = (gathered_row(pair, which, wide_ref) for which in range(4))
        left, near, far = (
            jnp.where(first, b, a), jnp.where(first, a, b_far), jnp.where(first, b_far, a_far)
        )
        stack_pair(pair, left, (near, far), (near_ref, far_ref))
        block_ref[pair, 0] = jnp.where(first, a, b).astype(BF16)
        block_ref[pair, 1] = jnp.where(first, b_far, a).astype(BF16)
        block_ref[pair, 2] = jnp.where(first, a_far, b_far).astype(BF16)
    unstack(out_ref, (near_ref, far_ref))


def mine_kernel(block_ref, out_ref, near_ref, far_ref):
    for pair in range(FEW):
        left, near, far = (block_ref[pair, k].astype(F32) for k in range(3))
        stack_pair(pair, left, (near, far), (near_ref, far_ref))
    unstack(out_ref, (near_ref, far_ref))


STACK = pltpu.VMEM((2 * FEW * CH, LANES), F32)
CROSS = jax.ShapeDtypeStruct((CH, CH, LANES), BF16)


def other_of(parts):
    vmem = pl.BlockSpec(memory_space=pltpu.VMEM)
    return pl.pallas_call(
        other_kernel,
        in_specs=[vmem],
        out_specs=[vmem, vmem],
        out_shape=[CROSS, jax.ShapeDtypeStruct((FEW, 3, BANDS * SEG, LANES), BF16)],
        scratch_shapes=[pltpu.VMEM((BANDS * PITCH, LANES), F32), STACK, STACK],
        compiler_params=pltpu.CompilerParams(vmem_limit_bytes=32 * 1024 * 1024),
        name="cross_other",
    )(parts)


def mine_of(blocks):
    vmem = pl.BlockSpec(memory_space=pltpu.VMEM)
    return pl.pallas_call(
        mine_kernel,
        in_specs=[vmem],
        out_specs=vmem,
        out_shape=CROSS,
        scratch_shapes=[STACK, STACK],
        compiler_params=pltpu.CompilerParams(vmem_limit_bytes=32 * 1024 * 1024),
        cost_estimate=pl.CostEstimate(flops=2**28, bytes_accessed=2**23, transcendentals=0),
        name="cross_mine",
    )(blocks)


def merge_kernel(own_ref, other_ref, out_hbm, out_ref, sems):
    first = lax.axis_index("rgrp") % 2 == 0
    even = (lane_index(CH) // 32) % 2 == 0
    copies = []
    for part in range(4):
        rows = pl.ds(part * (CH // 4), CH // 4)
        for i in range(part * (CH // 4), (part + 1) * (CH // 4)):
            own = own_ref[i].astype(F32)
            other = other_ref[i].astype(F32)
            low = jnp.where(first, own, other)
            high = jnp.where(first, other, own)
            out_ref[0, i] = jnp.where(even, low, pltpu.roll(high, 32, 1)).astype(BF16)
            out_ref[1, i] = jnp.where(even, pltpu.roll(low, 96, 1), high).astype(BF16)
        for back in range(2):
            copy = pltpu.make_async_copy(
                out_ref.at[back, rows], out_hbm.at[back, rows], sems.at[2 * part + back]
            )
            copy.start()
            copies.append(copy)
    for copy in copies:
        copy.wait()


def merged_of(own, other):
    vmem = pl.BlockSpec(memory_space=pltpu.VMEM)
    shape = (2, CH, CH, LANES)
    return pl.pallas_call(
        merge_kernel,
        in_specs=[vmem] * 2,
        out_specs=pl.BlockSpec(memory_space=pl.ANY),
        out_shape=jax.ShapeDtypeStruct(shape, BF16),
        scratch_shapes=[pltpu.VMEM(shape, BF16), pltpu.SemaphoreType.DMA((2 * 4,))],
        compiler_params=pltpu.CompilerParams(vmem_limit_bytes=32 * 1024 * 1024),
        name="merge",
    )(own, other)


def beside(value):
    return lax.ppermute(value, "rgrp", [(g, g ^ 1) for g in range(32)])


def local(table, traces, segment_offsets, channel_order, pilot_channel):
    own, guide = spectra_of(segment_offsets, channel_order, pilot_channel, traces, table)
    far = lax.ppermute(own, "rgrp", [(g, (g + 2) % 32) for g in range(32)])
    guide = guide + beside(guide)
    lines = [[2 * z + side for z in range(16)] for side in range(2)]
    guides = lax.all_to_all(
        jnp.broadcast_to(guide, (16, PAIRS, LANES)),
        "rgrp",
        split_axis=0,
        concat_axis=0,
        tiled=True,
        axis_index_groups=lines,
    )
    white = whitened_of(total_of(guides), own, far)
    planes = [[32 * f + 2 * z + side for f in range(BANDS) for side in range(2)] for z in range(16)]
    parts = lax.all_to_all(
        white, ("freq", "rgrp"), split_axis=0, concat_axis=0, tiled=True, axis_index_groups=planes
    )
    other, blocks = other_of(parts)
    other = beside(other)
    return merged_of(mine_of(blocks), other)


def solution(mesh):
    table = quarter_table()
    specs = (P(), P("rgrp", "freq"), P("freq"), P("rgrp", None), P())
    inner = jax.shard_map(
        local, mesh=mesh, in_specs=specs, out_specs=P(None, "rgrp", None, "freq"), check_vma=False
    )

    def run(traces, segment_offsets, channel_order, pilot_channel):
        return inner(jnp.asarray(table), traces, segment_offsets, channel_order, pilot_channel)

    return run
```

```python
import functools
import math

import jax
import jax.numpy as jnp
import ml_dtypes
import numpy as np
from jax import lax
from jax.experimental import pallas as pl
from jax.experimental.pallas import tpu as pltpu
from jax.sharding import PartitionSpec as P

L = 2048
QUARTER = 512
BANDS = 16
SEG = 4
CH = 32
PAIRS = 32
SPAN = 9216
HALVES = 2
FEW = 16
ROWS = SEG * FEW
PITCH = 4 * ROWS + 8
LANES = 128
BF16 = jnp.bfloat16
F32 = jnp.float32


def quarter_table():
    place = np.arange(PAIRS)
    pair = 16 * (place // 16) + 2 * (place % 8) + place // 8 % 2
    band = 64 * np.arange(BANDS)[:, None]
    bins = np.stack([band + 2 * pair + 1, band + 2 * pair + 2])
    residue = (bins[..., None] * np.arange(QUARTER)) % L
    phase_angle = residue.astype(np.float32) * np.float32(2.0 * math.pi / L)
    factor = np.float32(1.0 / math.sqrt(L))
    odd, even = np.stack([np.cos(phase_angle) * factor, np.sin(phase_angle) * factor], axis=2)
    even = even.reshape(BANDS, 2, 2, 2, 8, QUARTER).transpose(3, 0, 1, 2, 4, 5)
    rows = [part.reshape(-1, QUARTER) for part in (odd, even)]
    return np.stack(rows).astype(ml_dtypes.bfloat16)


def lane_index(rows):
    return lax.broadcasted_iota(jnp.int32, (rows, LANES), 1)


def cut_windows(offset_ref, order_ref, traces_ref, wide_ref, wave_ref):
    lane = lane_index(CH)
    row = lax.broadcasted_iota(jnp.int32, (CH, CH), 0)
    picked = jnp.zeros((CH, CH), jnp.int32)
    for channel in range(CH):
        picked = jnp.where(row == channel, order_ref[0, channel], picked)
    chosen = (lax.broadcasted_iota(jnp.int32, (CH, CH), 1) == picked).astype(F32).astype(BF16)
    tiles = L // LANES
    for seg in range(SEG):
        start = seg * L + offset_ref[seg]
        base = jnp.minimum((start // LANES) * LANES, SPAN - (L + LANES))
        base = pl.multiple_of(base, LANES)
        rest = start - base
        turn = lax.rem(LANES - rest, LANES)
        rolled = []
        for tile in range(tiles + 1):
            part = traces_ref[:, pl.ds(pl.multiple_of(base + tile * LANES, LANES), LANES)]
            rolled.append(pltpu.roll(part.astype(F32), turn, 1))
        window = [
            jnp.where(lane < LANES - rest, rolled[tile], rolled[tile + 1]) for tile in range(tiles)
        ]
        ordered = jnp.dot(
            chosen, jnp.concatenate(window, axis=1).astype(BF16), preferred_element_type=F32
        )
        first, second, third, fourth = (
            ordered[:, k * QUARTER : (k + 1) * QUARTER] for k in range(4)
        )
        even, odd = first + third, second + fourth
        for k, mix in enumerate((first - third, second - fourth, even - odd, even + odd)):
            at = (k % 2) * LANES + seg * CH
            wide_ref[k // 2, at : at + CH, :] = mix
    for parity in range(2):
        mix = jnp.transpose(wide_ref[parity])
        high = mix.astype(BF16)
        low = (mix - high.astype(F32)).astype(BF16)
        if parity == 0:
            wave_ref[0, 0] = high
            wave_ref[0, 1] = low
        else:
            for k in range(2):
                lanes = slice(k * LANES, (k + 1) * LANES)
                wave_ref[1, k] = jnp.concatenate([high[:, lanes], low[:, lanes]], axis=1)


def spectra_kernel(
    offset_hbm, order_hbm, pilot_hbm, traces_hbm, table_hbm, block_ref, guide_ref,
    offset_ref, order_ref, pilot_ref, traces_ref, table_ref, wide_ref, wave_ref,
    power_ref, sems,
):
    small = [
        pltpu.make_async_copy(source, target, sems.at[k])
        for k, (source, target) in enumerate(
            (
                (traces_hbm, traces_ref),
                (offset_hbm, offset_ref),
                (order_hbm, order_ref),
                (pilot_hbm, pilot_ref),
            )
        )
    ]
    for copy in small:
        copy.start()
    table = pltpu.make_async_copy(table_hbm, table_ref, sems.at[len(small)])
    table.start()
    power_ref[...] = jnp.zeros_like(power_ref)
    for copy in small:
        copy.wait()
    cut_windows(offset_ref, order_ref, traces_ref, wide_ref, wave_ref)

    lane = lane_index(PAIRS)
    channel = lax.rem(pilot_ref[0], CH)
    odd_pair = lax.broadcasted_iota(jnp.int32, (PAIRS, LANES), 0) // 8 % 2 == 1
    flip = jnp.where(odd_pair, -1.0, 1.0)
    table.wait()
    odd = jnp.dot(table_ref[0], wave_ref[0, 0], preferred_element_type=F32)
    odd = odd + jnp.dot(table_ref[0], wave_ref[0, 1], preferred_element_type=F32)
    even = []
    for k in range(2):
        rows = pl.ds(k * BANDS * PAIRS, BANDS * PAIRS)
        product = jnp.dot(table_ref[1, rows], wave_ref[1, k], preferred_element_type=F32)
        even.append(product[:, :LANES] + product[:, LANES:])
    for band in range(BANDS):
        at = 2 * PAIRS * band
        cosine, sine = odd[at : at + PAIRS], odd[at + PAIRS : at + 2 * PAIRS]
        parts = {
            (0, 0): cosine[:, :LANES] - flip * sine[:, LANES:],
            (1, 0): -sine[:, :LANES] - flip * cosine[:, LANES:],
        }
        for side in range(2):
            at = PAIRS * band + FEW * side
            rows = [even[k][at + 8 * half : at + 8 * half + 8] for half in range(2) for k in range(2)]
            parts[side, 1] = jnp.concatenate(rows, axis=0) * (1.0, -1.0)[side]
        for parity in range(2):
            real = parts[0, parity].astype(BF16).astype(F32)
            imag = parts[1, parity].astype(BF16).astype(F32)
            place = 2 * band + parity
            power = pltpu.roll(
                real * real + imag * imag, lax.rem(place - channel + LANES, LANES), 1
            )
            power_ref[...] = jnp.where(lane % 32 == place, power, power_ref[...])
        for seg in range(SEG):
            line = None
            for side in range(2):
                for parity in range(2):
                    group = side * 2 + parity
                    part = parts[side, parity]
                    if group != seg:
                        part = pltpu.roll(part, (group - seg) * 32 % LANES, 1)
                    line = part if line is None else jnp.where(lane // 32 == group, part, line)
            line = line.astype(BF16)
            for half in range(HALVES):
                block_ref[band, half, seg * FEW : (seg + 1) * FEW, :] = line[
                    half * FEW : (half + 1) * FEW
                ]
    mine = pilot_ref[0] // CH == lax.axis_index("rgrp")
    guide_ref[...] = jnp.where(mine, jnp.sqrt(power_ref[...]), 0.0).astype(BF16)


def spectra_of(offsets, order, pilot, traces, table):
    vmem = pl.BlockSpec(memory_space=pltpu.VMEM)
    offsets, order, traces, table = (
        pltpu.with_memory_space_constraint(value, pltpu.HBM)
        for value in (offsets, order, traces, table)
    )
    return pl.pallas_call(
        spectra_kernel,
        in_specs=[pl.BlockSpec(memory_space=pl.ANY)] * 5,
        out_specs=[vmem, vmem],
        out_shape=[
            jax.ShapeDtypeStruct((BANDS, HALVES, SEG * FEW, LANES), BF16),
            jax.ShapeDtypeStruct((PAIRS, LANES), BF16),
        ],
        scratch_shapes=[
            pltpu.SMEM((SEG,), jnp.int32),
            pltpu.SMEM((1, CH), jnp.int32),
            pltpu.SMEM((1,), jnp.int32),
            pltpu.VMEM((CH, SPAN), BF16),
            pltpu.VMEM((2, 2 * PAIRS * BANDS, QUARTER), BF16),
            pltpu.VMEM((2, 2 * LANES, QUARTER), F32),
            pltpu.VMEM((2, 2, QUARTER, 2 * LANES), BF16),
            pltpu.VMEM((PAIRS, LANES), F32),
            pltpu.SemaphoreType.DMA((5,)),
        ],
        compiler_params=pltpu.CompilerParams(vmem_limit_bytes=16 * 1024 * 1024),
        name="spectra",
    )(offsets, order, pilot, traces, table)


def total_kernel(guides_ref, guide_ref):
    guide = guides_ref[0].astype(F32)
    for line in range(1, 16):
        guide = guide + guides_ref[line].astype(F32)
    guide_ref[...] = guide


def total_of(guides):
    vmem = pl.BlockSpec(memory_space=pltpu.VMEM)
    return pl.pallas_call(
        total_kernel,
        in_specs=[vmem],
        out_specs=vmem,
        out_shape=jax.ShapeDtypeStruct((PAIRS, LANES), F32),
        compiler_params=pltpu.CompilerParams(vmem_limit_bytes=32 * 1024 * 1024),
        cost_estimate=pl.CostEstimate(flops=2**28, bytes_accessed=2**17, transcendentals=0),
        name="total",
    )(guides)


def whiten_kernel(guide_ref, own_ref, far_ref, white_ref, weight_ref):
    guide = guide_ref[...]
    place = lane_index(PAIRS) // 2
    parity = lax.broadcasted_iota(jnp.int32, (LANES, LANES), 0) % 2
    spread = (parity == (lane_index(LANES) // 32) % 2).astype(F32).astype(BF16)
    blocks = (own_ref, far_ref)
    totals = [[jnp.zeros((FEW, LANES), F32) for _ in range(SEG)] for _ in blocks]
    for band in range(BANDS):
        picked = [jnp.where(place == seg * BANDS + band, guide, 0.0) for seg in range(SEG)]
        weight = jnp.dot(
            jnp.concatenate(picked, axis=0).astype(BF16), spread, preferred_element_type=F32
        )
        weight_ref[band] = weight
        for seg in range(SEG):
            rows = slice(seg * FEW, (seg + 1) * FEW)
            for half in range(HALVES):
                at = seg * PAIRS + half * FEW
                part = weight[at : at + FEW]
                for k, block_ref in enumerate(blocks):
                    value = block_ref[band, half, rows, :].astype(F32) * part
                    totals[k][seg] = totals[k][seg] + value * value
    for k in range(len(blocks)):
        for seg in range(SEG):
            total = jnp.sum(totals[k][seg], axis=0, keepdims=True)
            total = jnp.broadcast_to(total, (8, LANES))
            total = total + pltpu.roll(total, 64, 1)
            total = total + pltpu.roll(total, 32, 1)
            level = (total * (0.1 / (64.0 * BANDS)) + 1e-06)[:1]
            rows = slice(seg * FEW, (seg + 1) * FEW)
            for place in range(BANDS * HALVES):
                at = seg * PAIRS + place % HALVES * FEW
                part = weight_ref[place // HALVES, at : at + FEW, :]
                value = blocks[k][place // HALVES, place % HALVES, rows, :].astype(F32) * part
                energy = value * value
                energy = energy + pltpu.roll(energy, 64, 1)
                white_ref[place, k, rows, :] = (value * lax.rsqrt(energy + level)).astype(BF16)


def whitened_of(guides, own, far):
    vmem = pl.BlockSpec(memory_space=pltpu.VMEM)
    shape = (BANDS * HALVES, 2, ROWS, LANES)
    return pl.pallas_call(
        whiten_kernel,
        in_specs=[vmem] * 3,
        out_specs=vmem,
        out_shape=jax.ShapeDtypeStruct(shape, BF16),
        scratch_shapes=[pltpu.VMEM((BANDS, SEG * PAIRS, LANES), F32)],
        compiler_params=pltpu.CompilerParams(vmem_limit_bytes=32 * 1024 * 1024),
        name="whiten",
    )(guides, own, far)


def spread_rows(parts_ref, wide_ref):
    for window in range(BANDS):
        for which in range(4):
            at = window * PITCH + which * ROWS
            part = parts_ref[window * HALVES + which // 2, which % 2]
            wide_ref[at : at + ROWS, :] = part.astype(F32)


def gathered_row(pair, which, wide_ref):
    rows = [
        wide_ref[pl.ds(which * ROWS + seg * FEW + pair, BANDS, stride=PITCH), :]
        for seg in range(SEG)
    ]
    return jnp.concatenate(rows, axis=0)


def stack_pair(pair, left, rights, stack_refs):
    pair = 2 * (pair % 8) + pair // 8
    sign = jnp.where(lane_index(BANDS * SEG) < 64, 1.0, -1.0)
    turned = jnp.transpose(left)
    left = jnp.concatenate([turned[:64], turned[64:]], axis=1).astype(BF16)
    for right, stack_ref in zip(rights, stack_refs):
        mix = jnp.concatenate([right * sign, pltpu.roll(right, 64, 1)], axis=0).astype(BF16)
        product = jnp.dot(left, mix, preferred_element_type=F32)
        stack_ref[pair * 2 * CH : (pair + 1) * 2 * CH, :] = product


def unstack(out_ref, stack_refs):
    lane = lane_index(CH)
    even = lane % 2 == 0
    for first in range(0, CH, 4):
        pieces = {}
        for back, stack_ref in enumerate(stack_refs):
            rows = [stack_ref[pl.ds(first + k, 2 * FEW, stride=CH), :] for k in range(4)]
            turned = jnp.transpose(jnp.concatenate(rows, axis=0)) * 0.125
            pieces[back] = jnp.where(even, turned[:32], turned[32:64])
            pieces[2 + back] = jnp.where(even, turned[64:96], turned[96:])
        for k in range(4):
            line = None
            for group in range(4):
                part = pieces[group]
                if group != k:
                    part = pltpu.roll(part, (group - k) * 32 % LANES, 1)
                line = part if line is None else jnp.where(lane // 32 == group, part, line)
            out_ref[first + k] = line.astype(BF16)


def other_kernel(parts_ref, out_ref, block_ref, wide_ref, near_ref, far_ref):
    spread_rows(parts_ref, wide_ref)
    first = lax.axis_index("rgrp") % 2 == 0
    for pair in range(FEW):
        a, a_far, b, b_far = (gathered_row(pair, which, wide_ref) for which in range(4))
        left, near, far = (
            jnp.where(first, b, a), jnp.where(first, a, b_far), jnp.where(first, b_far, a_far)
        )
        stack_pair(pair, left, (near, far), (near_ref, far_ref))
        block_ref[pair, 0] = jnp.where(first, a, b).astype(BF16)
        block_ref[pair, 1] = jnp.where(first, b_far, a).astype(BF16)
        block_ref[pair, 2] = jnp.where(first, a_far, b_far).astype(BF16)
    unstack(out_ref, (near_ref, far_ref))


def mine_kernel(block_ref, out_ref, near_ref, far_ref):
    for pair in range(FEW):
        left, near, far = (block_ref[pair, k].astype(F32) for k in range(3))
        stack_pair(pair, left, (near, far), (near_ref, far_ref))
    unstack(out_ref, (near_ref, far_ref))


STACK = pltpu.VMEM((2 * FEW * CH, LANES), F32)
CROSS = jax.ShapeDtypeStruct((CH, CH, LANES), BF16)


def other_of(parts):
    vmem = pl.BlockSpec(memory_space=pltpu.VMEM)
    return pl.pallas_call(
        other_kernel,
        in_specs=[vmem],
        out_specs=[vmem, vmem],
        out_shape=[CROSS, jax.ShapeDtypeStruct((FEW, 3, BANDS * SEG, LANES), BF16)],
        scratch_shapes=[pltpu.VMEM((BANDS * PITCH, LANES), F32), STACK, STACK],
        compiler_params=pltpu.CompilerParams(vmem_limit_bytes=32 * 1024 * 1024),
        name="cross_other",
    )(parts)


def mine_of(blocks):
    vmem = pl.BlockSpec(memory_space=pltpu.VMEM)
    return pl.pallas_call(
        mine_kernel,
        in_specs=[vmem],
        out_specs=vmem,
        out_shape=CROSS,
        scratch_shapes=[STACK, STACK],
        compiler_params=pltpu.CompilerParams(vmem_limit_bytes=32 * 1024 * 1024),
        cost_estimate=pl.CostEstimate(flops=2**28, bytes_accessed=2**23, transcendentals=0),
        name="cross_mine",
    )(blocks)


def merge_kernel(own_ref, other_ref, out_ref):
    first = lax.axis_index("rgrp") % 2 == 0
    even = (lane_index(CH) // 32) % 2 == 0

    def channel(i, carry):
        own = own_ref[i].astype(F32)
        other = other_ref[i].astype(F32)
        low = jnp.where(first, own, other)
        high = jnp.where(first, other, own)
        out_ref[0, i] = jnp.where(even, low, pltpu.roll(high, 32, 1)).astype(BF16)
        out_ref[1, i] = jnp.where(even, pltpu.roll(low, 96, 1), high).astype(BF16)
        return carry

    lax.fori_loop(0, CH, channel, 0, unroll=CH)


def merged_of(own, other):
    vmem = pl.BlockSpec(memory_space=pltpu.VMEM)
    return pl.pallas_call(
        merge_kernel,
        in_specs=[vmem] * 2,
        out_specs=vmem,
        out_shape=jax.ShapeDtypeStruct((2, CH, CH, LANES), BF16),
        compiler_params=pltpu.CompilerParams(vmem_limit_bytes=32 * 1024 * 1024),
        name="merge",
    )(own, other)


def beside(value):
    return lax.ppermute(value, "rgrp", [(g, g ^ 1) for g in range(32)])


def local(table, traces, segment_offsets, channel_order, pilot_channel):
    own, guide = spectra_of(segment_offsets, channel_order, pilot_channel, traces, table)
    far = lax.ppermute(own, "rgrp", [(g, (g + 2) % 32) for g in range(32)])
    guide = guide + beside(guide)
    lines = [[2 * z + side for z in range(16)] for side in range(2)]
    guides = lax.all_to_all(
        jnp.broadcast_to(guide, (16, PAIRS, LANES)),
        "rgrp",
        split_axis=0,
        concat_axis=0,
        tiled=True,
        axis_index_groups=lines,
    )
    white = whitened_of(total_of(guides), own, far)
    planes = [[32 * f + 2 * z + side for f in range(BANDS) for side in range(2)] for z in range(16)]
    parts = lax.all_to_all(
        white, ("freq", "rgrp"), split_axis=0, concat_axis=0, tiled=True, axis_index_groups=planes
    )
    other, blocks = other_of(parts)
    other = beside(other)
    return merged_of(mine_of(blocks), other)


def solution(mesh):
    table = quarter_table()
    specs = (P(), P("rgrp", "freq"), P("freq"), P("rgrp", None), P())
    inner = jax.shard_map(
        local, mesh=mesh, in_specs=specs, out_specs=P(None, "rgrp", None, "freq"), check_vma=False
    )

    def run(traces, segment_offsets, channel_order, pilot_channel):
        return inner(jnp.asarray(table), traces, segment_offsets, channel_order, pilot_channel)

    return run
```
